512 devices in a mesh: frame: 64 (over z, x, core), pool: 8 (over y).
Axes of the slice: x: 4, y: 8, z: 8, core: 2. Of those that a mesh axis runs over, the one named last changes fastest.
Arguments:
- frames_in: bfloat16 [256, 256, 1408], P('frame'), may hold values from -6 to 6
- qkv_weight: bfloat16 [1408, 3, 1408], P('frame', None, 'pool')
- out_weight: bfloat16 [1408, 1408], P('pool', 'frame'), may hold values from -0.15625 to 0.15625
- owners: int32 [256], P('frame'), may hold values from 0 to 7, as said below
- slots: int32 [256], P('frame'), may hold values from 0 to 0, as said below
Outputs:
- shipped: bfloat16 [512, 256, 1408], P(('frame', 'pool'))
- shipped_scales: bfloat16 [512, 11, 256], P(('frame', 'pool'))
The draws below stay inside these ranges and needn't reach their ends.
Inputs may be any that keep to these rules, and one draw needn't show every extreme that they name: `owners`: within each group of 4 frames f // 4, no owner receives more than 1 frames, and one owner receives exactly 1. Within each group of 4 frames, the frames sent to one owner hold distinct slots 0, 1, ... in the order of their count.
All inputs are finite; a program needn't handle non-finite values. Where the reference program divides by a largest or mean magnitude, that divisor is 1e-20 or more.
Results may differ from the reference program's by a relative error of at most 0.015.
Values may be sent and summed in bfloat16 or wider, within the bound.
No kernel may reach another device: no remote copies, remote signals or barrier semaphores. Data moves between devices by JAX's collectives and lax.ppermute only.
A program may use at most 64 MiB of HBM per device.

```python
import jax
import jax.numpy as jnp
from jax import lax

HEADS = 16
HEAD_DIM = 88
D = 1408
PATCHES = 256
FR_DEV = 4
FRAMES = 256
GROUP = 128
GROUPS = 11
CAP = 1
SLOTS = 512
N_POOL = 8


def owner_table(key):
    groups = FRAMES // FR_DEV
    first, second, third = jax.random.split(key, 3)
    owner_perm = jax.vmap(lambda k: jax.random.permutation(k, N_POOL))(jax.random.split(first, groups))
    frame_perm = jax.vmap(lambda k: jax.random.permutation(k, FR_DEV))(jax.random.split(second, groups))
    least = max(1, (FR_DEV - CAP + N_POOL - 2) // (N_POOL - 1))
    spread = jnp.minimum(jnp.maximum(jax.random.randint(third, (groups, 1), 1, CAP + 1), least), CAP)
    rest = jnp.maximum(frame_perm - CAP, 0)
    choose = jnp.where(frame_perm < CAP, 0, 1 + rest // spread)
    owner_ids = jnp.take_along_axis(owner_perm, choose, axis=1)
    slot_ids = jnp.where(frame_perm < CAP, frame_perm, rest % spread)
    return (owner_ids.reshape(-1).astype(jnp.int32), slot_ids.reshape(-1).astype(jnp.int32))


def draw_owners(key, part):
    owner_ids, slot_ids = owner_table(key)
    return owner_ids


def draw_slots(key, part):
    owner_ids, slot_ids = owner_table(key)
    return slot_ids


def draw_qkv_weight(key, part):
    key = jax.random.fold_in(key, 11)
    factor = D ** (-0.5)
    return (jax.random.normal(key, (D, 3, D), jnp.float32) * factor).astype(jnp.bfloat16)


def block_levels(stream_key, extent, pieces, smallest, top_value):
    loudness = 1.0
    for axis_at, shards_of in pieces:
        draws = jax.random.uniform(jax.random.fold_in(jax.random.fold_in(stream_key, 6), axis_at), (shards_of,), jnp.float32, smallest / len(pieces), top_value / len(pieces))
        loudness = loudness * jnp.repeat(jnp.exp(draws), extent[axis_at] // shards_of).reshape((-1,) + (1,) * (len(extent) - 1 - axis_at))
    return loudness


def noise(key, shape, deviation, most, pieces=(), kind=jnp.bfloat16):
    array = deviation * jax.random.normal(key, shape, jnp.float32)
    if pieces:
        array = array * block_levels(key, shape, pieces, -0.22, 0.18)
    return jnp.clip(array, -most, most).astype(kind)


def setup_inputs(seed: int = 0) -> dict:
    keys = jax.random.split(jax.random.key(seed), 6)
    frames_in = noise(keys[0], (FRAMES, PATCHES, D), 1.0, 6.0, ((0, 64),))
    qkv_weight = draw_qkv_weight(jax.random.fold_in(keys[5], 71), 0)
    out_weight = noise(keys[2], (D, D), D ** -0.5, 0.15625, ((0, 8), (1, 64)))
    owners = draw_owners(jax.random.fold_in(keys[5], 71), 0)
    slots = draw_slots(jax.random.fold_in(keys[5], 71), 0)
    return {"frames_in": frames_in, "qkv_weight": qkv_weight, "out_weight": out_weight, "owners": owners, "slots": slots}


def reference(frames_in, qkv_weight, out_weight, owners, slots):
    xf = frames_in.astype(jnp.float32)
    mean = lax.optimization_barrier(jnp.mean(xf, axis=-1, keepdims=True))
    centred = xf - mean
    var = lax.optimization_barrier(jnp.mean(centred * centred, axis=-1, keepdims=True))
    normed = (centred * lax.rsqrt(var + 1e-06)).astype(jnp.bfloat16)
    tokens = normed.reshape(FRAMES * PATCHES, D)
    query = jnp.dot(tokens, qkv_weight[:, 0, :], preferred_element_type=jnp.float32).astype(jnp.bfloat16).reshape(FRAMES, PATCHES, D)
    key = jnp.dot(tokens, qkv_weight[:, 1, :], preferred_element_type=jnp.float32).astype(jnp.bfloat16).reshape(FRAMES, PATCHES, D)
    value = jnp.dot(tokens, qkv_weight[:, 2, :], preferred_element_type=jnp.float32).astype(jnp.bfloat16).reshape(FRAMES, PATCHES, D)
    factor = 1.0 / HEAD_DIM ** 0.5

    def one_head(head):
        start = head * HEAD_DIM
        q_head = lax.dynamic_slice_in_dim(query, start, HEAD_DIM, 2).astype(jnp.float32)
        k_head = lax.dynamic_slice_in_dim(key, start, HEAD_DIM, 2).astype(jnp.float32)
        v_head = lax.dynamic_slice_in_dim(value, start, HEAD_DIM, 2).astype(jnp.float32)
        scores = jnp.einsum('fpc,gpc->pfg', q_head, k_head) * factor
        top = lax.optimization_barrier(jnp.max(scores, axis=-1, keepdims=True))
        expo = jnp.exp(scores - top)
        weights = (expo / lax.optimization_barrier(jnp.sum(expo, axis=-1, keepdims=True))).astype(jnp.bfloat16)
        return jnp.einsum('pfg,gpc->fpc', weights.astype(jnp.float32), v_head).astype(jnp.bfloat16)
    heads_out = lax.map(one_head, jnp.arange(HEADS, dtype=jnp.int32))
    attended = jnp.transpose(heads_out, (1, 2, 0, 3)).reshape(FRAMES * PATCHES, D)
    width = D // N_POOL
    summed = jnp.zeros((FRAMES * PATCHES, D), jnp.float32)
    for block in range(N_POOL):
        partial_value = jnp.dot(attended[:, block * width:(block + 1) * width], out_weight[block * width:(block + 1) * width], preferred_element_type=jnp.float32)
        partial_value = lax.optimization_barrier(partial_value.astype(jnp.bfloat16))
        summed = summed + partial_value.astype(jnp.float32)
    mixed = xf + summed.reshape(FRAMES, PATCHES, D)
    grouped = mixed.reshape(FRAMES, PATCHES, GROUPS, GROUP)
    scale = (lax.optimization_barrier(jnp.max(jnp.abs(grouped), axis=-1)) + 1e-06).astype(jnp.bfloat16)
    coded = (grouped / scale[..., None].astype(jnp.float32)).astype(jnp.bfloat16).reshape(FRAMES, PATCHES, D)
    scale_t = jnp.transpose(scale, (0, 2, 1))
    frame_ids = jnp.arange(FRAMES, dtype=jnp.int32)
    dest = (frame_ids // FR_DEV * N_POOL + owners) * CAP + slots
    shipped = jnp.zeros((SLOTS, PATCHES, D), jnp.bfloat16).at[dest].set(coded)
    shipped_scales = jnp.zeros((SLOTS, GROUPS, PATCHES), jnp.bfloat16).at[dest].set(scale_t)
    return (shipped, shipped_scales)
```

```python
import functools

import jax
import jax.numpy as jnp
from jax import lax
from jax.experimental import pallas as pl
from jax.experimental.pallas import tpu as pltpu
from jax.sharding import Mesh, PartitionSpec as P

HEAD_DIM = 88
GROUP = 128
MAIN = 64
SLOT = 32
FACTOR = 1.0 / HEAD_DIM**0.5
CHIP = ("zh", "zl", "x")
FRAME = CHIP + ("c",)
VMEM_LIMIT = 40 * 1024 * 1024
F32 = jnp.float32
BF16 = jnp.bfloat16


def lanes_of(shape):
    return lax.broadcasted_iota(jnp.int32, shape, len(shape) - 1)


def turn(value, shift):
    shift = shift % 128
    if shift == 0:
        return value
    return pltpu.roll(value, shift, len(value.shape) - 1)


def spread(value, axis):
    count = lax.axis_size(axis)
    copies = jnp.broadcast_to(value[None], (count,) + value.shape)
    return lax.all_to_all(copies, axis, 0, 0, tiled=True)


def project_kernel(core_ref, own_ref, other_ref, weight_ref, out_ref, rest_ref):
    step = pl.program_id(0)
    core = core_ref[0]
    chips = out_ref.shape[0]

    @pl.when(step == 0)
    def _():
        rest_ref[...] = jnp.zeros_like(rest_ref)

    lane = lanes_of(rest_ref.shape)
    for which, ref in enumerate((own_ref, other_ref)):
        frame = (core if which == 0 else 1 - core) * 4 + step
        rows = jnp.dot(ref[0], weight_ref[...], preferred_element_type=F32)
        for tile in range(2):
            block = rows[:, tile * 128 : (tile + 1) * 128].astype(BF16)
            out_ref[:, 2 * frame + tile] = block.reshape(chips, 8, 128)
        rest = jnp.where(lane < 8, rows[:, 256:384], 0.0)
        rest_ref[...] += pltpu.roll(rest, 8 * frame, 1)

    @pl.when(step == pl.num_programs(0) - 1)
    def _():
        out_ref[:, 16] = rest_ref[...].astype(BF16).reshape(chips, 8, 128)


def attend_kernel(x_ref, out_ref, q_ref, k_ref, v_ref, o_ref):
    chips = x_ref.shape[0]
    frames = chips * 8
    shape = (chips, 8, 128)
    lane = lanes_of(shape)
    rest = x_ref[:, 16].astype(F32)
    for fr in range(8):
        first = x_ref[:, 2 * fr].astype(F32)
        second = x_ref[:, 2 * fr + 1].astype(F32)
        rows = slice(fr * 8, fr * 8 + 8)
        q_ref[:, rows, :] = jnp.where(lane < HEAD_DIM, first, 0.0)
        k_ref[:, rows, :] = second
        v_ref[:, rows, :] = jnp.where(
            lane < 40,
            turn(first, 40),
            jnp.where(
                lane < 80,
                turn(second, 80),
                jnp.where(lane < HEAD_DIM, turn(rest, 80 - 8 * fr), 0.0),
            ),
        )
    for patch in range(8):
        pick = pl.ds(patch, 8, stride=8)
        query = q_ref[:, pick, :].reshape(frames, 128).astype(BF16)
        key = k_ref[:, pick, :].reshape(frames, 128).astype(BF16)
        value = v_ref[:, pick, :].reshape(frames, 128).astype(BF16)
        scores = lax.dot_general(query, key, (((1,), (1,)), ((), ())), preferred_element_type=F32)
        top = jnp.max(scores, axis=-1, keepdims=True)
        expo = jnp.exp((scores - top) * FACTOR)
        total = jnp.sum(expo, axis=-1, keepdims=True)
        mixed = jnp.dot(expo.astype(BF16), value, preferred_element_type=F32)
        o_ref[:, pick, :] = (mixed * (1.0 / total)).reshape(shape)
    for tile in range(4):
        even = o_ref[:, tile * 16 : tile * 16 + 8, :]
        odd = o_ref[:, tile * 16 + 8 : tile * 16 + 16, :]
        out_ref[:, tile] = jnp.where(lane < MAIN, even, turn(odd, MAIN)).astype(BF16)
    for tile in range(2):
        packed = None
        for part in range(4):
            fr = tile * 4 + part
            piece = turn(o_ref[:, fr * 8 : fr * 8 + 8, :], SLOT * part - MAIN)
            packed = piece if part == 0 else jnp.where(lane >= SLOT * part, piece, packed)
        out_ref[:, 4 + tile] = packed.astype(BF16)


def pack_kernel(owner_ref, x_ref, out_ref):
    chips = x_ref.shape[0]
    half, quarter = chips // 2, chips // 4
    out_ref[...] = jnp.zeros_like(out_ref)
    lane = lanes_of((half, 8, 128))
    lane_q = lanes_of((quarter, 8, 128))
    for fr in range(8):
        place = (fr // 4) * 8 + owner_ref[fr]
        tile = x_ref[:, fr // 2].astype(F32)
        low, high = tile[:half], tile[half:]
        side = fr % 2
        main = jnp.where(lane < MAIN, turn(low, MAIN * side), turn(high, MAIN * (1 - side)))
        out_ref[place, :half] = main.astype(BF16)
        tile = x_ref[:, 4 + fr // 4].astype(F32)
        packed = None
        for part in range(4):
            piece = turn(tile[part * quarter : (part + 1) * quarter], SLOT * (part - fr % 4))
            packed = piece if part == 0 else jnp.where(lane_q >= SLOT * part, piece, packed)
        out_ref[place, half:] = packed.astype(BF16)


def deliver_kernel(pick_ref, frame_ref, y_ref, weight_ref, out_ref, scale_ref):
    sources = y_ref.shape[0]
    patches, width = frame_ref.shape[1:]
    half, quarter = patches // 2, patches // 4
    tiles = half // 8
    valid = pick_ref[1] > 0
    lane = lanes_of((half, 128))
    lane_q = lanes_of((quarter, 128))
    mains, rests = [], []
    for pair in range(sources // 2):
        first = y_ref[2 * pair, :tiles].reshape(half, 128).astype(F32)
        second = y_ref[2 * pair + 1, :tiles].reshape(half, 128).astype(F32)
        low = jnp.where(lane < MAIN, first, turn(second, MAIN))
        high = jnp.where(lane < MAIN, turn(first, MAIN), second)
        mains.append(jnp.concatenate([low, high], axis=0).astype(BF16))
    for group in range(sources // 4):
        pieces = [
            y_ref[4 * group + part, tiles:].reshape(quarter, 128).astype(F32) for part in range(4)
        ]
        rows = []
        for block in range(4):
            packed = None
            for part in range(4):
                piece = turn(pieces[part], SLOT * (part - block))
                packed = piece if part == 0 else jnp.where(lane_q >= SLOT * part, piece, packed)
            rows.append(packed)
        rests.append(jnp.concatenate(rows, axis=0).astype(BF16))
    left = jnp.concatenate(mains, axis=1)
    left_rest = jnp.concatenate(rests, axis=1)
    lane_p = lanes_of((patches, 128))
    scales = jnp.zeros((patches, 128), F32)
    for start in range(0, width, 256):
        stop = min(start + 256, width)
        right = weight_ref[:, :MAIN, start:stop].reshape(sources * MAIN, stop - start)
        right_rest = weight_ref[:, MAIN:, start:stop].reshape(sources * SLOT, stop - start)
        total = jnp.dot(left, right, preferred_element_type=F32)
        total += jnp.dot(left_rest, right_rest, preferred_element_type=F32)
        total += frame_ref[0, :, start:stop].astype(F32)
        for at in range(0, stop - start, GROUP):
            part = total[:, at : at + GROUP]
            top = jnp.max(jnp.abs(part), axis=-1, keepdims=True)
            scale = (top + 1e-06).astype(BF16).astype(F32)
            coded = jnp.where(valid, part / scale, 0.0).astype(BF16)
            out_ref[0, :, start + at : start + at + GROUP] = coded
            scales = jnp.where(lane_p == (start + at) // GROUP, scale, scales)
    scales = jnp.where(valid, scales, 0.0).T
    scale_ref[0] = scales[: width // GROUP].astype(BF16)


def params():
    return pltpu.CompilerParams(vmem_limit_bytes=VMEM_LIMIT)


def local(frames_in, qkv_weight, out_weight, owners, slots):
    fr_count, patch_count, width = frames_in.shape
    rows_here = qkv_weight.shape[0]
    core = lax.axis_index("c")
    position = lax.axis_index("pool")
    chips = lax.axis_size("zh") * lax.axis_size("zl") * lax.axis_size("x")
    sources = 2 * lax.axis_size("pool")
    swap = [(0, 1), (1, 0)]

    xf = frames_in.astype(F32)
    mean = jnp.mean(xf, axis=-1, keepdims=True)
    centred = xf - mean
    var = jnp.mean(centred * centred, axis=-1, keepdims=True)
    normed = (centred * lax.rsqrt(var + 1e-06)).astype(BF16)
    normed_other = lax.ppermute(normed, "c", swap)
    owners_other = lax.ppermute(owners, "c", swap)

    parts = qkv_weight.reshape(rows_here, 3, 2, HEAD_DIM)
    query, key, value = parts[:, 0], parts[:, 1], parts[:, 2]
    back = out_weight.T.reshape(rows_here, 2, HEAD_DIM)
    blank = functools.partial(jnp.zeros, dtype=BF16)
    payload = jnp.concatenate(
        [
            query,
            value[..., :40],
            key,
            value[..., 40:80],
            value[..., 80:],
            blank((rows_here, 2, 24)),
            back,
            blank((rows_here, 2, 8)),
        ],
        axis=-1,
    )
    both = lax.all_gather(payload, "c", axis=0, tiled=True)
    mine = lax.dynamic_index_in_dim(both, core, 1, keepdims=False)
    mine = spread(mine, "zh").reshape(-1, mine.shape[-1])
    mine = spread(mine, ("zl", "x"))
    mine = mine.reshape(8, 4, 2 * rows_here, -1).transpose(1, 0, 2, 3).reshape(width, -1)

    projected = pl.pallas_call(
        project_kernel,
        grid=(fr_count,),
        in_specs=[
            pl.BlockSpec(memory_space=pltpu.SMEM),
            pl.BlockSpec((1, patch_count, width), lambda j: (j, 0, 0)),
            pl.BlockSpec((1, patch_count, width), lambda j: (j, 0, 0)),
            pl.BlockSpec((width, 384), lambda j: (0, 0)),
        ],
        out_specs=pl.BlockSpec((chips, 17, 8, 128), lambda j: (0, 0, 0, 0)),
        out_shape=jax.ShapeDtypeStruct((chips, 17, 8, 128), BF16),
        scratch_shapes=[pltpu.VMEM((patch_count, 128), F32)],
        compiler_params=params(),
        name="project",
    )(core.reshape(1), normed, normed_other, mine)
    tracks = lax.all_to_all(projected, CHIP, 0, 0, tiled=True)

    out_rows = lax.all_gather(mine[:, 288:].T, ("c", "pool"), axis=0, tiled=False)

    attended = pl.pallas_call(
        attend_kernel,
        out_shape=jax.ShapeDtypeStruct((chips, 6, 8, 128), BF16),
        scratch_shapes=[pltpu.VMEM((chips, 64, 128), F32)] * 4,
        compiler_params=params(),
        name="attend",
    )(tracks)
    returned = lax.all_to_all(attended, CHIP, 0, 0, tiled=True)

    pair = jnp.where(
        core == 0,
        jnp.concatenate([owners, owners_other]),
        jnp.concatenate([owners_other, owners]),
    )
    packed = pl.pallas_call(
        pack_kernel,
        in_specs=[
            pl.BlockSpec(memory_space=pltpu.SMEM),
            pl.BlockSpec(memory_space=pltpu.VMEM),
        ],
        out_specs=pl.BlockSpec(memory_space=pltpu.VMEM),
        out_shape=jax.ShapeDtypeStruct((sources, 3 * chips // 4, 8, 128), BF16),
        compiler_params=params(),
        name="pack",
    )(pair, returned)
    gathered = lax.all_to_all(packed, ("c", "pool"), 0, 0, tiled=True)

    match = (owners == position) & (slots == 0)
    chosen = jnp.sum(jnp.where(match, jnp.arange(fr_count, dtype=jnp.int32), 0))
    pick = jnp.stack([chosen, jnp.any(match).astype(jnp.int32)])
    groups = width // GROUP
    return pl.pallas_call(
        deliver_kernel,
        grid_spec=pltpu.PrefetchScalarGridSpec(
            num_scalar_prefetch=1,
            grid=(1,),
            in_specs=[
                pl.BlockSpec((1, patch_count, width), lambda g, pick: (pick[0], 0, 0)),
                pl.BlockSpec(gathered.shape, lambda g, pick: (0, 0, 0, 0)),
                pl.BlockSpec(out_rows.shape, lambda g, pick: (0, 0, 0)),
            ],
            out_specs=[
                pl.BlockSpec((1, patch_count, width), lambda g, pick: (0, 0, 0)),
                pl.BlockSpec((1, groups, patch_count), lambda g, pick: (0, 0, 0)),
            ],
        ),
        out_shape=[
            jax.ShapeDtypeStruct((1, patch_count, width), BF16),
            jax.ShapeDtypeStruct((1, groups, patch_count), BF16),
        ],
        compiler_params=params(),
        name="deliver",
    )(pick, frames_in, gathered, out_rows)


def solution(mesh):
    fine = Mesh(mesh.devices.reshape(4, 2, 4, 2, 8), ("zh", "zl", "x", "c", "pool"))
    run = jax.shard_map(
        local,
        mesh=fine,
        in_specs=(
            P(FRAME, None, None),
            P(FRAME, None, "pool"),
            P("pool", FRAME),
            P(FRAME),
            P(FRAME),
        ),
        out_specs=(P(FRAME + ("pool",), None, None), P(FRAME + ("pool",), None, None)),
        check_vma=False,
    )

    def whole(*args):
        shipped, scales = run(*args)
        return shipped, scales

    return whole
```

```python
import functools

import jax
import jax.numpy as jnp
from jax import lax
from jax.experimental import pallas as pl
from jax.experimental.pallas import tpu as pltpu
from jax.sharding import Mesh, PartitionSpec as P

HEAD_DIM = 88
GROUP = 128
MAIN = 64
SLOT = 32
FACTOR = 1.0 / HEAD_DIM**0.5
CHIP = ("zh", "zl", "x")
FRAME = CHIP + ("c",)
F32 = jnp.float32
BF16 = jnp.bfloat16


def lanes_of(shape):
    return lax.broadcasted_iota(jnp.int32, shape, len(shape) - 1)


def turn(value, shift):
    shift = shift % 128
    if shift == 0:
        return value
    return pltpu.roll(value, shift, len(value.shape) - 1)


def spread(value, axis):
    count = lax.axis_size(axis)
    copies = jnp.broadcast_to(value[None], (count,) + value.shape)
    return lax.all_to_all(copies, axis, 0, 0, tiled=True)


def project_kernel(
    core_ref, own_ref, other_ref, weight_ref, out_ref, back_ref, rest_ref, order_ref, right_ref
):
    step = pl.program_id(0)
    core = core_ref[0]
    chips = out_ref.shape[0]
    inner, height = weight_ref.shape[:2]
    outer = 4
    rows = height // outer

    @pl.when(step == 0)
    def _():
        rest_ref[...] = jnp.zeros_like(rest_ref)
        for low in range(inner):
            block = weight_ref[low].astype(F32)
            for high in range(outer):
                start = (high * inner + low) * rows
                order_ref[start : start + rows, :] = block[high * rows : (high + 1) * rows]
        right_ref[...] = order_ref[...].astype(BF16)
        back_ref[...] = order_ref[:, 256:384].T[32:].astype(BF16)

    lane = lanes_of(rest_ref.shape)
    for which, ref in enumerate((own_ref, other_ref)):
        frame = (core if which == 0 else 1 - core) * 4 + step
        out = jnp.dot(ref[0], right_ref[...], preferred_element_type=F32)
        for tile in range(2):
            block = out[:, tile * 128 : (tile + 1) * 128].astype(BF16)
            out_ref[:, 2 * frame + tile] = block.reshape(chips, 8, 128)
        rest = jnp.where(lane < 8, out[:, 256:384], 0.0)
        rest_ref[...] += pltpu.roll(rest, 8 * frame, 1)

    @pl.when(step == pl.num_programs(0) - 1)
    def _():
        out_ref[:, 16] = rest_ref[...].astype(BF16).reshape(chips, 8, 128)


def attend_kernel(x_ref, out_ref, q_ref, k_ref, v_ref, o_ref):
    chips = x_ref.shape[0]
    frames = chips * 8
    shape = (chips, 8, 128)
    lane = lanes_of(shape)
    rest = x_ref[:, 16].astype(F32)
    for fr in range(8):
        first = x_ref[:, 2 * fr].astype(F32)
        second = x_ref[:, 2 * fr + 1].astype(F32)
        rows = slice(fr * 8, fr * 8 + 8)
        q_ref[:, rows, :] = jnp.where(lane < HEAD_DIM, first, 0.0)
        k_ref[:, rows, :] = second
        v_ref[:, rows, :] = jnp.where(
            lane < 40,
            turn(first, 40),
            jnp.where(
                lane < 80,
                turn(second, 80),
                jnp.where(lane < HEAD_DIM, turn(rest, 80 - 8 * fr), 0.0),
            ),
        )
    for patch in range(8):
        pick = pl.ds(patch, 8, stride=8)
        query = q_ref[:, pick, :].reshape(frames, 128).astype(BF16)
        key = k_ref[:, pick, :].reshape(frames, 128).astype(BF16)
        value = v_ref[:, pick, :].reshape(frames, 128).astype(BF16)
        scores = lax.dot_general(query, key, (((1,), (1,)), ((), ())), preferred_element_type=F32)
        top = jnp.max(scores, axis=-1, keepdims=True)
        expo = jnp.exp((scores - top) * FACTOR)
        total = jnp.sum(expo, axis=-1, keepdims=True)
        mixed = jnp.dot(expo.astype(BF16), value, preferred_element_type=F32)
        o_ref[:, pick, :] = (mixed * (1.0 / total)).reshape(shape)
    for tile in range(4):
        even = o_ref[:, tile * 16 : tile * 16 + 8, :]
        odd = o_ref[:, tile * 16 + 8 : tile * 16 + 16, :]
        out_ref[:, tile] = jnp.where(lane < MAIN, even, turn(odd, MAIN)).astype(BF16)
    for tile in range(2):
        packed = None
        for part in range(4):
            fr = tile * 4 + part
            piece = turn(o_ref[:, fr * 8 : fr * 8 + 8, :], SLOT * part - MAIN)
            packed = piece if part == 0 else jnp.where(lane >= SLOT * part, piece, packed)
        out_ref[:, 4 + tile] = packed.astype(BF16)


def pack_kernel(owner_ref, x_ref, ready_ref, out_ref):
    chips = x_ref.shape[0]
    half, quarter = chips // 2, chips // 4
    out_ref[...] = jnp.zeros_like(out_ref)
    lane = lanes_of((half, 8, 128))
    lane_q = lanes_of((quarter, 8, 128))
    for fr in range(8):
        place = (fr // 4) * 8 + owner_ref[fr]
        tile = x_ref[:, fr // 2].astype(F32)
        low, high = tile[:half], tile[half:]
        side = fr % 2
        main = jnp.where(lane < MAIN, turn(low, MAIN * side), turn(high, MAIN * (1 - side)))
        out_ref[place, :half] = main.astype(BF16)
        tile = x_ref[:, 4 + fr // 4].astype(F32)
        packed = None
        for part in range(4):
            piece = turn(tile[part * quarter : (part + 1) * quarter], SLOT * (part - fr % 4))
            packed = piece if part == 0 else jnp.where(lane_q >= SLOT * part, piece, packed)
        out_ref[place, half:] = packed.astype(BF16)


def deliver_kernel(pick_ref, frame_ref, y_ref, far_ref, out_ref, scale_ref, weight_ref, sems):
    sources = y_ref.shape[0]
    patches, width = frame_ref.shape[1:]
    chunks = [(start, min(start + 256, width)) for start in range(0, width, 256)]
    copies = []
    for index, (start, stop) in enumerate(chunks):
        columns = pl.ds(start, stop - start)
        copies.append(
            pltpu.make_async_copy(
                far_ref.at[:, :, columns], weight_ref.at[:, :, columns], sems.at[index]
            )
        )
        copies[-1].start()
    half, quarter = patches // 2, patches // 4
    tiles = half // 8
    valid = pick_ref[1] > 0
    lane = lanes_of((half, 128))
    lane_q = lanes_of((quarter, 128))
    mains, rests = [], []
    for pair in range(sources // 2):
        first = y_ref[2 * pair, :tiles].reshape(half, 128).astype(F32)
        second = y_ref[2 * pair + 1, :tiles].reshape(half, 128).astype(F32)
        low = jnp.where(lane < MAIN, first, turn(second, MAIN))
        high = jnp.where(lane < MAIN, turn(first, MAIN), second)
        mains.append(jnp.concatenate([low, high], axis=0).astype(BF16))
    for group in range(sources // 4):
        pieces = [
            y_ref[4 * group + part, tiles:].reshape(quarter, 128).astype(F32) for part in range(4)
        ]
        rows = []
        for block in range(4):
            packed = None
            for part in range(4):
                piece = turn(pieces[part], SLOT * (part - block))
                packed = piece if part == 0 else jnp.where(lane_q >= SLOT * part, piece, packed)
            rows.append(packed)
        rests.append(jnp.concatenate(rows, axis=0).astype(BF16))
    left = jnp.concatenate(mains, axis=1)
    left_rest = jnp.concatenate(rests, axis=1)
    lane_p = lanes_of((patches, 128))
    scales = jnp.zeros((patches, 128), F32)
    for copy, (start, stop) in zip(copies, chunks):
        copy.wait()
        right = weight_ref[:, :MAIN, start:stop].reshape(sources * MAIN, stop - start)
        right_rest = weight_ref[:, MAIN:, start:stop].reshape(sources * SLOT, stop - start)
        total = jnp.dot(left, right, preferred_element_type=F32)
        total += jnp.dot(left_rest, right_rest, preferred_element_type=F32)
        total += frame_ref[0, :, start:stop].astype(F32)
        for at in range(0, stop - start, GROUP):
            part = total[:, at : at + GROUP]
            top = jnp.max(jnp.abs(part), axis=-1, keepdims=True)
            scale = (top + 1e-06).astype(BF16).astype(F32)
            coded = jnp.where(valid, part / scale, 0.0).astype(BF16)
            out_ref[0, :, start + at : start + at + GROUP] = coded
            scales = jnp.where(lane_p == (start + at) // GROUP, scale, scales)
    scales = jnp.where(valid, scales, 0.0).T
    scale_ref[0] = scales[: width // GROUP].astype(BF16)


def normalise(frames):
    xf = frames.astype(F32)
    mean = jnp.mean(xf, axis=-1, keepdims=True)
    centred = xf - mean
    var = jnp.mean(centred * centred, axis=-1, keepdims=True)
    return (centred * lax.rsqrt(var + 1e-06)).astype(BF16)


def params(mebibytes):
    return pltpu.CompilerParams(vmem_limit_bytes=mebibytes * 1024 * 1024)


def local(frames_in, qkv_weight, out_weight, owners, slots):
    fr_count, patch_count, width = frames_in.shape
    rows_here = qkv_weight.shape[0]
    core = lax.axis_index("c")
    position = lax.axis_index("pool")
    chips = lax.axis_size("zh") * lax.axis_size("zl") * lax.axis_size("x")
    sources = 2 * lax.axis_size("pool")
    swap = [(0, 1), (1, 0)]

    normed = normalise(frames_in)
    normed_other = normalise(lax.ppermute(frames_in, "c", swap))
    owners_other = lax.ppermute(owners, "c", swap)

    parts = qkv_weight.reshape(rows_here, 3, 2, HEAD_DIM)
    query, key, value = parts[:, 0], parts[:, 1], parts[:, 2]
    back = out_weight.T.reshape(rows_here, 2, HEAD_DIM)
    blank = functools.partial(jnp.zeros, dtype=BF16)
    payload = jnp.concatenate(
        [
            query,
            value[..., :40],
            key,
            value[..., 40:80],
            value[..., 80:],
            blank((rows_here, 2, 24)),
            back,
            blank((rows_here, 2, 8)),
        ],
        axis=-1,
    )
    both = lax.all_gather(payload, "c", axis=0, tiled=True)
    mine = lax.dynamic_index_in_dim(both, core, 1, keepdims=False)
    mine = spread(mine, "zh").reshape(-1, mine.shape[-1])
    mine = spread(mine, ("zl", "x"))
    projected, back = pl.pallas_call(
        project_kernel,
        grid=(fr_count,),
        in_specs=[
            pl.BlockSpec(memory_space=pltpu.SMEM),
            pl.BlockSpec((1, patch_count, width), lambda j: (j, 0, 0)),
            pl.BlockSpec((1, patch_count, width), lambda j: (j, 0, 0)),
            pl.BlockSpec(mine.shape, lambda j: (0, 0, 0)),
        ],
        out_specs=[
            pl.BlockSpec((chips, 17, 8, 128), lambda j: (0, 0, 0, 0)),
            pl.BlockSpec((96, width), lambda j: (0, 0)),
        ],
        out_shape=[
            jax.ShapeDtypeStruct((chips, 17, 8, 128), BF16),
            jax.ShapeDtypeStruct((96, width), BF16),
        ],
        scratch_shapes=[
            pltpu.VMEM((patch_count, 128), F32),
            pltpu.VMEM((width, 384), F32),
            pltpu.VMEM((width, 384), BF16),
        ],
        compiler_params=params(60),
        name="project",
    )(core.reshape(1), normed, normed_other, mine)
    tracks = lax.all_to_all(projected, CHIP, 0, 0, tiled=True)

    out_rows = lax.all_gather(back, ("c", "pool"), axis=0, tiled=False)

    attended = pl.pallas_call(
        attend_kernel,
        out_shape=jax.ShapeDtypeStruct((chips, 6, 8, 128), BF16),
        scratch_shapes=[pltpu.VMEM((chips, 64, 128), F32)] * 4,
        compiler_params=params(60),
        name="attend",
    )(tracks)
    returned = lax.all_to_all(attended, CHIP, 0, 0, tiled=True)

    pair = jnp.where(
        core == 0,
        jnp.concatenate([owners, owners_other]),
        jnp.concatenate([owners_other, owners]),
    )
    packed = pl.pallas_call(
        pack_kernel,
        in_specs=[
            pl.BlockSpec(memory_space=pltpu.SMEM),
            pl.BlockSpec(memory_space=pltpu.VMEM),
            pl.BlockSpec(memory_space=pltpu.VMEM),
        ],
        out_specs=pl.BlockSpec(memory_space=pltpu.VMEM),
        out_shape=jax.ShapeDtypeStruct((sources, 3 * chips // 4, 8, 128), BF16),
        compiler_params=params(60),
        name="pack",
    )(pair, returned, out_rows[0, :16, :128])
    gathered = lax.all_to_all(packed, ("c", "pool"), 0, 0, tiled=True)

    match = (owners == position) & (slots == 0)
    chosen = jnp.sum(jnp.where(match, jnp.arange(fr_count, dtype=jnp.int32), 0))
    pick = jnp.stack([chosen, jnp.any(match).astype(jnp.int32)])
    groups = width // GROUP
    return pl.pallas_call(
        deliver_kernel,
        grid_spec=pltpu.PrefetchScalarGridSpec(
            num_scalar_prefetch=1,
            grid=(1,),
            in_specs=[
                pl.BlockSpec((1, patch_count, width), lambda g, pick: (pick[0], 0, 0)),
                pl.BlockSpec(gathered.shape, lambda g, pick: (0, 0, 0, 0)),
                pl.BlockSpec(memory_space=pltpu.HBM),
            ],
            out_specs=[
                pl.BlockSpec((1, patch_count, width), lambda g, pick: (0, 0, 0)),
                pl.BlockSpec((1, groups, patch_count), lambda g, pick: (0, 0, 0)),
            ],
            scratch_shapes=[
                pltpu.VMEM(out_rows.shape, BF16),
                pltpu.SemaphoreType.DMA((-(-width // 256),)),
            ],
        ),
        out_shape=[
            jax.ShapeDtypeStruct((1, patch_count, width), BF16),
            jax.ShapeDtypeStruct((1, groups, patch_count), BF16),
        ],
        compiler_params=params(60),
        name="deliver",
    )(pick, frames_in, gathered, out_rows)


def solution(mesh):
    fine = Mesh(mesh.devices.reshape(4, 2, 4, 2, 8), ("zh", "zl", "x", "c", "pool"))
    run = jax.shard_map(
        local,
        mesh=fine,
        in_specs=(
            P(FRAME, None, None),
            P(FRAME, None, "pool"),
            P("pool", FRAME),
            P(FRAME),
            P(FRAME),
        ),
        out_specs=(P(FRAME + ("pool",), None, None), P(FRAME + ("pool",), None, None)),
        check_vma=False,
    )

    def whole(*args):
        shipped, scales = run(*args)
        return shipped, scales

    return whole
```

```python
import jax
import jax.numpy as jnp
from jax import lax
from jax.experimental import pallas as pl
from jax.experimental.pallas import tpu as pltpu
from jax.sharding import Mesh, PartitionSpec as P

HEAD_DIM = 88
GROUP = 128
MAIN = 64
SLOT = 32
TRACK, PACK, DELIVER = 60, 60, 30
FACTOR = 1.0 / HEAD_DIM**0.5
CHIP = ("zh", "zl", "x")
FRAME = CHIP + ("c",)
F32 = jnp.float32
BF16 = jnp.bfloat16


def lanes_of(shape):
    return lax.broadcasted_iota(jnp.int32, shape, len(shape) - 1)


def turn(value, shift):
    shift = shift % 128
    if shift == 0:
        return value
    return pltpu.roll(value, shift, len(value.shape) - 1)


def spread(value, axis):
    count = lax.axis_size(axis)
    copies = jnp.broadcast_to(value[None], (count,) + value.shape)
    return lax.all_to_all(copies, axis, 0, 0, tiled=True)


def order_rows(source_ref, order_ref):
    inner, height = source_ref.shape[:2]
    outer = 4
    rows = height // outer
    for low in range(inner):
        block = source_ref[low].astype(F32)
        for high in range(outer):
            start = (high * inner + low) * rows
            order_ref[start : start + rows, :] = block[high * rows : (high + 1) * rows]


def track_kernel(
    core_ref, tokens_ref, own_ref, other_ref, out_ref, back_ref, order_ref, right_ref, o_ref
):
    step = pl.program_id(0)
    core = core_ref[0]
    frames = 2 * tokens_ref.shape[1]
    lane = lanes_of((frames, 128))

    @pl.when(step == 0)
    def _():
        for which, ref in enumerate((own_ref, other_ref)):
            order_rows(ref, order_ref)
            right_ref[:, which * 384 : which * 384 + 384] = order_ref[...].astype(BF16)
            if which == 0:
                turned = [order_ref[:, at : at + 128].T[HEAD_DIM:] for at in (0, 128, 256)]
                back_ref[...] = jnp.concatenate(turned, axis=0)[:96].astype(BF16)

    tokens = tokens_ref[...].reshape(frames, tokens_ref.shape[2])
    both = jnp.dot(tokens, right_ref[...], preferred_element_type=F32)
    for which in range(2):
        head = core if which == 0 else 1 - core
        out = both[:, which * 384 : which * 384 + 384]
        query = jnp.where(lane < HEAD_DIM, out[:, :128], 0.0).astype(BF16)
        key = out[:, 128:256].astype(BF16)
        value = jnp.where(lane < HEAD_DIM, out[:, 256:], 0.0).astype(BF16)
        scores = lax.dot_general(query, key, (((1,), (1,)), ((), ())), preferred_element_type=F32)
        top = jnp.max(scores, axis=-1, keepdims=True)
        expo = jnp.exp((scores - top) * FACTOR)
        total = jnp.sum(expo, axis=-1, keepdims=True)
        mixed = jnp.dot(expo.astype(BF16), value, preferred_element_type=F32)
        mixed = (mixed * (1.0 / total)).reshape(frames // 8, 8, 128)
        o_ref[:, pl.ds(head * 4 + step, 8, stride=8), :] = mixed

    @pl.when(step == pl.num_programs(0) - 1)
    def _():
        pairs = frames // 16
        lane_o = lanes_of((pairs, 8, 128))

        def piece_of(side, owner, late, odd):
            start = (side * 4 + owner * 2 + odd) * 8
            return o_ref[late * pairs : (late + 1) * pairs, start : start + 8, :]

        for side in range(2):
            for owner in range(2):
                rest = None
                for late in range(2):
                    even, odd = (piece_of(side, owner, late, at) for at in range(2))
                    main = jnp.where(lane_o < MAIN, even, turn(odd, MAIN))
                    out_ref[:, side, owner * 2 + late] = main.astype(BF16)
                    for at, piece in enumerate((even, odd)):
                        part = late * 2 + at
                        piece = turn(piece, SLOT * part - MAIN)
                        rest = piece if part == 0 else jnp.where(lane_o >= SLOT * part, piece, rest)
                out_ref[:, side, 4 + owner] = rest.astype(BF16)


def half_turn(value):
    return pltpu.roll(value, 4, 1)


def pack_kernel(owner_ref, x_ref, out_ref):
    pairs = x_ref.shape[0]
    out_ref[...] = jnp.zeros_like(out_ref)

    def join(even, odd, lane, edges):
        shape = even[0].shape
        upper = lax.broadcasted_iota(jnp.int32, shape, 1) < 4
        first = jnp.where(upper, even[0], half_turn(odd[0]))
        second = jnp.where(upper, half_turn(even[1]), odd[1])
        return jnp.where(lane < edges, first, second)

    lane = lanes_of((pairs, 8, 128))
    lane_h = lanes_of((pairs // 2, 8, 128))
    for fr in range(8):
        place = (fr // 4) * 8 + owner_ref[fr]
        tiles = [x_ref[:, side, fr // 2].astype(F32) for side in range(2)]
        even, odd = (
            [turn(tile, MAIN * head - MAIN * (fr % 2)) for head in range(2)] for tile in tiles
        )
        out_ref[place, :pairs] = join(even, odd, lane, MAIN).astype(BF16)
        tiles = [x_ref[:, side, 4 + fr // 4].astype(F32) for side in range(2)]
        rests = []
        for half in range(2):
            rows = slice(half * (pairs // 2), (half + 1) * (pairs // 2))
            even, odd = (
                [
                    turn(tile[rows], 2 * SLOT * half + SLOT * head - SLOT * (fr % 4))
                    for head in range(2)
                ]
                for tile in tiles
            )
            rests.append(join(even, odd, lane_h, 2 * SLOT * half + SLOT))
        rest = jnp.where(lane_h < 2 * SLOT, rests[0], rests[1])
        out_ref[place, pairs:] = rest.astype(BF16)


def deliver_kernel(pick_ref, frame_ref, y_ref, first_ref, second_ref, out_ref, scale_ref):
    sources = y_ref.shape[0]
    heads = sources // 2
    patches, width = frame_ref.shape[1:]
    half = patches // 2
    tiles = half // 8
    valid = pick_ref[1] > 0
    lane = lanes_of((half, 128))

    def weave(first, second):
        upper = lax.broadcasted_iota(jnp.int32, first.shape, 1) < 4
        even = jnp.where(upper, first, half_turn(second))
        odd = jnp.where(upper, half_turn(first), second)
        return jnp.stack([even, odd], axis=1).reshape(first.shape[0] * 16, 128)

    mains, rests = [], []
    for at in range(heads):
        pair = [y_ref[core * heads + at, :tiles].astype(F32) for core in range(2)]
        mains.append(weave(*pair).astype(BF16))
    for at in range(0, heads, 2):
        first, second = (
            weave(*(y_ref[core * heads + one, tiles:].astype(F32) for core in range(2)))
            for one in (at, at + 1)
        )
        low = jnp.where(lane < MAIN, first, turn(second, MAIN))
        high = jnp.where(lane < MAIN, turn(first, MAIN), second)
        rests.append(jnp.concatenate([low, high], axis=0).astype(BF16))
    left = jnp.concatenate(mains, axis=1)
    left_rest = jnp.concatenate(rests, axis=1)
    lane_p = lanes_of((patches, 128))
    scales = jnp.zeros((patches, 128), F32)
    for start in range(0, width, 256):
        stop = min(start + 256, width)
        right, right_rest = (
            jnp.concatenate([ref[:, rows, start:stop] for ref in (first_ref, second_ref)], axis=1)
            for rows in (slice(0, MAIN), slice(MAIN, MAIN + SLOT))
        )
        right = right.reshape(heads * 2 * MAIN, stop - start)
        right_rest = right_rest.reshape(heads * 2 * SLOT, stop - start)
        total = jnp.dot(left, right, preferred_element_type=F32)
        total += jnp.dot(left_rest, right_rest, preferred_element_type=F32)
        total += frame_ref[0, :, start:stop].astype(F32)
        for at in range(0, stop - start, GROUP):
            part = total[:, at : at + GROUP]
            top = jnp.max(jnp.abs(part), axis=-1, keepdims=True)
            scale = (top + 1e-06).astype(BF16).astype(F32)
            coded = jnp.where(valid, part / scale, 0.0).astype(BF16)
            out_ref[0, :, start + at : start + at + GROUP] = coded
            scales = jnp.where(lane_p == (start + at) // GROUP, scale, scales)
    scales = jnp.where(valid, scales, 0.0).T
    scale_ref[0] = scales[: width // GROUP].astype(BF16)


def normalise(frames):
    xf = frames.astype(F32)
    mean = jnp.mean(xf, axis=-1, keepdims=True)
    centred = xf - mean
    var = jnp.mean(centred * centred, axis=-1, keepdims=True)
    return (centred * lax.rsqrt(var + 1e-06)).astype(BF16)


def params(mebibytes):
    return pltpu.CompilerParams(vmem_limit_bytes=mebibytes * 1024 * 1024)


def local(frames_in, qkv_weight, out_weight, owners, slots):
    fr_count, patch_count, width = frames_in.shape
    rows_here = qkv_weight.shape[0]
    core = lax.axis_index("c")
    position = lax.axis_index("pool")
    chips = lax.axis_size("zh") * lax.axis_size("zl") * lax.axis_size("x")
    sources = 2 * lax.axis_size("pool")
    swap = [(0, 1), (1, 0)]

    share = frames_in.reshape(2, 2, 2 * chips, 4, width)
    share = lax.dynamic_index_in_dim(share, position % 2, 0, keepdims=False)
    share = lax.dynamic_index_in_dim(share, position // 2, 2, keepdims=False)
    share = normalise(share).transpose(1, 0, 2)
    share = lax.all_to_all(share, FRAME, 0, 0, tiled=True).reshape(4 * chips, width)
    tracks = lax.all_gather(share, "pool", axis=0, tiled=False)
    owners_other = lax.ppermute(owners, "c", swap)

    parts = qkv_weight.reshape(rows_here, 3, 2, HEAD_DIM)
    query, key, value = parts[:, 0], parts[:, 1], parts[:, 2]
    back = out_weight.T.reshape(rows_here, 2, HEAD_DIM)
    payload = jnp.concatenate(
        [
            query,
            back[..., :40],
            key,
            back[..., 40:80],
            value,
            back[..., 80:],
            jnp.zeros((rows_here, 2, 32), BF16),
        ],
        axis=-1,
    )
    both = lax.all_gather(payload, "c", axis=0, tiled=True)
    mine = lax.dynamic_index_in_dim(both, core, 1, keepdims=False)
    mine = spread(mine, "zh").reshape(-1, mine.shape[-1])
    mine = spread(mine, ("zl", "x"))
    mine_other = lax.ppermute(mine, "c", swap)
    attended, back_rows = pl.pallas_call(
        track_kernel,
        grid=(4,),
        in_specs=[
            pl.BlockSpec(memory_space=pltpu.SMEM),
            pl.BlockSpec((2, 4 * chips, width), lambda p: (p, 0, 0)),
            pl.BlockSpec(mine.shape, lambda p: (0, 0, 0)),
            pl.BlockSpec(mine.shape, lambda p: (0, 0, 0)),
        ],
        out_specs=[
            pl.BlockSpec((chips // 2, 2, 6, 8, 128), lambda p: (0, 0, 0, 0, 0)),
            pl.BlockSpec((96, width), lambda p: (0, 0)),
        ],
        out_shape=[
            jax.ShapeDtypeStruct((chips // 2, 2, 6, 8, 128), BF16),
            jax.ShapeDtypeStruct((96, width), BF16),
        ],
        scratch_shapes=[
            pltpu.VMEM((width, 384), F32),
            pltpu.VMEM((width, 768), BF16),
            pltpu.VMEM((chips, 64, 128), F32),
        ],
        compiler_params=params(TRACK),
        name="track",
    )(core.reshape(1), tracks, mine, mine_other)
    attended = attended.reshape(chips, 6, 8, 128)
    out_rows = lax.all_gather(back_rows, "pool", axis=0, tiled=False)

    returned = lax.all_to_all(attended, CHIP, 0, 0, tiled=True)

    pair = jnp.where(
        core == 0,
        jnp.concatenate([owners, owners_other]),
        jnp.concatenate([owners_other, owners]),
    )
    packed = pl.pallas_call(
        pack_kernel,
        in_specs=[
            pl.BlockSpec(memory_space=pltpu.SMEM),
            pl.BlockSpec(memory_space=pltpu.VMEM),
        ],
        out_specs=pl.BlockSpec(memory_space=pltpu.VMEM),
        out_shape=jax.ShapeDtypeStruct((sources, 3 * chips // 4, 8, 128), BF16),
        compiler_params=params(PACK),
        name="pack",
    )(pair, returned.reshape(chips // 2, 2, 6, 8, 128))
    gathered = lax.all_to_all(packed, ("c", "pool"), 0, 0, tiled=True)

    match = (owners == position) & (slots == 0)
    chosen = jnp.sum(jnp.where(match, jnp.arange(fr_count, dtype=jnp.int32), 0))
    pick = jnp.stack([chosen, jnp.any(match).astype(jnp.int32)])
    groups = width // GROUP
    one = 1.0 - packed[0, 0, 0, 0].astype(F32) * 0.0
    near_rows = out_rows * one.astype(BF16)
    far_rows = lax.ppermute(near_rows, "c", swap)
    first_rows = jnp.where(core == 0, near_rows, far_rows)
    second_rows = jnp.where(core == 0, far_rows, near_rows)
    return pl.pallas_call(
        deliver_kernel,
        grid_spec=pltpu.PrefetchScalarGridSpec(
            num_scalar_prefetch=1,
            grid=(1,),
            in_specs=[
                pl.BlockSpec((1, patch_count, width), lambda g, pick: (pick[0], 0, 0)),
                pl.BlockSpec(gathered.shape, lambda g, pick: (0, 0, 0, 0)),
                pl.BlockSpec(out_rows.shape, lambda g, pick: (0, 0, 0)),
                pl.BlockSpec(out_rows.shape, lambda g, pick: (0, 0, 0)),
            ],
            out_specs=[
                pl.BlockSpec((1, patch_count, width), lambda g, pick: (0, 0, 0)),
                pl.BlockSpec((1, groups, patch_count), lambda g, pick: (0, 0, 0)),
            ],
        ),
        out_shape=[
            jax.ShapeDtypeStruct((1, patch_count, width), BF16),
            jax.ShapeDtypeStruct((1, groups, patch_count), BF16),
        ],
        compiler_params=params(DELIVER),
        name="deliver",
    )(pick, frames_in, gathered, first_rows, second_rows)


def solution(mesh):
    fine = Mesh(mesh.devices.reshape(4, 2, 4, 2, 8), ("zh", "zl", "x", "c", "pool"))
    run = jax.shard_map(
        local,
        mesh=fine,
        in_specs=(
            P(FRAME, None, None),
            P(FRAME, None, "pool"),
            P("pool", FRAME),
            P(FRAME),
            P(FRAME),
        ),
        out_specs=(P(FRAME + ("pool",), None, None), P(FRAME + ("pool",), None, None)),
        check_vma=False,
    )

    def whole(*args):
        shipped, scales = run(*args)
        return shipped, scales

    return whole
```

```python
import jax
import jax.numpy as jnp
from jax import lax
from jax.experimental import pallas as pl
from jax.experimental.pallas import tpu as pltpu
from jax.sharding import Mesh, PartitionSpec as P

HEAD_DIM = 88
GROUP = 128
MAIN = 64
SLOT = 32
ORDER, TRACK, PACK, DELIVER = 30, 40, 40, 30
FACTOR = 1.0 / HEAD_DIM**0.5
CHIP = ("zh", "zl", "x")
FRAME = CHIP + ("c",)
F32 = jnp.float32
BF16 = jnp.bfloat16


def lanes_of(shape):
    return lax.broadcasted_iota(jnp.int32, shape, len(shape) - 1)


def turn(value, shift):
    shift = shift % 128
    if shift == 0:
        return value
    return pltpu.roll(value, shift, len(value.shape) - 1)


def spread(value, axis):
    count = lax.axis_size(axis)
    copies = jnp.broadcast_to(value[None], (count,) + value.shape)
    return lax.all_to_all(copies, axis, 0, 0, tiled=True)


def order_kernel(source_ref, right_ref, back_ref, order_ref):
    inner, height = source_ref.shape[:2]
    outer = 4
    rows = height // outer
    for low in range(inner):
        block = source_ref[low].astype(F32)
        for high in range(outer):
            start = (high * inner + low) * rows
            order_ref[start : start + rows, :] = block[high * rows : (high + 1) * rows]
    right_ref[...] = order_ref[...].astype(BF16)
    turned = [order_ref[:, at : at + 128].T[HEAD_DIM:] for at in (0, 128, 256)]
    back_ref[...] = jnp.concatenate(turned, axis=0)[:96].astype(BF16)


def track_kernel(core_ref, tokens_ref, own_ref, other_ref, out_ref, o_ref):
    step = pl.program_id(0)
    core = core_ref[0]
    frames = 2 * tokens_ref.shape[1]
    lane = lanes_of((frames, 128))
    tokens = tokens_ref[...].reshape(frames, tokens_ref.shape[2])
    right = jnp.concatenate([own_ref[...], other_ref[...]], axis=1)
    both = jnp.dot(tokens, right, preferred_element_type=F32)
    for which in range(2):
        head = core if which == 0 else 1 - core
        out = both[:, which * 384 : which * 384 + 384]
        query = jnp.where(lane < HEAD_DIM, out[:, :128], 0.0).astype(BF16)
        key = out[:, 128:256].astype(BF16)
        value = jnp.where(lane < HEAD_DIM, out[:, 256:], 0.0).astype(BF16)
        scores = lax.dot_general(query, key, (((1,), (1,)), ((), ())), preferred_element_type=F32)
        top = jnp.max(scores, axis=-1, keepdims=True)
        expo = jnp.exp((scores - top) * FACTOR)
        total = jnp.sum(expo, axis=-1, keepdims=True)
        mixed = jnp.dot(expo.astype(BF16), value, preferred_element_type=F32)
        mixed = (mixed * (1.0 / total)).reshape(frames // 8, 8, 128)
        o_ref[:, pl.ds(head * 4 + step, 8, stride=8), :] = mixed

    @pl.when(step == pl.num_programs(0) - 1)
    def _():
        pairs = frames // 16
        lane_o = lanes_of((pairs, 8, 128))

        def piece_of(side, owner, late, odd):
            start = (side * 4 + owner * 2 + odd) * 8
            return o_ref[late * pairs : (late + 1) * pairs, start : start + 8, :]

        for side in range(2):
            for owner in range(2):
                rest = None
                for late in range(2):
                    even, odd = (piece_of(side, owner, late, at) for at in range(2))
                    main = jnp.where(lane_o < MAIN, even, turn(odd, MAIN))
                    out_ref[:, side, owner * 2 + late] = main.astype(BF16)
                    for at, piece in enumerate((even, odd)):
                        part = late * 2 + at
                        piece = turn(piece, SLOT * part - MAIN)
                        rest = piece if part == 0 else jnp.where(lane_o >= SLOT * part, piece, rest)
                out_ref[:, side, 4 + owner] = rest.astype(BF16)


def half_turn(value):
    return pltpu.roll(value, 4, 1)


def pack_kernel(owner_ref, x_ref, out_ref):
    pairs = x_ref.shape[0]
    out_ref[...] = jnp.zeros_like(out_ref)

    def join(even, odd, lane, edges):
        shape = even[0].shape
        upper = lax.broadcasted_iota(jnp.int32, shape, 1) < 4
        first = jnp.where(upper, even[0], half_turn(odd[0]))
        second = jnp.where(upper, half_turn(even[1]), odd[1])
        return jnp.where(lane < edges, first, second)

    lane = lanes_of((pairs, 8, 128))
    lane_h = lanes_of((pairs // 2, 8, 128))
    for fr in range(8):
        place = (fr // 4) * 8 + owner_ref[fr]
        tiles = [x_ref[:, side, fr // 2].astype(F32) for side in range(2)]
        even, odd = (
            [turn(tile, MAIN * head - MAIN * (fr % 2)) for head in range(2)] for tile in tiles
        )
        out_ref[place, :pairs] = join(even, odd, lane, MAIN).astype(BF16)
        tiles = [x_ref[:, side, 4 + fr // 4].astype(F32) for side in range(2)]
        rests = []
        for half in range(2):
            rows = slice(half * (pairs // 2), (half + 1) * (pairs // 2))
            even, odd = (
                [
                    turn(tile[rows], 2 * SLOT * half + SLOT * head - SLOT * (fr % 4))
                    for head in range(2)
                ]
                for tile in tiles
            )
            rests.append(join(even, odd, lane_h, 2 * SLOT * half + SLOT))
        rest = jnp.where(lane_h < 2 * SLOT, rests[0], rests[1])
        out_ref[place, pairs:] = rest.astype(BF16)


def deliver_kernel(pick_ref, frame_ref, y_ref, weight_ref, out_ref, scale_ref):
    sources = y_ref.shape[0]
    heads = sources // 2
    patches, width = frame_ref.shape[1:]
    half = patches // 2
    tiles = half // 8
    valid = pick_ref[1] > 0
    lane = lanes_of((half, 128))

    def weave(first, second):
        upper = lax.broadcasted_iota(jnp.int32, first.shape, 1) < 4
        even = jnp.where(upper, first, half_turn(second))
        odd = jnp.where(upper, half_turn(first), second)
        return jnp.stack([even, odd], axis=1).reshape(first.shape[0] * 16, 128)

    mains, rests = [], []
    for at in range(heads):
        pair = [y_ref[core * heads + at, :tiles].astype(F32) for core in range(2)]
        mains.append(weave(*pair).astype(BF16))
    for at in range(0, heads, 2):
        first, second = (
            weave(*(y_ref[core * heads + one, tiles:].astype(F32) for core in range(2)))
            for one in (at, at + 1)
        )
        low = jnp.where(lane < MAIN, first, turn(second, MAIN))
        high = jnp.where(lane < MAIN, turn(first, MAIN), second)
        rests.append(jnp.concatenate([low, high], axis=0).astype(BF16))
    left = jnp.concatenate(mains, axis=1)
    left_rest = jnp.concatenate(rests, axis=1)
    lane_p = lanes_of((patches, 128))
    scales = jnp.zeros((patches, 128), F32)
    for start in range(0, width, 256):
        stop = min(start + 256, width)
        right, right_rest = (
            jnp.concatenate(
                [weight_ref[at : at + heads, rows, start:stop] for at in (0, heads)], axis=1
            )
            for rows in (slice(0, MAIN), slice(MAIN, MAIN + SLOT))
        )
        right = right.reshape(heads * 2 * MAIN, stop - start)
        right_rest = right_rest.reshape(heads * 2 * SLOT, stop - start)
        total = jnp.dot(left, right, preferred_element_type=F32)
        total += jnp.dot(left_rest, right_rest, preferred_element_type=F32)
        total += frame_ref[0, :, start:stop].astype(F32)
        for at in range(0, stop - start, GROUP):
            part = total[:, at : at + GROUP]
            top = jnp.max(jnp.abs(part), axis=-1, keepdims=True)
            scale = (top + 1e-06).astype(BF16).astype(F32)
            coded = jnp.where(valid, part / scale, 0.0).astype(BF16)
            out_ref[0, :, start + at : start + at + GROUP] = coded
            scales = jnp.where(lane_p == (start + at) // GROUP, scale, scales)
    scales = jnp.where(valid, scales, 0.0).T
    scale_ref[0] = scales[: width // GROUP].astype(BF16)


def normalise(frames):
    xf = frames.astype(F32)
    mean = jnp.mean(xf, axis=-1, keepdims=True)
    centred = xf - mean
    var = jnp.mean(centred * centred, axis=-1, keepdims=True)
    return (centred * lax.rsqrt(var + 1e-06)).astype(BF16)


def params(mebibytes):
    return pltpu.CompilerParams(vmem_limit_bytes=mebibytes * 1024 * 1024)


def local(frames_in, qkv_weight, out_weight, owners, slots):
    fr_count, patch_count, width = frames_in.shape
    rows_here = qkv_weight.shape[0]
    core = lax.axis_index("c")
    position = lax.axis_index("pool")
    chips = lax.axis_size("zh") * lax.axis_size("zl") * lax.axis_size("x")
    sources = 2 * lax.axis_size("pool")
    swap = [(0, 1), (1, 0)]

    share = lax.dynamic_slice_in_dim(frames_in, (position % 2) * 2, 2, 0)
    share = share.reshape(2, chips, 8, width)
    share = jnp.concatenate(
        [lax.dynamic_slice_in_dim(share, position // 2 + at, 1, 2) for at in (0, 4)], axis=2
    )
    share = normalise(share).transpose(1, 2, 0, 3).reshape(2 * chips, 2, width)
    share = lax.all_to_all(share, FRAME, 0, 0, tiled=True).reshape(4 * chips, width)
    tracks = lax.all_gather(share, "pool", axis=0, tiled=False)
    owners_other = lax.ppermute(owners, "c", swap)

    parts = qkv_weight.reshape(rows_here, 3, 2, HEAD_DIM)
    query, key, value = parts[:, 0], parts[:, 1], parts[:, 2]
    back = out_weight.T.reshape(rows_here, 2, HEAD_DIM)
    payload = jnp.concatenate(
        [
            query,
            back[..., :40],
            key,
            back[..., 40:80],
            value,
            back[..., 80:],
            jnp.zeros((rows_here, 2, 32), BF16),
        ],
        axis=-1,
    )
    both = lax.all_gather(payload, "c", axis=0, tiled=True)
    mine = lax.dynamic_index_in_dim(both, core, 1, keepdims=False)
    mine = spread(mine, "zh").reshape(-1, mine.shape[-1])
    mine = spread(mine, ("zl", "x"))
    mine, back_rows = pl.pallas_call(
        order_kernel,
        out_shape=[
            jax.ShapeDtypeStruct((width, 384), BF16),
            jax.ShapeDtypeStruct((96, width), BF16),
        ],
        scratch_shapes=[pltpu.VMEM((width, 384), F32)],
        compiler_params=params(ORDER),
        name="order",
    )(mine)
    mine_other = lax.ppermute(mine, "c", swap)
    out_rows = lax.all_gather(back_rows, ("c", "pool"), axis=0, tiled=False)

    attended = pl.pallas_call(
        track_kernel,
        grid=(4,),
        in_specs=[
            pl.BlockSpec(memory_space=pltpu.SMEM),
            pl.BlockSpec((2, 4 * chips, width), lambda p: (p, 0, 0)),
            pl.BlockSpec(mine.shape, lambda p: (0, 0)),
            pl.BlockSpec(mine.shape, lambda p: (0, 0)),
        ],
        out_specs=pl.BlockSpec((chips // 2, 2, 6, 8, 128), lambda p: (0, 0, 0, 0, 0)),
        out_shape=jax.ShapeDtypeStruct((chips // 2, 2, 6, 8, 128), BF16),
        scratch_shapes=[pltpu.VMEM((chips, 64, 128), F32)],
        compiler_params=params(TRACK),
        name="track",
    )(core.reshape(1), tracks, mine, mine_other)
    attended = attended.reshape(chips, 6, 8, 128)
    returned = lax.all_to_all(attended, CHIP, 0, 0, tiled=True)

    pair = jnp.where(
        core == 0,
        jnp.concatenate([owners, owners_other]),
        jnp.concatenate([owners_other, owners]),
    )
    packed = pl.pallas_call(
        pack_kernel,
        in_specs=[
            pl.BlockSpec(memory_space=pltpu.SMEM),
            pl.BlockSpec(memory_space=pltpu.VMEM),
        ],
        out_specs=pl.BlockSpec(memory_space=pltpu.VMEM),
        out_shape=jax.ShapeDtypeStruct((sources, 3 * chips // 4, 8, 128), BF16),
        compiler_params=params(PACK),
        name="pack",
    )(pair, returned.reshape(chips // 2, 2, 6, 8, 128))
    gathered = lax.all_to_all(packed, ("c", "pool"), 0, 0, tiled=True)

    match = (owners == position) & (slots == 0)
    chosen = jnp.sum(jnp.where(match, jnp.arange(fr_count, dtype=jnp.int32), 0))
    pick = jnp.stack([chosen, jnp.any(match).astype(jnp.int32)])
    groups = width // GROUP
    return pl.pallas_call(
        deliver_kernel,
        grid_spec=pltpu.PrefetchScalarGridSpec(
            num_scalar_prefetch=1,
            grid=(1,),
            in_specs=[
                pl.BlockSpec((1, patch_count, width), lambda g, pick: (pick[0], 0, 0)),
                pl.BlockSpec(gathered.shape, lambda g, pick: (0, 0, 0, 0)),
                pl.BlockSpec(out_rows.shape, lambda g, pick: (0, 0, 0)),
            ],
            out_specs=[
                pl.BlockSpec((1, patch_count, width), lambda g, pick: (0, 0, 0)),
                pl.BlockSpec((1, groups, patch_count), lambda g, pick: (0, 0, 0)),
            ],
        ),
        out_shape=[
            jax.ShapeDtypeStruct((1, patch_count, width), BF16),
            jax.ShapeDtypeStruct((1, groups, patch_count), BF16),
        ],
        compiler_params=params(DELIVER),
        name="deliver",
    )(pick, frames_in, gathered, out_rows)


def solution(mesh):
    fine = Mesh(mesh.devices.reshape(4, 2, 4, 2, 8), ("zh", "zl", "x", "c", "pool"))
    run = jax.shard_map(
        local,
        mesh=fine,
        in_specs=(
            P(FRAME, None, None),
            P(FRAME, None, "pool"),
            P("pool", FRAME),
            P(FRAME),
            P(FRAME),
        ),
        out_specs=(P(FRAME + ("pool",), None, None), P(FRAME + ("pool",), None, None)),
        check_vma=False,
    )

    def whole(*args):
        shipped, scales = run(*args)
        return shipped, scales

    return whole
```

```python
import jax
import jax.numpy as jnp
from jax import lax
from jax.experimental import pallas as pl
from jax.experimental.pallas import tpu as pltpu
from jax.sharding import Mesh, PartitionSpec as P

HEAD_DIM = 88
GROUP = 128
MAIN = 64
SLOT = 32
ORDER, TRACK, PACK, DELIVER = 30, 57, 40, 30
FACTOR = 1.0 / HEAD_DIM**0.5
CHIP = ("zh", "zl", "x")
FRAME = CHIP + ("c",)
F32 = jnp.float32
BF16 = jnp.bfloat16


def lanes_of(shape):
    return lax.broadcasted_iota(jnp.int32, shape, len(shape) - 1)


def turn(value, shift):
    shift = shift % 128
    if shift == 0:
        return value
    return pltpu.roll(value, shift, len(value.shape) - 1)


def spread(value, axis):
    count = lax.axis_size(axis)
    copies = jnp.broadcast_to(value[None], (count,) + value.shape)
    return lax.all_to_all(copies, axis, 0, 0, tiled=True)


def order_kernel(source_ref, right_ref, back_ref, order_ref):
    inner, height = source_ref.shape[:2]
    outer = 4
    rows = height // outer
    for low in range(inner):
        block = source_ref[low].astype(F32)
        for high in range(outer):
            start = (high * inner + low) * rows
            order_ref[start : start + rows, :] = block[high * rows : (high + 1) * rows]
    right_ref[...] = order_ref[...].astype(BF16)
    turned = [order_ref[:, at : at + 128].T[HEAD_DIM:] for at in (0, 128, 256)]
    back_ref[...] = jnp.concatenate(turned, axis=0)[:96].astype(BF16)


def track_kernel(core_ref, tokens_ref, own_ref, other_ref, out_ref, o_ref):
    step = pl.program_id(0)
    core = core_ref[0]
    frames = 2 * tokens_ref.shape[1]
    lane = lanes_of((frames, 128))
    tokens = tokens_ref[...].reshape(frames, tokens_ref.shape[2])
    right = jnp.concatenate([own_ref[...], other_ref[...]], axis=1)
    both = jnp.dot(tokens, right, preferred_element_type=F32)
    for which in range(2):
        head = core if which == 0 else 1 - core
        out = both[:, which * 384 : which * 384 + 384]
        query = jnp.where(lane < HEAD_DIM, out[:, :128], 0.0).astype(BF16)
        key = out[:, 128:256].astype(BF16)
        value = jnp.where(lane < HEAD_DIM, out[:, 256:], 0.0).astype(BF16)
        scores = lax.dot_general(query, key, (((1,), (1,)), ((), ())), preferred_element_type=F32)
        top = jnp.max(scores, axis=-1, keepdims=True)
        expo = jnp.exp((scores - top) * FACTOR)
        total = jnp.sum(expo, axis=-1, keepdims=True)
        mixed = jnp.dot(expo.astype(BF16), value, preferred_element_type=F32)
        mixed = (mixed * (1.0 / total)).reshape(frames // 8, 8, 128)
        o_ref[:, pl.ds(head * 4 + step, 8, stride=8), :] = mixed

    @pl.when(step == pl.num_programs(0) - 1)
    def _():
        pairs = frames // 16
        lane_o = lanes_of((pairs, 8, 128))

        def piece_of(side, owner, late, odd):
            start = (side * 4 + owner * 2 + odd) * 8
            return o_ref[late * pairs : (late + 1) * pairs, start : start + 8, :]

        for side in range(2):
            for owner in range(2):
                rest = None
                for late in range(2):
                    even, odd = (piece_of(side, owner, late, at) for at in range(2))
                    main = jnp.where(lane_o < MAIN, even, turn(odd, MAIN))
                    out_ref[:, side, owner, late] = main.astype(BF16)
                    for at, piece in enumerate((even, odd)):
                        part = late * 2 + at
                        piece = turn(piece, SLOT * part - MAIN)
                        rest = piece if part == 0 else jnp.where(lane_o >= SLOT * part, piece, rest)
                out_ref[:, side, owner, 2] = rest.astype(BF16)


def half_turn(value):
    return pltpu.roll(value, 4, 1)


def pack_kernel(owner_ref, x_ref, out_ref):
    pairs = x_ref.shape[0]
    out_ref[...] = jnp.zeros_like(out_ref)

    def join(even, odd, lane, edges):
        shape = even[0].shape
        upper = lax.broadcasted_iota(jnp.int32, shape, 1) < 4
        first = jnp.where(upper, even[0], half_turn(odd[0]))
        second = jnp.where(upper, half_turn(even[1]), odd[1])
        return jnp.where(lane < edges, first, second)

    lane = lanes_of((pairs, 8, 128))
    lane_h = lanes_of((pairs // 2, 8, 128))
    for fr in range(4):
        place = owner_ref[fr]
        for core in range(2):
            tiles = [x_ref[:, side, core, fr // 2].astype(F32) for side in range(2)]
            even, odd = (
                [turn(tile, MAIN * head - MAIN * (fr % 2)) for head in range(2)] for tile in tiles
            )
            out_ref[place, core, :pairs] = join(even, odd, lane, MAIN).astype(BF16)
            tiles = [x_ref[:, side, core, 2].astype(F32) for side in range(2)]
            rests = []
            for half in range(2):
                rows = slice(half * (pairs // 2), (half + 1) * (pairs // 2))
                even, odd = (
                    [
                        turn(tile[rows], 2 * SLOT * half + SLOT * head - SLOT * fr)
                        for head in range(2)
                    ]
                    for tile in tiles
                )
                rests.append(join(even, odd, lane_h, 2 * SLOT * half + SLOT))
            rest = jnp.where(lane_h < 2 * SLOT, rests[0], rests[1])
            out_ref[place, core, pairs:] = rest.astype(BF16)


def deliver_kernel(pick_ref, frame_ref, y_ref, weight_ref, out_ref, scale_ref):
    heads = y_ref.shape[0]
    patches, width = frame_ref.shape[1:]
    half = patches // 2
    tiles = half // 8
    valid = pick_ref[1] > 0
    lane = lanes_of((half, 128))

    def weave(first, second):
        upper = lax.broadcasted_iota(jnp.int32, first.shape, 1) < 4
        even = jnp.where(upper, first, half_turn(second))
        odd = jnp.where(upper, half_turn(first), second)
        return jnp.stack([even, odd], axis=1).reshape(first.shape[0] * 16, 128)

    mains, rests = [], []
    for at in range(heads):
        pair = [y_ref[at, core, :tiles].astype(F32) for core in range(2)]
        mains.append(weave(*pair).astype(BF16))
    for at in range(0, heads, 2):
        first, second = (
            weave(*(y_ref[one, core, tiles:].astype(F32) for core in range(2)))
            for one in (at, at + 1)
        )
        low = jnp.where(lane < MAIN, first, turn(second, MAIN))
        high = jnp.where(lane < MAIN, turn(first, MAIN), second)
        rests.append(jnp.concatenate([low, high], axis=0).astype(BF16))
    left = jnp.concatenate(mains, axis=1)
    left_rest = jnp.concatenate(rests, axis=1)
    lane_p = lanes_of((patches, 128))
    scales = jnp.zeros((patches, 128), F32)
    for start in range(0, width, 256):
        stop = min(start + 256, width)
        right, right_rest = (
            jnp.concatenate(
                [weight_ref[at : at + heads, rows, start:stop] for at in (0, heads)], axis=1
            )
            for rows in (slice(0, MAIN), slice(MAIN, MAIN + SLOT))
        )
        right = right.reshape(heads * 2 * MAIN, stop - start)
        right_rest = right_rest.reshape(heads * 2 * SLOT, stop - start)
        total = jnp.dot(left, right, preferred_element_type=F32)
        total += jnp.dot(left_rest, right_rest, preferred_element_type=F32)
        total += frame_ref[0, :, start:stop].astype(F32)
        for at in range(0, stop - start, GROUP):
            part = total[:, at : at + GROUP]
            top = jnp.max(jnp.abs(part), axis=-1, keepdims=True)
            scale = (top + 1e-06).astype(BF16).astype(F32)
            coded = jnp.where(valid, part / scale, 0.0).astype(BF16)
            out_ref[0, :, start + at : start + at + GROUP] = coded
            scales = jnp.where(lane_p == (start + at) // GROUP, scale, scales)
    scales = jnp.where(valid, scales, 0.0).T
    scale_ref[0] = scales[: width // GROUP].astype(BF16)


def normalise(frames):
    xf = frames.astype(F32)
    mean = jnp.mean(xf, axis=-1, keepdims=True)
    centred = xf - mean
    var = jnp.mean(centred * centred, axis=-1, keepdims=True)
    return (centred * lax.rsqrt(var + 1e-06)).astype(BF16)


def params(mebibytes):
    return pltpu.CompilerParams(vmem_limit_bytes=mebibytes * 1024 * 1024)


def local(frames_in, qkv_weight, out_weight, owners, slots):
    fr_count, patch_count, width = frames_in.shape
    rows_here = qkv_weight.shape[0]
    core = lax.axis_index("c")
    position = lax.axis_index("pool")
    chips = lax.axis_size("zh") * lax.axis_size("zl") * lax.axis_size("x")
    pool = lax.axis_size("pool")
    swap = [(0, 1), (1, 0)]

    grid = frames_in.reshape(2, 2, chips, 8, width)
    share = jnp.concatenate(
        [
            lax.dynamic_slice(
                grid, (position % 2, 0, 0, position // 2 + at, 0), (1, 2, chips, 1, width)
            )[0]
            for at in (0, 4)
        ],
        axis=2,
    )
    share = normalise(share).transpose(1, 2, 0, 3).reshape(2 * chips, 2, width)
    share = lax.all_to_all(share, FRAME, 0, 0, tiled=True).reshape(4 * chips, width)
    tracks = lax.all_gather(share, "pool", axis=0, tiled=False)

    parts = qkv_weight.reshape(rows_here, 3, 2, HEAD_DIM)
    query, key, value = parts[:, 0], parts[:, 1], parts[:, 2]
    back = out_weight.T.reshape(rows_here, 2, HEAD_DIM)
    payload = jnp.concatenate(
        [
            query,
            back[..., :40],
            key,
            back[..., 40:80],
            value,
            back[..., 80:],
            jnp.zeros((rows_here, 2, 32), BF16),
        ],
        axis=-1,
    )
    both = lax.all_gather(payload, "c", axis=0, tiled=True)
    mine = lax.dynamic_index_in_dim(both, core, 1, keepdims=False)
    mine = spread(mine, "zh").reshape(-1, mine.shape[-1])
    mine = spread(mine, ("zl", "x"))
    mine, back_rows = pl.pallas_call(
        order_kernel,
        out_shape=[
            jax.ShapeDtypeStruct((width, 384), BF16),
            jax.ShapeDtypeStruct((96, width), BF16),
        ],
        scratch_shapes=[pltpu.VMEM((width, 384), F32)],
        compiler_params=params(ORDER),
        name="order",
    )(mine)
    mine_other = lax.ppermute(mine, "c", swap)
    out_rows = lax.all_gather(back_rows, ("c", "pool"), axis=0, tiled=False)

    attended = pl.pallas_call(
        track_kernel,
        grid=(4,),
        in_specs=[
            pl.BlockSpec(memory_space=pltpu.SMEM),
            pl.BlockSpec((2, 4 * chips, width), lambda p: (p, 0, 0)),
            pl.BlockSpec(mine.shape, lambda p: (0, 0)),
            pl.BlockSpec(mine.shape, lambda p: (0, 0)),
        ],
        out_specs=pl.BlockSpec((chips // 2, 2, 2, 3, 8, 128), lambda p: (0, 0, 0, 0, 0, 0)),
        out_shape=jax.ShapeDtypeStruct((chips // 2, 2, 2, 3, 8, 128), BF16),
        scratch_shapes=[pltpu.VMEM((chips, 64, 128), F32)],
        compiler_params=params(TRACK),
        name="track",
    )(core.reshape(1), tracks, mine, mine_other)
    attended = attended.reshape(2 * chips, 3, 8, 128)
    returned = lax.all_to_all(attended, FRAME, 0, 0, tiled=True)

    packed = pl.pallas_call(
        pack_kernel,
        in_specs=[
            pl.BlockSpec(memory_space=pltpu.SMEM),
            pl.BlockSpec(memory_space=pltpu.VMEM),
        ],
        out_specs=pl.BlockSpec(memory_space=pltpu.VMEM),
        out_shape=jax.ShapeDtypeStruct((pool, 2, 3 * chips // 4, 8, 128), BF16),
        compiler_params=params(PACK),
        name="pack",
    )(owners, returned.reshape(chips // 2, 2, 2, 3, 8, 128))
    gathered = lax.all_to_all(packed, "pool", 0, 0, tiled=True)

    match = (owners == position) & (slots == 0)
    chosen = jnp.sum(jnp.where(match, jnp.arange(fr_count, dtype=jnp.int32), 0))
    pick = jnp.stack([chosen, jnp.any(match).astype(jnp.int32)])
    groups = width // GROUP
    return pl.pallas_call(
        deliver_kernel,
        grid_spec=pltpu.PrefetchScalarGridSpec(
            num_scalar_prefetch=1,
            grid=(1,),
            in_specs=[
                pl.BlockSpec((1, patch_count, width), lambda g, pick: (pick[0], 0, 0)),
                pl.BlockSpec(gathered.shape, lambda g, pick: (0, 0, 0, 0, 0)),
                pl.BlockSpec(out_rows.shape, lambda g, pick: (0, 0, 0)),
            ],
            out_specs=[
                pl.BlockSpec((1, patch_count, width), lambda g, pick: (0, 0, 0)),
                pl.BlockSpec((1, groups, patch_count), lambda g, pick: (0, 0, 0)),
            ],
        ),
        out_shape=[
            jax.ShapeDtypeStruct((1, patch_count, width), BF16),
            jax.ShapeDtypeStruct((1, groups, patch_count), BF16),
        ],
        compiler_params=params(DELIVER),
        name="deliver",
    )(pick, frames_in, gathered, out_rows)


def solution(mesh):
    fine = Mesh(mesh.devices.reshape(4, 2, 4, 2, 8), ("zh", "zl", "x", "c", "pool"))
    run = jax.shard_map(
        local,
        mesh=fine,
        in_specs=(
            P(FRAME, None, None),
            P(FRAME, None, "pool"),
            P("pool", FRAME),
            P(FRAME),
            P(FRAME),
        ),
        out_specs=(P(FRAME + ("pool",), None, None), P(FRAME + ("pool",), None, None)),
        check_vma=False,
    )

    def whole(*args):
        shipped, scales = run(*args)
        return shipped, scales

    return whole
```

```python
import functools

import jax
import jax.numpy as jnp
from jax import lax
from jax.experimental import pallas as pl
from jax.experimental.pallas import tpu as pltpu
from jax.sharding import Mesh, PartitionSpec as P

HEAD_DIM = 88
GROUP = 128
MAIN = 64
SLOT = 32
NORMALISE, ORDER, PROJECT = 57, 30, 57
ATTEND, PACK, DELIVER = 40, 40, 30
FACTOR = 1.0 / HEAD_DIM**0.5
CHIP = ("zh", "zl", "x")
FRAME = CHIP + ("c",)
F32 = jnp.float32
BF16 = jnp.bfloat16


def lanes_of(shape):
    return lax.broadcasted_iota(jnp.int32, shape, len(shape) - 1)


def turn(value, shift):
    shift = shift % 128
    if shift == 0:
        return value
    return pltpu.roll(value, shift, len(value.shape) - 1)


def spread(value, axis):
    count = lax.axis_size(axis)
    copies = jnp.broadcast_to(value[None], (count,) + value.shape)
    return lax.all_to_all(copies, axis, 0, 0, tiled=True)


def normalise_kernel(own_ref, other_ref, own_out, other_out, mark_ref):
    for source, target in ((own_ref, own_out), (other_ref, other_out)):
        rows = source[0].astype(F32)
        mean = jnp.mean(rows, axis=-1, keepdims=True)
        centred = rows - mean
        var = jnp.mean(centred * centred, axis=-1, keepdims=True)
        target[0] = (centred * lax.rsqrt(var + 1e-06)).astype(BF16)
    mark_ref[...] = jnp.zeros_like(mark_ref)


def order_kernel(source_ref, mark_ref, right_ref, back_ref, order_ref):
    inner, height = source_ref.shape[:2]
    outer = 4
    rows = height // outer
    for low in range(inner):
        block = source_ref[low].astype(F32)
        for high in range(outer):
            start = (high * inner + low) * rows
            order_ref[start : start + rows, :] = block[high * rows : (high + 1) * rows]
    right_ref[...] = order_ref[...].astype(BF16)
    back_ref[...] = order_ref[:, 256:384].T[32:].astype(BF16)


def project_kernel(core_ref, own_ref, other_ref, weight_ref, out_ref, rest_ref):
    step = pl.program_id(0)
    core = core_ref[0]
    chips = out_ref.shape[0]

    @pl.when(step == 0)
    def _():
        rest_ref[...] = jnp.zeros_like(rest_ref)

    lane = lanes_of(rest_ref.shape)
    for which, ref in enumerate((own_ref, other_ref)):
        frame = (core if which == 0 else 1 - core) * 4 + step
        out = jnp.dot(ref[0], weight_ref[...], preferred_element_type=F32)
        for tile in range(2):
            block = out[:, tile * 128 : (tile + 1) * 128].astype(BF16)
            out_ref[:, 2 * frame + tile] = block.reshape(chips, 8, 128)
        rest = jnp.where(lane < 8, out[:, 256:384], 0.0)
        rest_ref[...] += pltpu.roll(rest, 8 * frame, 1)

    @pl.when(step == pl.num_programs(0) - 1)
    def _():
        out_ref[:, 16] = rest_ref[...].astype(BF16).reshape(chips, 8, 128)


def attend_kernel(x_ref, out_ref, q_ref, k_ref, v_ref, o_ref):
    chips = x_ref.shape[0]
    frames = chips * 8
    shape = (chips, 8, 128)
    lane = lanes_of(shape)
    rest = x_ref[:, 16].astype(F32)
    for fr in range(8):
        first = x_ref[:, 2 * fr].astype(F32)
        second = x_ref[:, 2 * fr + 1].astype(F32)
        rows = slice(fr * 8, fr * 8 + 8)
        q_ref[:, rows, :] = jnp.where(lane < HEAD_DIM, first, 0.0)
        k_ref[:, rows, :] = second
        v_ref[:, rows, :] = jnp.where(
            lane < 40,
            turn(first, 40),
            jnp.where(
                lane < 80,
                turn(second, 80),
                jnp.where(lane < HEAD_DIM, turn(rest, 80 - 8 * fr), 0.0),
            ),
        )
    for patch in range(8):
        pick = pl.ds(patch, 8, stride=8)
        query = q_ref[:, pick, :].reshape(frames, 128).astype(BF16)
        key = k_ref[:, pick, :].reshape(frames, 128).astype(BF16)
        value = v_ref[:, pick, :].reshape(frames, 128).astype(BF16)
        scores = lax.dot_general(query, key, (((1,), (1,)), ((), ())), preferred_element_type=F32)
        top = jnp.max(scores, axis=-1, keepdims=True)
        expo = jnp.exp((scores - top) * FACTOR)
        total = jnp.sum(expo, axis=-1, keepdims=True)
        mixed = jnp.dot(expo.astype(BF16), value, preferred_element_type=F32)
        o_ref[:, pick, :] = (mixed * (1.0 / total)).reshape(shape)
    for tile in range(4):
        even = o_ref[:, tile * 16 : tile * 16 + 8, :]
        odd = o_ref[:, tile * 16 + 8 : tile * 16 + 16, :]
        out_ref[:, tile] = jnp.where(lane < MAIN, even, turn(odd, MAIN)).astype(BF16)
    for tile in range(2):
        packed = None
        for part in range(4):
            fr = tile * 4 + part
            piece = turn(o_ref[:, fr * 8 : fr * 8 + 8, :], SLOT * part - MAIN)
            packed = piece if part == 0 else jnp.where(lane >= SLOT * part, piece, packed)
        out_ref[:, 4 + tile] = packed.astype(BF16)


def pack_kernel(owner_ref, x_ref, out_ref):
    chips = x_ref.shape[0]
    half, quarter = chips // 2, chips // 4
    out_ref[...] = jnp.zeros_like(out_ref)
    lane = lanes_of((half, 8, 128))
    lane_q = lanes_of((quarter, 8, 128))
    for fr in range(8):
        place = (fr // 4) * 8 + owner_ref[fr]
        tile = x_ref[:, fr // 2].astype(F32)
        low, high = tile[:half], tile[half:]
        side = fr % 2
        main = jnp.where(lane < MAIN, turn(low, MAIN * side), turn(high, MAIN * (1 - side)))
        out_ref[place, :half] = main.astype(BF16)
        tile = x_ref[:, 4 + fr // 4].astype(F32)
        packed = None
        for part in range(4):
            piece = turn(tile[part * quarter : (part + 1) * quarter], SLOT * (part - fr % 4))
            packed = piece if part == 0 else jnp.where(lane_q >= SLOT * part, piece, packed)
        out_ref[place, half:] = packed.astype(BF16)


def deliver_kernel(pick_ref, frame_ref, y_ref, weight_ref, out_ref, scale_ref):
    sources = y_ref.shape[0]
    patches, width = frame_ref.shape[1:]
    half, quarter = patches // 2, patches // 4
    tiles = half // 8
    valid = pick_ref[1] > 0
    lane = lanes_of((half, 128))
    lane_q = lanes_of((quarter, 128))
    mains, rests = [], []
    for pair in range(sources // 2):
        first = y_ref[2 * pair, :tiles].reshape(half, 128).astype(F32)
        second = y_ref[2 * pair + 1, :tiles].reshape(half, 128).astype(F32)
        low = jnp.where(lane < MAIN, first, turn(second, MAIN))
        high = jnp.where(lane < MAIN, turn(first, MAIN), second)
        mains.append(jnp.concatenate([low, high], axis=0).astype(BF16))
    for group in range(sources // 4):
        pieces = [
            y_ref[4 * group + part, tiles:].reshape(quarter, 128).astype(F32) for part in range(4)
        ]
        rows = []
        for block in range(4):
            packed = None
            for part in range(4):
                piece = turn(pieces[part], SLOT * (part - block))
                packed = piece if part == 0 else jnp.where(lane_q >= SLOT * part, piece, packed)
            rows.append(packed)
        rests.append(jnp.concatenate(rows, axis=0).astype(BF16))
    left = jnp.concatenate(mains, axis=1)
    left_rest = jnp.concatenate(rests, axis=1)
    lane_p = lanes_of((patches, 128))
    scales = jnp.zeros((patches, 128), F32)
    for start in range(0, width, 256):
        stop = min(start + 256, width)
        right = weight_ref[:, :MAIN, start:stop].reshape(sources * MAIN, stop - start)
        right_rest = weight_ref[:, MAIN:, start:stop].reshape(sources * SLOT, stop - start)
        total = jnp.dot(left, right, preferred_element_type=F32)
        total += jnp.dot(left_rest, right_rest, preferred_element_type=F32)
        total += frame_ref[0, :, start:stop].astype(F32)
        for at in range(0, stop - start, GROUP):
            part = total[:, at : at + GROUP]
            top = jnp.max(jnp.abs(part), axis=-1, keepdims=True)
            scale = (top + 1e-06).astype(BF16).astype(F32)
            coded = jnp.where(valid, part / scale, 0.0).astype(BF16)
            out_ref[0, :, start + at : start + at + GROUP] = coded
            scales = jnp.where(lane_p == (start + at) // GROUP, scale, scales)
    scales = jnp.where(valid, scales, 0.0).T
    scale_ref[0] = scales[: width // GROUP].astype(BF16)


def params(mebibytes):
    return pltpu.CompilerParams(vmem_limit_bytes=mebibytes * 1024 * 1024)


def local(frames_in, qkv_weight, out_weight, owners, slots):
    fr_count, patch_count, width = frames_in.shape
    rows_here = qkv_weight.shape[0]
    core = lax.axis_index("c")
    position = lax.axis_index("pool")
    chips = lax.axis_size("zh") * lax.axis_size("zl") * lax.axis_size("x")
    sources = 2 * lax.axis_size("pool")
    swap = [(0, 1), (1, 0)]

    frames_other = lax.ppermute(frames_in, "c", swap)
    frame_spec = pl.BlockSpec((1, patch_count, width), lambda j: (j, 0, 0))
    normed, normed_other, mark = pl.pallas_call(
        normalise_kernel,
        grid=(fr_count,),
        in_specs=[frame_spec, frame_spec],
        out_specs=[frame_spec, frame_spec, pl.BlockSpec((8, 128), lambda j: (0, 0))],
        out_shape=[
            jax.ShapeDtypeStruct(frames_in.shape, BF16),
            jax.ShapeDtypeStruct(frames_in.shape, BF16),
            jax.ShapeDtypeStruct((8, 128), F32),
        ],
        compiler_params=params(NORMALISE),
        name="normalise",
    )(frames_in, frames_other)
    owners_other = lax.ppermute(owners, "c", swap)

    parts = qkv_weight.reshape(rows_here, 3, 2, HEAD_DIM)
    query, key, value = parts[:, 0], parts[:, 1], parts[:, 2]
    back = out_weight.T.reshape(rows_here, 2, HEAD_DIM)
    blank = functools.partial(jnp.zeros, dtype=BF16)
    payload = jnp.concatenate(
        [
            query,
            value[..., :40],
            key,
            value[..., 40:80],
            value[..., 80:],
            blank((rows_here, 2, 24)),
            back,
            blank((rows_here, 2, 8)),
        ],
        axis=-1,
    )
    both = lax.all_gather(payload, "c", axis=0, tiled=True)
    mine = lax.dynamic_index_in_dim(both, core, 1, keepdims=False)
    mine = spread(mine, "zh").reshape(-1, mine.shape[-1])
    mine = spread(mine, ("zl", "x"))
    mine, back = pl.pallas_call(
        order_kernel,
        out_shape=[
            jax.ShapeDtypeStruct((width, 384), BF16),
            jax.ShapeDtypeStruct((96, width), BF16),
        ],
        scratch_shapes=[pltpu.VMEM((width, 384), F32)],
        compiler_params=params(ORDER),
        name="order",
    )(mine, mark)
    projected = pl.pallas_call(
        project_kernel,
        grid=(fr_count,),
        in_specs=[
            pl.BlockSpec(memory_space=pltpu.SMEM),
            frame_spec,
            frame_spec,
            pl.BlockSpec(mine.shape, lambda j: (0, 0)),
        ],
        out_specs=pl.BlockSpec((chips, 17, 8, 128), lambda j: (0, 0, 0, 0)),
        out_shape=jax.ShapeDtypeStruct((chips, 17, 8, 128), BF16),
        scratch_shapes=[pltpu.VMEM((patch_count, 128), F32)],
        compiler_params=params(PROJECT),
        name="project",
    )(core.reshape(1), normed, normed_other, mine)
    tracks = lax.all_to_all(projected, CHIP, 0, 0, tiled=True)

    out_rows = lax.all_gather(back, ("c", "pool"), axis=0, tiled=False)

    attended = pl.pallas_call(
        attend_kernel,
        out_shape=jax.ShapeDtypeStruct((chips, 6, 8, 128), BF16),
        scratch_shapes=[pltpu.VMEM((chips, 64, 128), F32)] * 4,
        compiler_params=params(ATTEND),
        name="attend",
    )(tracks)
    returned = lax.all_to_all(attended, CHIP, 0, 0, tiled=True)

    pair = jnp.where(
        core == 0,
        jnp.concatenate([owners, owners_other]),
        jnp.concatenate([owners_other, owners]),
    )
    packed = pl.pallas_call(
        pack_kernel,
        in_specs=[
            pl.BlockSpec(memory_space=pltpu.SMEM),
            pl.BlockSpec(memory_space=pltpu.VMEM),
        ],
        out_specs=pl.BlockSpec(memory_space=pltpu.VMEM),
        out_shape=jax.ShapeDtypeStruct((sources, 3 * chips // 4, 8, 128), BF16),
        compiler_params=params(PACK),
        name="pack",
    )(pair, returned)
    gathered = lax.all_to_all(packed, ("c", "pool"), 0, 0, tiled=True)

    match = (owners == position) & (slots == 0)
    chosen = jnp.sum(jnp.where(match, jnp.arange(fr_count, dtype=jnp.int32), 0))
    pick = jnp.stack([chosen, jnp.any(match).astype(jnp.int32)])
    groups = width // GROUP
    return pl.pallas_call(
        deliver_kernel,
        grid_spec=pltpu.PrefetchScalarGridSpec(
            num_scalar_prefetch=1,
            grid=(1,),
            in_specs=[
                pl.BlockSpec((1, patch_count, width), lambda g, pick: (pick[0], 0, 0)),
                pl.BlockSpec(gathered.shape, lambda g, pick: (0, 0, 0, 0)),
                pl.BlockSpec(out_rows.shape, lambda g, pick: (0, 0, 0)),
            ],
            out_specs=[
                pl.BlockSpec((1, patch_count, width), lambda g, pick: (0, 0, 0)),
                pl.BlockSpec((1, groups, patch_count), lambda g, pick: (0, 0, 0)),
            ],
        ),
        out_shape=[
            jax.ShapeDtypeStruct((1, patch_count, width), BF16),
            jax.ShapeDtypeStruct((1, groups, patch_count), BF16),
        ],
        compiler_params=params(DELIVER),
        name="deliver",
    )(pick, frames_in, gathered, out_rows)


def solution(mesh):
    fine = Mesh(mesh.devices.reshape(4, 2, 4, 2, 8), ("zh", "zl", "x", "c", "pool"))
    run = jax.shard_map(
        local,
        mesh=fine,
        in_specs=(
            P(FRAME, None, None),
            P(FRAME, None, "pool"),
            P("pool", FRAME),
            P(FRAME),
            P(FRAME),
        ),
        out_specs=(P(FRAME + ("pool",), None, None), P(FRAME + ("pool",), None, None)),
        check_vma=False,
    )

    def whole(*args):
        shipped, scales = run(*args)
        return shipped, scales

    return whole
```

```python
import jax
import jax.numpy as jnp
from jax import lax
from jax.experimental import pallas as pl
from jax.experimental.pallas import tpu as pltpu
from jax.sharding import Mesh, PartitionSpec as P

HEAD_DIM = 88
GROUP = 128
MAIN = 64
SLOT = 32
ORDER, TRACK, PACK, DELIVER = 30, 57, 40, 30
FACTOR = 1.4426950408889634 / HEAD_DIM**0.5
CHIP = ("zh", "zl", "x")
FRAME = CHIP + ("c",)
F32 = jnp.float32
BF16 = jnp.bfloat16


def lanes_of(shape):
    return lax.broadcasted_iota(jnp.int32, shape, len(shape) - 1)


def turn(value, shift):
    shift = shift % 128
    if shift == 0:
        return value
    return pltpu.roll(value, shift, len(value.shape) - 1)


def spread(value, axis):
    count = lax.axis_size(axis)
    copies = jnp.broadcast_to(value[None], (count,) + value.shape)
    return lax.all_to_all(copies, axis, 0, 0, tiled=True)


def order_kernel(source_ref, right_ref, back_ref, order_ref):
    inner, height = source_ref.shape[:2]
    outer = 4
    rows = height // outer
    for low in range(inner):
        block = source_ref[low].astype(F32)
        for high in range(outer):
            start = (high * inner + low) * rows
            order_ref[start : start + rows, :] = block[high * rows : (high + 1) * rows]
    right_ref[...] = order_ref[...].astype(BF16)
    turned = [order_ref[:, at : at + 128].T[HEAD_DIM:] for at in (0, 128, 256)]
    back_ref[...] = jnp.concatenate(turned, axis=0)[:96].astype(BF16)


def track_kernel(core_ref, tokens_ref, own_ref, other_ref, out_ref, o_ref):
    step = pl.program_id(0)
    core = core_ref[0]
    frames = 2 * tokens_ref.shape[1]
    lane = lanes_of((frames, 128))
    tokens = tokens_ref[...].reshape(frames, tokens_ref.shape[2])
    right = jnp.concatenate([own_ref[...], other_ref[...]], axis=1)
    both = jnp.dot(tokens, right, preferred_element_type=F32)
    ones = jnp.where(lane == 127, 1.0, 0.0)
    for which in range(2):
        head = core if which == 0 else 1 - core
        out = both[:, which * 384 : which * 384 + 384]
        query = jnp.where(lane < HEAD_DIM, out[:, :128] * FACTOR, 0.0).astype(BF16)
        key = out[:, 128:256].astype(BF16)
        value = jnp.where(lane < HEAD_DIM, out[:, 256:], ones).astype(BF16)
        scores = lax.dot_general(query, key, (((1,), (1,)), ((), ())), preferred_element_type=F32)
        top = jnp.max(scores, axis=-1, keepdims=True)
        expo = jnp.exp2(scores - top).astype(BF16)
        mixed = jnp.dot(expo, value, preferred_element_type=F32)
        mixed = jnp.where(lane < HEAD_DIM, mixed * (1.0 / mixed[:, 127:]), 0.0)
        mixed = mixed.reshape(frames // 8, 8, 128)
        o_ref[:, pl.ds(head * 4 + step, 8, stride=8), :] = mixed

    @pl.when(step == pl.num_programs(0) - 1)
    def _():
        pairs = frames // 16
        lane_o = lanes_of((pairs, 8, 128))

        def piece_of(side, owner, late, odd):
            start = (side * 4 + owner * 2 + odd) * 8
            return o_ref[late * pairs : (late + 1) * pairs, start : start + 8, :]

        for side in range(2):
            for owner in range(2):
                rest = None
                for late in range(2):
                    even, odd = (piece_of(side, owner, late, at) for at in range(2))
                    main = jnp.where(lane_o < MAIN, even, turn(odd, MAIN))
                    out_ref[:, side, owner * 2 + late] = main.astype(BF16)
                    for at, piece in enumerate((even, odd)):
                        part = late * 2 + at
                        piece = turn(piece, SLOT * part - MAIN)
                        rest = piece if part == 0 else jnp.where(lane_o >= SLOT * part, piece, rest)
                out_ref[:, side, 4 + owner] = rest.astype(BF16)


def half_turn(value):
    return pltpu.roll(value, 4, 1)


def pack_kernel(owner_ref, x_ref, out_ref):
    pairs = x_ref.shape[0]
    out_ref[...] = jnp.zeros_like(out_ref)

    def join(even, odd, lane, edges):
        shape = even[0].shape
        upper = lax.broadcasted_iota(jnp.int32, shape, 1) < 4
        first = jnp.where(upper, even[0], half_turn(odd[0]))
        second = jnp.where(upper, half_turn(even[1]), odd[1])
        return jnp.where(lane < edges, first, second)

    lane = lanes_of((pairs, 8, 128))
    lane_h = lanes_of((pairs // 2, 8, 128))
    for fr in range(8):
        place = (fr // 4) * 8 + owner_ref[fr]
        tiles = [x_ref[:, side, fr // 2].astype(F32) for side in range(2)]
        even, odd = (
            [turn(tile, MAIN * head - MAIN * (fr % 2)) for head in range(2)] for tile in tiles
        )
        out_ref[place, :pairs] = join(even, odd, lane, MAIN).astype(BF16)
        tiles = [x_ref[:, side, 4 + fr // 4].astype(F32) for side in range(2)]
        rests = []
        for half in range(2):
            rows = slice(half * (pairs // 2), (half + 1) * (pairs // 2))
            even, odd = (
                [
                    turn(tile[rows], 2 * SLOT * half + SLOT * head - SLOT * (fr % 4))
                    for head in range(2)
                ]
                for tile in tiles
            )
            rests.append(join(even, odd, lane_h, 2 * SLOT * half + SLOT))
        rest = jnp.where(lane_h < 2 * SLOT, rests[0], rests[1])
        out_ref[place, pairs:] = rest.astype(BF16)


def deliver_kernel(pick_ref, frame_ref, y_ref, weight_ref, out_ref, scale_ref):
    sources = y_ref.shape[0]
    heads = sources // 2
    patches, width = frame_ref.shape[1:]
    half = patches // 2
    tiles = half // 8
    valid = pick_ref[1] > 0
    lane = lanes_of((half, 128))

    def weave(first, second):
        upper = lax.broadcasted_iota(jnp.int32, first.shape, 1) < 4
        even = jnp.where(upper, first, half_turn(second))
        odd = jnp.where(upper, half_turn(first), second)
        return jnp.stack([even, odd], axis=1).reshape(first.shape[0] * 16, 128)

    mains, rests = [], []
    for at in range(heads):
        pair = [y_ref[core * heads + at, :tiles].astype(F32) for core in range(2)]
        mains.append(weave(*pair).astype(BF16))
    for at in range(0, heads, 2):
        first, second = (
            weave(*(y_ref[core * heads + one, tiles:].astype(F32) for core in range(2)))
            for one in (at, at + 1)
        )
        low = jnp.where(lane < MAIN, first, turn(second, MAIN))
        high = jnp.where(lane < MAIN, turn(first, MAIN), second)
        rests.append(jnp.concatenate([low, high], axis=0).astype(BF16))
    left = jnp.concatenate(mains, axis=1)
    left_rest = jnp.concatenate(rests, axis=1)
    lane_p = lanes_of((patches, 128))
    scales = jnp.zeros((patches, 128), F32)
    for start in range(0, width, 256):
        stop = min(start + 256, width)
        right, right_rest = (
            jnp.concatenate(
                [weight_ref[at : at + heads, rows, start:stop] for at in (0, heads)], axis=1
            )
            for rows in (slice(0, MAIN), slice(MAIN, MAIN + SLOT))
        )
        right = right.reshape(heads * 2 * MAIN, stop - start)
        right_rest = right_rest.reshape(heads * 2 * SLOT, stop - start)
        total = jnp.dot(left, right, preferred_element_type=F32)
        total += jnp.dot(left_rest, right_rest, preferred_element_type=F32)
        total += frame_ref[0, :, start:stop].astype(F32)
        for at in range(0, stop - start, GROUP):
            part = total[:, at : at + GROUP]
            top = jnp.max(jnp.abs(part), axis=-1, keepdims=True)
            scale = (top + 1e-06).astype(BF16).astype(F32)
            coded = jnp.where(valid, part / scale, 0.0).astype(BF16)
            out_ref[0, :, start + at : start + at + GROUP] = coded
            scales = jnp.where(lane_p == (start + at) // GROUP, scale, scales)
    scales = jnp.where(valid, scales, 0.0).T
    scale_ref[0] = scales[: width // GROUP].astype(BF16)


def normalise(frames):
    xf = frames.astype(F32)
    mean = jnp.mean(xf, axis=-1, keepdims=True)
    centred = xf - mean
    var = jnp.mean(centred * centred, axis=-1, keepdims=True)
    return (centred * lax.rsqrt(var + 1e-06)).astype(BF16)


def params(mebibytes):
    return pltpu.CompilerParams(vmem_limit_bytes=mebibytes * 1024 * 1024)


def local(frames_in, qkv_weight, out_weight, owners, slots):
    fr_count, patch_count, width = frames_in.shape
    rows_here = qkv_weight.shape[0]
    core = lax.axis_index("c")
    position = lax.axis_index("pool")
    chips = lax.axis_size("zh") * lax.axis_size("zl") * lax.axis_size("x")
    sources = 2 * lax.axis_size("pool")
    swap = [(0, 1), (1, 0)]

    grid = frames_in.reshape(2, 2, chips, 8, width)
    share = jnp.concatenate(
        [
            lax.dynamic_slice(
                grid, (position % 2, 0, 0, position // 2 + at, 0), (1, 2, chips, 1, width)
            )[0]
            for at in (0, 4)
        ],
        axis=2,
    )
    share = normalise(share).transpose(1, 2, 0, 3).reshape(2 * chips, 2, width)
    share = lax.all_to_all(share, FRAME, 0, 0, tiled=True).reshape(4 * chips, width)
    tracks = lax.all_gather(share, "pool", axis=0, tiled=False)
    owners_other = lax.ppermute(owners, "c", swap)

    parts = qkv_weight.reshape(rows_here, 3, 2, HEAD_DIM)
    query, key, value = parts[:, 0], parts[:, 1], parts[:, 2]
    back = out_weight.T.reshape(rows_here, 2, HEAD_DIM)
    payload = jnp.concatenate(
        [
            query,
            back[..., :40],
            key,
            back[..., 40:80],
            value,
            back[..., 80:],
            jnp.zeros((rows_here, 2, 32), BF16),
        ],
        axis=-1,
    )
    both = lax.all_gather(payload, "c", axis=0, tiled=True)
    mine = lax.dynamic_index_in_dim(both, core, 1, keepdims=False)
    mine = spread(mine, "zh").reshape(-1, mine.shape[-1])
    mine = spread(mine, ("zl", "x"))
    mine, back_rows = pl.pallas_call(
        order_kernel,
        out_shape=[
            jax.ShapeDtypeStruct((width, 384), BF16),
            jax.ShapeDtypeStruct((96, width), BF16),
        ],
        scratch_shapes=[pltpu.VMEM((width, 384), F32)],
        compiler_params=params(ORDER),
        name="order",
    )(mine)
    mine_other = lax.ppermute(mine, "c", swap)
    out_rows = lax.all_gather(back_rows, ("c", "pool"), axis=0, tiled=False)

    attended = pl.pallas_call(
        track_kernel,
        grid=(4,),
        in_specs=[
            pl.BlockSpec(memory_space=pltpu.SMEM),
            pl.BlockSpec((2, 4 * chips, width), lambda p: (p, 0, 0)),
            pl.BlockSpec(mine.shape, lambda p: (0, 0)),
            pl.BlockSpec(mine.shape, lambda p: (0, 0)),
        ],
        out_specs=pl.BlockSpec((chips // 2, 2, 6, 8, 128), lambda p: (0, 0, 0, 0, 0)),
        out_shape=jax.ShapeDtypeStruct((chips // 2, 2, 6, 8, 128), BF16),
        scratch_shapes=[pltpu.VMEM((chips, 64, 128), F32)],
        compiler_params=params(TRACK),
        name="track",
    )(core.reshape(1), tracks, mine, mine_other)
    attended = attended.reshape(chips, 6, 8, 128)
    returned = lax.all_to_all(attended, CHIP, 0, 0, tiled=True)

    pair = jnp.where(
        core == 0,
        jnp.concatenate([owners, owners_other]),
        jnp.concatenate([owners_other, owners]),
    )
    packed = pl.pallas_call(
        pack_kernel,
        in_specs=[
            pl.BlockSpec(memory_space=pltpu.SMEM),
            pl.BlockSpec(memory_space=pltpu.VMEM),
        ],
        out_specs=pl.BlockSpec(memory_space=pltpu.VMEM),
        out_shape=jax.ShapeDtypeStruct((sources, 3 * chips // 4, 8, 128), BF16),
        compiler_params=params(PACK),
        name="pack",
    )(pair, returned.reshape(chips // 2, 2, 6, 8, 128))
    gathered = lax.all_to_all(packed, ("c", "pool"), 0, 0, tiled=True)

    match = (owners == position) & (slots == 0)
    chosen = jnp.sum(jnp.where(match, jnp.arange(fr_count, dtype=jnp.int32), 0))
    pick = jnp.stack([chosen, jnp.any(match).astype(jnp.int32)])
    groups = width // GROUP
    return pl.pallas_call(
        deliver_kernel,
        grid_spec=pltpu.PrefetchScalarGridSpec(
            num_scalar_prefetch=1,
            grid=(1,),
            in_specs=[
                pl.BlockSpec((1, patch_count, width), lambda g, pick: (pick[0], 0, 0)),
                pl.BlockSpec(gathered.shape, lambda g, pick: (0, 0, 0, 0)),
                pl.BlockSpec(out_rows.shape, lambda g, pick: (0, 0, 0)),
            ],
            out_specs=[
                pl.BlockSpec((1, patch_count, width), lambda g, pick: (0, 0, 0)),
                pl.BlockSpec((1, groups, patch_count), lambda g, pick: (0, 0, 0)),
            ],
        ),
        out_shape=[
            jax.ShapeDtypeStruct((1, patch_count, width), BF16),
            jax.ShapeDtypeStruct((1, groups, patch_count), BF16),
        ],
        compiler_params=params(DELIVER),
        name="deliver",
    )(pick, frames_in, gathered, out_rows)


def solution(mesh):
    fine = Mesh(mesh.devices.reshape(4, 2, 4, 2, 8), ("zh", "zl", "x", "c", "pool"))
    run = jax.shard_map(
        local,
        mesh=fine,
        in_specs=(
            P(FRAME, None, None),
            P(FRAME, None, "pool"),
            P("pool", FRAME),
            P(FRAME),
            P(FRAME),
        ),
        out_specs=(P(FRAME + ("pool",), None, None), P(FRAME + ("pool",), None, None)),
        check_vma=False,
    )

    def whole(*args):
        shipped, scales = run(*args)
        return shipped, scales

    return whole
```

```python
import jax
import jax.numpy as jnp
from jax import lax
from jax.experimental import pallas as pl
from jax.experimental.pallas import tpu as pltpu
from jax.sharding import Mesh, PartitionSpec as P

HEAD_DIM = 88
GROUP = 128
MAIN = 64
SLOT = 32
ORDER, TRACK, PACK, DELIVER = 30, 50, 40, 30
FACTOR = 1.4426950408889634 / HEAD_DIM**0.5
CHIP = ("zh", "zl", "x")
FRAME = CHIP + ("c",)
F32 = jnp.float32
BF16 = jnp.bfloat16


def lanes_of(shape):
    return lax.broadcasted_iota(jnp.int32, shape, len(shape) - 1)


def turn(value, shift):
    shift = shift % 128
    if shift == 0:
        return value
    return pltpu.roll(value, shift, len(value.shape) - 1)


def spread(value, axis):
    count = lax.axis_size(axis)
    copies = jnp.broadcast_to(value[None], (count,) + value.shape)
    return lax.all_to_all(copies, axis, 0, 0, tiled=True)


def order_kernel(source_ref, right_ref, back_ref, order_ref):
    inner, height = source_ref.shape[:2]
    outer = 4
    rows = height // outer
    for low in range(inner):
        block = source_ref[low].astype(F32)
        for high in range(outer):
            start = (high * inner + low) * rows
            order_ref[start : start + rows, :] = block[high * rows : (high + 1) * rows]
    right_ref[...] = order_ref[...].astype(BF16)
    turned = [order_ref[:, at : at + 128].T[HEAD_DIM:] for at in (0, 128, 256)]
    back_ref[...] = jnp.concatenate(turned, axis=0)[:96].astype(BF16)


def track_kernel(core_ref, tokens_ref, own_ref, other_ref, out_ref, o_ref):
    step = pl.program_id(0)
    core = core_ref[0]
    frames = 2 * tokens_ref.shape[2]
    lane = lanes_of((frames, 128))
    tokens = tokens_ref[...].reshape(frames, tokens_ref.shape[3])
    right = jnp.concatenate([own_ref[...], other_ref[...]], axis=1)
    both = jnp.dot(tokens, right, preferred_element_type=F32)
    ones = jnp.where(lane == 127, 1.0, 0.0)
    for which in range(2):
        head = core if which == 0 else 1 - core
        out = both[:, which * 384 : which * 384 + 384]
        query = jnp.where(lane < HEAD_DIM, out[:, :128] * FACTOR, 0.0).astype(BF16)
        key = out[:, 128:256].astype(BF16)
        value = jnp.where(lane < HEAD_DIM, out[:, 256:], ones).astype(BF16)
        scores = lax.dot_general(query, key, (((1,), (1,)), ((), ())), preferred_element_type=F32)
        top = jnp.max(scores, axis=-1, keepdims=True)
        expo = jnp.exp2(scores - top).astype(BF16)
        mixed = jnp.dot(expo, value, preferred_element_type=F32)
        mixed = jnp.where(lane < HEAD_DIM, mixed * (1.0 / mixed[:, 127:]), 0.0)
        mixed = mixed.reshape(frames // 8, 8, 128)
        o_ref[:, pl.ds(head * 4 + step, 8, stride=8), :] = mixed

    @pl.when(step == pl.num_programs(0) - 1)
    def _():
        pairs = frames // 16
        lane_o = lanes_of((pairs, 8, 128))

        def piece_of(side, owner, late, odd):
            start = (side * 4 + late * 2 + odd) * 8
            return o_ref[owner * pairs : (owner + 1) * pairs, start : start + 8, :]

        for side in range(2):
            for owner in range(2):
                rest = None
                for late in range(2):
                    even, odd = (piece_of(side, owner, late, at) for at in range(2))
                    main = jnp.where(lane_o < MAIN, even, turn(odd, MAIN))
                    out_ref[:, side, owner * 2 + late] = main.astype(BF16)
                    for at, piece in enumerate((even, odd)):
                        part = late * 2 + at
                        piece = turn(piece, SLOT * part - MAIN)
                        rest = piece if part == 0 else jnp.where(lane_o >= SLOT * part, piece, rest)
                out_ref[:, side, 4 + owner] = rest.astype(BF16)


def half_turn(value):
    return pltpu.roll(value, 4, 1)


def pack_kernel(owner_ref, x_ref, out_ref):
    pairs = x_ref.shape[0]
    out_ref[...] = jnp.zeros_like(out_ref)

    def join(even, odd, lane, edges):
        shape = even[0].shape
        upper = lax.broadcasted_iota(jnp.int32, shape, 1) < 4
        first = jnp.where(upper, even[0], half_turn(odd[0]))
        second = jnp.where(upper, half_turn(even[1]), odd[1])
        return jnp.where(lane < edges, first, second)

    lane = lanes_of((pairs, 8, 128))
    lane_h = lanes_of((pairs // 2, 8, 128))
    for fr in range(8):
        place = (fr // 4) * 8 + owner_ref[fr]
        tiles = [x_ref[:, side, fr // 2].astype(F32) for side in range(2)]
        even, odd = (
            [turn(tile, MAIN * head - MAIN * (fr % 2)) for head in range(2)] for tile in tiles
        )
        out_ref[place, :pairs] = join(even, odd, lane, MAIN).astype(BF16)
        tiles = [x_ref[:, side, 4 + fr // 4].astype(F32) for side in range(2)]
        rests = []
        for half in range(2):
            rows = slice(half * (pairs // 2), (half + 1) * (pairs // 2))
            even, odd = (
                [
                    turn(tile[rows], 2 * SLOT * half + SLOT * head - SLOT * (fr % 4))
                    for head in range(2)
                ]
                for tile in tiles
            )
            rests.append(join(even, odd, lane_h, 2 * SLOT * half + SLOT))
        rest = jnp.where(lane_h < 2 * SLOT, rests[0], rests[1])
        out_ref[place, pairs:] = rest.astype(BF16)


def deliver_kernel(pick_ref, frame_ref, y_ref, weight_ref, out_ref, scale_ref):
    sources = y_ref.shape[0]
    heads = sources // 2
    patches, width = frame_ref.shape[1:]
    half = patches // 2
    tiles = half // 8
    valid = pick_ref[1] > 0
    lane = lanes_of((half, 128))

    def weave(first, second):
        upper = lax.broadcasted_iota(jnp.int32, first.shape, 1) < 4
        even = jnp.where(upper, first, half_turn(second))
        odd = jnp.where(upper, half_turn(first), second)
        return jnp.stack([even, odd], axis=1).reshape(first.shape[0] * 16, 128)

    mains, rests = [], []
    for at in range(heads):
        pair = [y_ref[core * heads + at, :tiles].astype(F32) for core in range(2)]
        mains.append(weave(*pair).astype(BF16))
    for at in range(0, heads, 2):
        first, second = (
            weave(*(y_ref[core * heads + one, tiles:].astype(F32) for core in range(2)))
            for one in (at, at + 1)
        )
        low = jnp.where(lane < MAIN, first, turn(second, MAIN))
        high = jnp.where(lane < MAIN, turn(first, MAIN), second)
        rests.append(jnp.concatenate([low, high], axis=0).astype(BF16))
    left = jnp.concatenate(mains, axis=1)
    left_rest = jnp.concatenate(rests, axis=1)
    lane_p = lanes_of((patches, 128))
    scales = jnp.zeros((patches, 128), F32)
    for start in range(0, width, 256):
        stop = min(start + 256, width)
        right, right_rest = (
            jnp.concatenate(
                [weight_ref[at : at + heads, rows, start:stop] for at in (0, heads)], axis=1
            )
            for rows in (slice(0, MAIN), slice(MAIN, MAIN + SLOT))
        )
        right = right.reshape(heads * 2 * MAIN, stop - start)
        right_rest = right_rest.reshape(heads * 2 * SLOT, stop - start)
        total = jnp.dot(left, right, preferred_element_type=F32)
        total += jnp.dot(left_rest, right_rest, preferred_element_type=F32)
        total += frame_ref[0, :, start:stop].astype(F32)
        for at in range(0, stop - start, GROUP):
            part = total[:, at : at + GROUP]
            top = jnp.max(jnp.abs(part), axis=-1, keepdims=True)
            scale = (top + 1e-06).astype(BF16).astype(F32)
            coded = jnp.where(valid, part / scale, 0.0).astype(BF16)
            out_ref[0, :, start + at : start + at + GROUP] = coded
            scales = jnp.where(lane_p == (start + at) // GROUP, scale, scales)
    scales = jnp.where(valid, scales, 0.0).T
    scale_ref[0] = scales[: width // GROUP].astype(BF16)


def normalise(frames):
    xf = frames.astype(F32)
    mean = jnp.mean(xf, axis=-1, keepdims=True)
    centred = xf - mean
    var = jnp.mean(centred * centred, axis=-1, keepdims=True)
    return (centred * lax.rsqrt(var + 1e-06)).astype(BF16)


def params(mebibytes):
    return pltpu.CompilerParams(vmem_limit_bytes=mebibytes * 1024 * 1024)


def local(frames_in, qkv_weight, out_weight, owners, slots):
    fr_count, patch_count, width = frames_in.shape
    rows_here = qkv_weight.shape[0]
    core = lax.axis_index("c")
    position = lax.axis_index("pool")
    chips = lax.axis_size("zh") * lax.axis_size("zl") * lax.axis_size("x")
    pool = lax.axis_size("pool")
    sources = 2 * pool
    swap = [(0, 1), (1, 0)]

    share = frames_in.reshape(fr_count, chips, 8, width)
    share = lax.dynamic_index_in_dim(share, position, 2, keepdims=False)
    share = normalise(share).transpose(1, 0, 2)
    share = lax.all_to_all(share, CHIP, 0, 0, tiled=True).reshape(chips * fr_count, width)
    tracks = lax.all_gather(share, ("c", "pool"), axis=0, tiled=False)
    tracks = tracks.reshape(2, pool, chips * fr_count, width)
    owners_other = lax.ppermute(owners, "c", swap)

    parts = qkv_weight.reshape(rows_here, 3, 2, HEAD_DIM)
    query, key, value = parts[:, 0], parts[:, 1], parts[:, 2]
    back = out_weight.T.reshape(rows_here, 2, HEAD_DIM)
    payload = jnp.concatenate(
        [
            query,
            back[..., :40],
            key,
            back[..., 40:80],
            value,
            back[..., 80:],
            jnp.zeros((rows_here, 2, 32), BF16),
        ],
        axis=-1,
    )
    both = lax.all_gather(payload, "c", axis=0, tiled=True)
    mine = lax.dynamic_index_in_dim(both, core, 1, keepdims=False)
    mine = spread(mine, "zh").reshape(-1, mine.shape[-1])
    mine = spread(mine, ("zl", "x"))
    mine, back_rows = pl.pallas_call(
        order_kernel,
        out_shape=[
            jax.ShapeDtypeStruct((width, 384), BF16),
            jax.ShapeDtypeStruct((96, width), BF16),
        ],
        scratch_shapes=[pltpu.VMEM((width, 384), F32)],
        compiler_params=params(ORDER),
        name="order",
    )(mine)
    mine_other = lax.ppermute(mine, "c", swap)
    out_rows = lax.all_gather(back_rows, ("c", "pool"), axis=0, tiled=False)

    attended = pl.pallas_call(
        track_kernel,
        grid_spec=pltpu.PrefetchScalarGridSpec(
            num_scalar_prefetch=1,
            grid=(4,),
            in_specs=[
                pl.BlockSpec(
                    (2, 1, chips * fr_count, width), lambda p, core: (0, 4 * core[0] + p, 0, 0)
                ),
                pl.BlockSpec(mine.shape, lambda p, core: (0, 0)),
                pl.BlockSpec(mine.shape, lambda p, core: (0, 0)),
            ],
            out_specs=pl.BlockSpec((chips // 2, 2, 6, 8, 128), lambda p, core: (0, 0, 0, 0, 0)),
            scratch_shapes=[pltpu.VMEM((chips, 64, 128), F32)],
        ),
        out_shape=jax.ShapeDtypeStruct((chips // 2, 2, 6, 8, 128), BF16),
        compiler_params=params(TRACK),
        name="track",
    )(core.reshape(1), tracks, mine, mine_other)
    attended = attended.reshape(chips, 6, 8, 128)
    returned = lax.all_to_all(attended, CHIP, 0, 0, tiled=True)

    pair = jnp.where(
        core == 0,
        jnp.concatenate([owners, owners_other]),
        jnp.concatenate([owners_other, owners]),
    )
    packed = pl.pallas_call(
        pack_kernel,
        in_specs=[
            pl.BlockSpec(memory_space=pltpu.SMEM),
            pl.BlockSpec(memory_space=pltpu.VMEM),
        ],
        out_specs=pl.BlockSpec(memory_space=pltpu.VMEM),
        out_shape=jax.ShapeDtypeStruct((sources, 3 * chips // 4, 8, 128), BF16),
        compiler_params=params(PACK),
        name="pack",
    )(pair, returned.reshape(chips // 2, 2, 6, 8, 128))
    gathered = lax.all_to_all(packed, ("c", "pool"), 0, 0, tiled=True)

    match = (owners == position) & (slots == 0)
    chosen = jnp.sum(jnp.where(match, jnp.arange(fr_count, dtype=jnp.int32), 0))
    pick = jnp.stack([chosen, jnp.any(match).astype(jnp.int32)])
    groups = width // GROUP
    return pl.pallas_call(
        deliver_kernel,
        grid_spec=pltpu.PrefetchScalarGridSpec(
            num_scalar_prefetch=1,
            grid=(1,),
            in_specs=[
                pl.BlockSpec((1, patch_count, width), lambda g, pick: (pick[0], 0, 0)),
                pl.BlockSpec(gathered.shape, lambda g, pick: (0, 0, 0, 0)),
                pl.BlockSpec(out_rows.shape, lambda g, pick: (0, 0, 0)),
            ],
            out_specs=[
                pl.BlockSpec((1, patch_count, width), lambda g, pick: (0, 0, 0)),
                pl.BlockSpec((1, groups, patch_count), lambda g, pick: (0, 0, 0)),
            ],
        ),
        out_shape=[
            jax.ShapeDtypeStruct((1, patch_count, width), BF16),
            jax.ShapeDtypeStruct((1, groups, patch_count), BF16),
        ],
        compiler_params=params(DELIVER),
        name="deliver",
    )(pick, frames_in, gathered, out_rows)


def solution(mesh):
    fine = Mesh(mesh.devices.reshape(4, 2, 4, 2, 8), ("zh", "zl", "x", "c", "pool"))
    run = jax.shard_map(
        local,
        mesh=fine,
        in_specs=(
            P(FRAME, None, None),
            P(FRAME, None, "pool"),
            P("pool", FRAME),
            P(FRAME),
            P(FRAME),
        ),
        out_specs=(P(FRAME + ("pool",), None, None), P(FRAME + ("pool",), None, None)),
        check_vma=False,
    )

    def whole(*args):
        shipped, scales = run(*args)
        return shipped, scales

    return whole
```

```python
import jax
import jax.numpy as jnp
from jax import lax
from jax.experimental import pallas as pl
from jax.experimental.pallas import tpu as pltpu
from jax.sharding import Mesh, PartitionSpec as P

HEAD_DIM = 88
GROUP = 128
MAIN = 64
SLOT = 32
ORDER, TRACK, PACK, DELIVER = 30, 50, 40, 30
FACTOR = 1.4426950408889634 / HEAD_DIM**0.5
CHIP = ("zh", "zl", "x")
FRAME = CHIP + ("c",)
F32 = jnp.float32
BF16 = jnp.bfloat16


def lanes_of(shape):
    return lax.broadcasted_iota(jnp.int32, shape, len(shape) - 1)


def turn(value, shift):
    shift = shift % 128
    if shift == 0:
        return value
    return pltpu.roll(value, shift, len(value.shape) - 1)


def spread(value, axis):
    count = lax.axis_size(axis)
    copies = jnp.broadcast_to(value[None], (count,) + value.shape)
    return lax.all_to_all(copies, axis, 0, 0, tiled=True)


def order_kernel(source_ref, right_ref, back_ref, order_ref):
    inner, height = source_ref.shape[:2]
    outer = 4
    rows = height // outer
    for low in range(inner):
        block = source_ref[low].astype(F32)
        for high in range(outer):
            start = (high * inner + low) * rows
            order_ref[start : start + rows, :] = block[high * rows : (high + 1) * rows]
    right_ref[...] = order_ref[...].astype(BF16)
    turned = [order_ref[:, at : at + 128].T[HEAD_DIM:] for at in (0, 128, 256)]
    back_ref[...] = jnp.concatenate(turned, axis=0)[:96].astype(BF16)


def track_kernel(core_ref, tokens_ref, own_ref, other_ref, out_ref, o_ref):
    step = pl.program_id(0)
    core = core_ref[0]
    frames = 2 * tokens_ref.shape[1]
    lane = lanes_of((frames, 128))
    tokens = tokens_ref[...].reshape(frames, tokens_ref.shape[2])
    right = jnp.concatenate([own_ref[...], other_ref[...]], axis=1)
    both = jnp.dot(tokens, right, preferred_element_type=F32)
    ones = jnp.where(lane == 127, 1.0, 0.0)
    for which in range(2):
        head = core if which == 0 else 1 - core
        out = both[:, which * 384 : which * 384 + 384]
        query = jnp.where(lane < HEAD_DIM, out[:, :128] * FACTOR, 0.0).astype(BF16)
        key = out[:, 128:256].astype(BF16)
        value = jnp.where(lane < HEAD_DIM, out[:, 256:], ones).astype(BF16)
        scores = lax.dot_general(query, key, (((1,), (1,)), ((), ())), preferred_element_type=F32)
        top = jnp.max(scores, axis=-1, keepdims=True)
        expo = jnp.exp2(scores - top).astype(BF16)
        mixed = jnp.dot(expo, value, preferred_element_type=F32)
        mixed = jnp.where(lane < HEAD_DIM, mixed * (1.0 / mixed[:, 127:]), 0.0)
        mixed = mixed.reshape(frames // 8, 8, 128)
        o_ref[:, pl.ds(head * 4 + step, 8, stride=8), :] = mixed

    @pl.when(step == pl.num_programs(0) - 1)
    def _():
        pairs = frames // 16
        lane_o = lanes_of((pairs, 8, 128))

        def piece_of(side, owner, late, odd):
            start = (side * 4 + owner * 2 + odd) * 8
            return o_ref[late * pairs : (late + 1) * pairs, start : start + 8, :]

        for side in range(2):
            for owner in range(2):
                rest = None
                for late in range(2):
                    even, odd = (piece_of(side, owner, late, at) for at in range(2))
                    main = jnp.where(lane_o < MAIN, even, turn(odd, MAIN))
                    out_ref[:, side, owner * 2 + late] = main.astype(BF16)
                    for at, piece in enumerate((even, odd)):
                        part = late * 2 + at
                        piece = turn(piece, SLOT * part - MAIN)
                        rest = piece if part == 0 else jnp.where(lane_o >= SLOT * part, piece, rest)
                out_ref[:, side, 4 + owner] = rest.astype(BF16)


def half_turn(value):
    return pltpu.roll(value, 4, 1)


def pack_kernel(owner_ref, x_ref, out_ref):
    pairs = x_ref.shape[0]
    out_ref[...] = jnp.zeros_like(out_ref)

    def join(even, odd, lane, edges):
        shape = even[0].shape
        upper = lax.broadcasted_iota(jnp.int32, shape, 1) < 4
        first = jnp.where(upper, even[0], half_turn(odd[0]))
        second = jnp.where(upper, half_turn(even[1]), odd[1])
        return jnp.where(lane < edges, first, second)

    lane = lanes_of((pairs, 8, 128))
    lane_h = lanes_of((pairs // 2, 8, 128))
    for fr in range(8):
        place = (fr // 4) * 8 + owner_ref[fr]
        tiles = [x_ref[:, side, fr // 2].astype(F32) for side in range(2)]
        even, odd = (
            [turn(tile, MAIN * head - MAIN * (fr % 2)) for head in range(2)] for tile in tiles
        )
        out_ref[place, :pairs] = join(even, odd, lane, MAIN).astype(BF16)
        tiles = [x_ref[:, side, 4 + fr // 4].astype(F32) for side in range(2)]
        rests = []
        for half in range(2):
            rows = slice(half * (pairs // 2), (half + 1) * (pairs // 2))
            even, odd = (
                [
                    turn(tile[rows], 2 * SLOT * half + SLOT * head - SLOT * (fr % 4))
                    for head in range(2)
                ]
                for tile in tiles
            )
            rests.append(join(even, odd, lane_h, 2 * SLOT * half + SLOT))
        rest = jnp.where(lane_h < 2 * SLOT, rests[0], rests[1])
        out_ref[place, pairs:] = rest.astype(BF16)


def deliver_kernel(pick_ref, frame_ref, y_ref, weight_ref, out_ref, scale_ref):
    sources = y_ref.shape[0]
    heads = sources // 2
    patches, width = frame_ref.shape[1:]
    half = patches // 2
    tiles = half // 8
    valid = pick_ref[1] > 0
    lane = lanes_of((half, 128))

    def weave(first, second):
        upper = lax.broadcasted_iota(jnp.int32, first.shape, 1) < 4
        even = jnp.where(upper, first, half_turn(second))
        odd = jnp.where(upper, half_turn(first), second)
        return jnp.stack([even, odd], axis=1).reshape(first.shape[0] * 16, 128)

    mains, rests = [], []
    for at in range(heads):
        pair = [y_ref[core * heads + at, :tiles].astype(F32) for core in range(2)]
        mains.append(weave(*pair).astype(BF16))
    for at in range(0, heads, 2):
        first, second = (
            weave(*(y_ref[core * heads + one, tiles:].astype(F32) for core in range(2)))
            for one in (at, at + 1)
        )
        low = jnp.where(lane < MAIN, first, turn(second, MAIN))
        high = jnp.where(lane < MAIN, turn(first, MAIN), second)
        rests.append(jnp.concatenate([low, high], axis=0).astype(BF16))
    left = jnp.concatenate(mains, axis=1)
    left_rest = jnp.concatenate(rests, axis=1)
    lane_p = lanes_of((patches, 128))
    scales = jnp.zeros((patches, 128), F32)
    for start in range(0, width, 256):
        stop = min(start + 256, width)
        right, right_rest = (
            jnp.concatenate(
                [weight_ref[at : at + heads, rows, start:stop] for at in (0, heads)], axis=1
            )
            for rows in (slice(0, MAIN), slice(MAIN, MAIN + SLOT))
        )
        right = right.reshape(heads * 2 * MAIN, stop - start)
        right_rest = right_rest.reshape(heads * 2 * SLOT, stop - start)
        total = jnp.dot(left, right, preferred_element_type=F32)
        total += jnp.dot(left_rest, right_rest, preferred_element_type=F32)
        total += frame_ref[0, :, start:stop].astype(F32)
        for at in range(0, stop - start, GROUP):
            part = total[:, at : at + GROUP]
            top = jnp.max(jnp.abs(part), axis=-1, keepdims=True)
            scale = (top + 1e-06).astype(BF16).astype(F32)
            coded = jnp.where(valid, part * (1.0 / scale), 0.0).astype(BF16)
            out_ref[0, :, start + at : start + at + GROUP] = coded
            scales = jnp.where(lane_p == (start + at) // GROUP, scale, scales)
    scales = jnp.where(valid, scales, 0.0).T
    scale_ref[0] = scales[: width // GROUP].astype(BF16)


def normalise(frames):
    xf = frames.astype(F32)
    mean = jnp.mean(xf, axis=-1, keepdims=True)
    centred = xf - mean
    var = jnp.mean(centred * centred, axis=-1, keepdims=True)
    return (centred * lax.rsqrt(var + 1e-06)).astype(BF16)


def params(mebibytes):
    return pltpu.CompilerParams(vmem_limit_bytes=mebibytes * 1024 * 1024)


def local(frames_in, qkv_weight, out_weight, owners, slots):
    fr_count, patch_count, width = frames_in.shape
    rows_here = qkv_weight.shape[0]
    core = lax.axis_index("c")
    position = lax.axis_index("pool")
    chips = lax.axis_size("zh") * lax.axis_size("zl") * lax.axis_size("x")
    sources = 2 * lax.axis_size("pool")
    swap = [(0, 1), (1, 0)]

    grid = frames_in.reshape(2, 2, chips, 8, width)
    share = jnp.concatenate(
        [
            lax.dynamic_slice(
                grid, (position % 2, 0, 0, position // 2 + at, 0), (1, 2, chips, 1, width)
            )[0]
            for at in (0, 4)
        ],
        axis=2,
    )
    share = normalise(share).transpose(1, 2, 0, 3).reshape(2 * chips, 2, width)
    share = lax.all_to_all(share, FRAME, 0, 0, tiled=True).reshape(4 * chips, width)
    tracks = lax.all_gather(share, "pool", axis=0, tiled=False)
    owners_other = lax.ppermute(owners, "c", swap)

    parts = qkv_weight.reshape(rows_here, 3, 2, HEAD_DIM)
    query, key, value = parts[:, 0], parts[:, 1], parts[:, 2]
    back = out_weight.T.reshape(rows_here, 2, HEAD_DIM)
    payload = jnp.concatenate(
        [
            query,
            back[..., :40],
            key,
            back[..., 40:80],
            value,
            back[..., 80:],
            jnp.zeros((rows_here, 2, 32), BF16),
        ],
        axis=-1,
    )
    both = lax.all_gather(payload, "c", axis=0, tiled=True)
    mine = lax.dynamic_index_in_dim(both, core, 1, keepdims=False)
    mine = spread(mine, "zh").reshape(-1, mine.shape[-1])
    mine = spread(mine, ("zl", "x"))
    mine, back_rows = pl.pallas_call(
        order_kernel,
        out_shape=[
            jax.ShapeDtypeStruct((width, 384), BF16),
            jax.ShapeDtypeStruct((96, width), BF16),
        ],
        scratch_shapes=[pltpu.VMEM((width, 384), F32)],
        compiler_params=params(ORDER),
        name="order",
    )(mine)
    mine_other = lax.ppermute(mine, "c", swap)
    out_rows = lax.all_gather(back_rows, ("c", "pool"), axis=0, tiled=False)

    attended = pl.pallas_call(
        track_kernel,
        grid=(4,),
        in_specs=[
            pl.BlockSpec(memory_space=pltpu.SMEM),
            pl.BlockSpec((2, 4 * chips, width), lambda p: (p, 0, 0)),
            pl.BlockSpec(mine.shape, lambda p: (0, 0)),
            pl.BlockSpec(mine.shape, lambda p: (0, 0)),
        ],
        out_specs=pl.BlockSpec((chips // 2, 2, 6, 8, 128), lambda p: (0, 0, 0, 0, 0)),
        out_shape=jax.ShapeDtypeStruct((chips // 2, 2, 6, 8, 128), BF16),
        scratch_shapes=[pltpu.VMEM((chips, 64, 128), F32)],
        compiler_params=params(TRACK),
        name="track",
    )(core.reshape(1), tracks, mine, mine_other)
    attended = attended.reshape(chips, 6, 8, 128)
    returned = lax.all_to_all(attended, CHIP, 0, 0, tiled=True)

    pair = jnp.where(
        core == 0,
        jnp.concatenate([owners, owners_other]),
        jnp.concatenate([owners_other, owners]),
    )
    packed = pl.pallas_call(
        pack_kernel,
        in_specs=[
            pl.BlockSpec(memory_space=pltpu.SMEM),
            pl.BlockSpec(memory_space=pltpu.VMEM),
        ],
        out_specs=pl.BlockSpec(memory_space=pltpu.VMEM),
        out_shape=jax.ShapeDtypeStruct((sources, 3 * chips // 4, 8, 128), BF16),
        compiler_params=params(PACK),
        name="pack",
    )(pair, returned.reshape(chips // 2, 2, 6, 8, 128))
    gathered = lax.all_to_all(packed, ("c", "pool"), 0, 0, tiled=True)

    match = (owners == position) & (slots == 0)
    chosen = jnp.sum(jnp.where(match, jnp.arange(fr_count, dtype=jnp.int32), 0))
    pick = jnp.stack([chosen, jnp.any(match).astype(jnp.int32)])
    groups = width // GROUP
    return pl.pallas_call(
        deliver_kernel,
        grid_spec=pltpu.PrefetchScalarGridSpec(
            num_scalar_prefetch=1,
            grid=(1,),
            in_specs=[
                pl.BlockSpec((1, patch_count, width), lambda g, pick: (pick[0], 0, 0)),
                pl.BlockSpec(gathered.shape, lambda g, pick: (0, 0, 0, 0)),
                pl.BlockSpec(out_rows.shape, lambda g, pick: (0, 0, 0)),
            ],
            out_specs=[
                pl.BlockSpec((1, patch_count, width), lambda g, pick: (0, 0, 0)),
                pl.BlockSpec((1, groups, patch_count), lambda g, pick: (0, 0, 0)),
            ],
        ),
        out_shape=[
            jax.ShapeDtypeStruct((1, patch_count, width), BF16),
            jax.ShapeDtypeStruct((1, groups, patch_count), BF16),
        ],
        compiler_params=params(DELIVER),
        name="deliver",
    )(pick, frames_in, gathered, out_rows)


def solution(mesh):
    fine = Mesh(mesh.devices.reshape(4, 2, 4, 2, 8), ("zh", "zl", "x", "c", "pool"))
    run = jax.shard_map(
        local,
        mesh=fine,
        in_specs=(
            P(FRAME, None, None),
            P(FRAME, None, "pool"),
            P("pool", FRAME),
            P(FRAME),
            P(FRAME),
        ),
        out_specs=(P(FRAME + ("pool",), None, None), P(FRAME + ("pool",), None, None)),
        check_vma=False,
    )

    def whole(*args):
        shipped, scales = run(*args)
        return shipped, scales

    return whole
```

```python
import jax
import jax.numpy as jnp
from jax import lax
from jax.experimental import pallas as pl
from jax.experimental.pallas import tpu as pltpu
from jax.sharding import Mesh, PartitionSpec as P

HEAD_DIM = 88
GROUP = 128
MAIN = 64
SLOT = 32
SHARE, ORDER, TRACK, PACK, DELIVER = 58, 30, 50, 40, 30
FACTOR = 1.4426950408889634 / HEAD_DIM**0.5
CHIP = ("zh", "zl", "x")
FRAME = CHIP + ("c",)
F32 = jnp.float32
BF16 = jnp.bfloat16


def lanes_of(shape):
    return lax.broadcasted_iota(jnp.int32, shape, len(shape) - 1)


def turn(value, shift):
    shift = shift % 128
    if shift == 0:
        return value
    return pltpu.roll(value, shift, len(value.shape) - 1)


def spread(value, axis):
    count = lax.axis_size(axis)
    copies = jnp.broadcast_to(value[None], (count,) + value.shape)
    return lax.all_to_all(copies, axis, 0, 0, tiled=True)


def share_kernel(at_ref, frames_ref, out_ref):
    count, patches, width = frames_ref.shape
    rows = out_ref.shape[0] * out_ref.shape[1]
    row = lax.broadcasted_iota(jnp.int32, (rows, count * patches), 0)
    column = lax.broadcasted_iota(jnp.int32, (rows, count * patches), 1)
    wanted = (row & 1) * patches + (row >> 2) * 8 + ((row >> 1) & 1) * 4 + (at_ref[0] >> 1)
    pick = jnp.where(column == wanted, 1.0, 0.0).astype(BF16)
    tokens = frames_ref[...].reshape(count * patches, width)
    xf = jnp.dot(pick, tokens, preferred_element_type=F32)
    mean = jnp.mean(xf, axis=-1, keepdims=True)
    centred = xf - mean
    var = jnp.mean(centred * centred, axis=-1, keepdims=True)
    normed = centred * lax.rsqrt(var + 1e-06)
    out_ref[...] = normed.reshape(out_ref.shape).astype(BF16)


def order_kernel(source_ref, right_ref, back_ref, order_ref):
    inner, height = source_ref.shape[:2]
    outer = 4
    rows = height // outer
    for low in range(inner):
        block = source_ref[low].astype(F32)
        for high in range(outer):
            start = (high * inner + low) * rows
            order_ref[start : start + rows, :] = block[high * rows : (high + 1) * rows]
    right_ref[...] = order_ref[...].astype(BF16)
    turned = [order_ref[:, at : at + 128].T[HEAD_DIM:] for at in (0, 128, 256)]
    back_ref[...] = jnp.concatenate(turned, axis=0)[:96].astype(BF16)


def track_kernel(core_ref, tokens_ref, own_ref, other_ref, out_ref, o_ref):
    step = pl.program_id(0)
    core = core_ref[0]
    frames = 2 * tokens_ref.shape[1]
    lane = lanes_of((frames, 128))
    tokens = tokens_ref[...].reshape(frames, tokens_ref.shape[2])
    right = jnp.concatenate([own_ref[...], other_ref[...]], axis=1)
    both = jnp.dot(tokens, right, preferred_element_type=F32)
    ones = jnp.where(lane == 127, 1.0, 0.0)
    for which in range(2):
        head = core if which == 0 else 1 - core
        out = both[:, which * 384 : which * 384 + 384]
        query = jnp.where(lane < HEAD_DIM, out[:, :128] * FACTOR, 0.0).astype(BF16)
        key = out[:, 128:256].astype(BF16)
        value = jnp.where(lane < HEAD_DIM, out[:, 256:], ones).astype(BF16)
        scores = lax.dot_general(query, key, (((1,), (1,)), ((), ())), preferred_element_type=F32)
        top = jnp.max(scores, axis=-1, keepdims=True)
        expo = jnp.exp2(scores - top).astype(BF16)
        mixed = jnp.dot(expo, value, preferred_element_type=F32)
        mixed = jnp.where(lane < HEAD_DIM, mixed * (1.0 / mixed[:, 127:]), 0.0)
        mixed = mixed.reshape(frames // 8, 8, 128)
        o_ref[:, pl.ds(head * 4 + step, 8, stride=8), :] = mixed

    @pl.when(step == pl.num_programs(0) - 1)
    def _():
        pairs = frames // 16
        lane_o = lanes_of((pairs, 8, 128))

        def piece_of(side, owner, late, odd):
            start = (side * 4 + owner * 2 + odd) * 8
            return o_ref[late * pairs : (late + 1) * pairs, start : start + 8, :]

        for side in range(2):
            for owner in range(2):
                rest = None
                for late in range(2):
                    even, odd = (piece_of(side, owner, late, at) for at in range(2))
                    main = jnp.where(lane_o < MAIN, even, turn(odd, MAIN))
                    out_ref[:, side, owner * 2 + late] = main.astype(BF16)
                    for at, piece in enumerate((even, odd)):
                        part = late * 2 + at
                        piece = turn(piece, SLOT * part - MAIN)
                        rest = piece if part == 0 else jnp.where(lane_o >= SLOT * part, piece, rest)
                out_ref[:, side, 4 + owner] = rest.astype(BF16)


def half_turn(value):
    return pltpu.roll(value, 4, 1)


def pack_kernel(owner_ref, x_ref, out_ref):
    pairs = x_ref.shape[0]
    out_ref[...] = jnp.zeros_like(out_ref)

    def join(even, odd, lane, edges):
        shape = even[0].shape
        upper = lax.broadcasted_iota(jnp.int32, shape, 1) < 4
        first = jnp.where(upper, even[0], half_turn(odd[0]))
        second = jnp.where(upper, half_turn(even[1]), odd[1])
        return jnp.where(lane < edges, first, second)

    lane = lanes_of((pairs, 8, 128))
    lane_h = lanes_of((pairs // 2, 8, 128))
    for fr in range(8):
        place = (fr // 4) * 8 + owner_ref[fr]
        tiles = [x_ref[:, side, fr // 2].astype(F32) for side in range(2)]
        even, odd = (
            [turn(tile, MAIN * head - MAIN * (fr % 2)) for head in range(2)] for tile in tiles
        )
        out_ref[place, :pairs] = join(even, odd, lane, MAIN).astype(BF16)
        tiles = [x_ref[:, side, 4 + fr // 4].astype(F32) for side in range(2)]
        rests = []
        for half in range(2):
            rows = slice(half * (pairs // 2), (half + 1) * (pairs // 2))
            even, odd = (
                [
                    turn(tile[rows], 2 * SLOT * half + SLOT * head - SLOT * (fr % 4))
                    for head in range(2)
                ]
                for tile in tiles
            )
            rests.append(join(even, odd, lane_h, 2 * SLOT * half + SLOT))
        rest = jnp.where(lane_h < 2 * SLOT, rests[0], rests[1])
        out_ref[place, pairs:] = rest.astype(BF16)


def deliver_kernel(pick_ref, frame_ref, y_ref, weight_ref, out_ref, scale_ref):
    sources = y_ref.shape[0]
    heads = sources // 2
    patches, width = frame_ref.shape[1:]
    half = patches // 2
    tiles = half // 8
    valid = pick_ref[1] > 0
    lane = lanes_of((half, 128))

    def weave(first, second):
        upper = lax.broadcasted_iota(jnp.int32, first.shape, 1) < 4
        even = jnp.where(upper, first, half_turn(second))
        odd = jnp.where(upper, half_turn(first), second)
        return jnp.stack([even, odd], axis=1).reshape(first.shape[0] * 16, 128)

    mains, rests = [], []
    for at in range(heads):
        pair = [y_ref[core * heads + at, :tiles].astype(F32) for core in range(2)]
        mains.append(weave(*pair).astype(BF16))
    for at in range(0, heads, 2):
        first, second = (
            weave(*(y_ref[core * heads + one, tiles:].astype(F32) for core in range(2)))
            for one in (at, at + 1)
        )
        low = jnp.where(lane < MAIN, first, turn(second, MAIN))
        high = jnp.where(lane < MAIN, turn(first, MAIN), second)
        rests.append(jnp.concatenate([low, high], axis=0).astype(BF16))
    left = jnp.concatenate(mains, axis=1)
    left_rest = jnp.concatenate(rests, axis=1)
    lane_p = lanes_of((patches, 128))
    scales = jnp.zeros((patches, 128), F32)
    for start in range(0, width, 256):
        stop = min(start + 256, width)
        right, right_rest = (
            jnp.concatenate(
                [weight_ref[at : at + heads, rows, start:stop] for at in (0, heads)], axis=1
            )
            for rows in (slice(0, MAIN), slice(MAIN, MAIN + SLOT))
        )
        right = right.reshape(heads * 2 * MAIN, stop - start)
        right_rest = right_rest.reshape(heads * 2 * SLOT, stop - start)
        total = jnp.dot(left, right, preferred_element_type=F32)
        total += jnp.dot(left_rest, right_rest, preferred_element_type=F32)
        total += frame_ref[0, :, start:stop].astype(F32)
        for at in range(0, stop - start, GROUP):
            part = total[:, at : at + GROUP]
            top = jnp.max(jnp.abs(part), axis=-1, keepdims=True)
            scale = (top + 1e-06).astype(BF16).astype(F32)
            coded = jnp.where(valid, part * (1.0 / scale), 0.0).astype(BF16)
            out_ref[0, :, start + at : start + at + GROUP] = coded
            scales = jnp.where(lane_p == (start + at) // GROUP, scale, scales)
    scales = jnp.where(valid, scales, 0.0).T
    scale_ref[0] = scales[: width // GROUP].astype(BF16)


def params(mebibytes):
    return pltpu.CompilerParams(vmem_limit_bytes=mebibytes * 1024 * 1024)


def local(frames_in, qkv_weight, out_weight, owners, slots):
    fr_count, patch_count, width = frames_in.shape
    rows_here = qkv_weight.shape[0]
    core = lax.axis_index("c")
    position = lax.axis_index("pool")
    chips = lax.axis_size("zh") * lax.axis_size("zl") * lax.axis_size("x")
    sources = 2 * lax.axis_size("pool")
    swap = [(0, 1), (1, 0)]

    share = pl.pallas_call(
        share_kernel,
        grid_spec=pltpu.PrefetchScalarGridSpec(
            num_scalar_prefetch=1,
            grid=(1,),
            in_specs=[pl.BlockSpec((2, patch_count, width), lambda g, at: (at[0] & 1, 0, 0))],
            out_specs=pl.BlockSpec((2 * chips, 2, width), lambda g, at: (0, 0, 0)),
        ),
        out_shape=jax.ShapeDtypeStruct((2 * chips, 2, width), BF16),
        compiler_params=params(SHARE),
        name="share",
    )(position.reshape(1), frames_in)
    share = lax.all_to_all(share, FRAME, 0, 0, tiled=True).reshape(4 * chips, width)
    tracks = lax.all_gather(share, "pool", axis=0, tiled=False)
    owners_other = lax.ppermute(owners, "c", swap)

    parts = qkv_weight.reshape(rows_here, 3, 2, HEAD_DIM)
    query, key, value = parts[:, 0], parts[:, 1], parts[:, 2]
    back = out_weight.T.reshape(rows_here, 2, HEAD_DIM)
    payload = jnp.concatenate(
        [
            query,
            back[..., :40],
            key,
            back[..., 40:80],
            value,
            back[..., 80:],
            jnp.zeros((rows_here, 2, 32), BF16),
        ],
        axis=-1,
    )
    both = lax.all_gather(payload, "c", axis=0, tiled=True)
    mine = lax.dynamic_index_in_dim(both, core, 1, keepdims=False)
    mine = spread(mine, "zh").reshape(-1, mine.shape[-1])
    mine = spread(mine, ("zl", "x"))
    mine, back_rows = pl.pallas_call(
        order_kernel,
        out_shape=[
            jax.ShapeDtypeStruct((width, 384), BF16),
            jax.ShapeDtypeStruct((96, width), BF16),
        ],
        scratch_shapes=[pltpu.VMEM((width, 384), F32)],
        compiler_params=params(ORDER),
        name="order",
    )(mine)
    mine_other = lax.ppermute(mine, "c", swap)
    out_rows = lax.all_gather(back_rows, ("c", "pool"), axis=0, tiled=False)

    attended = pl.pallas_call(
        track_kernel,
        grid=(4,),
        in_specs=[
            pl.BlockSpec(memory_space=pltpu.SMEM),
            pl.BlockSpec((2, 4 * chips, width), lambda p: (p, 0, 0)),
            pl.BlockSpec(mine.shape, lambda p: (0, 0)),
            pl.BlockSpec(mine.shape, lambda p: (0, 0)),
        ],
        out_specs=pl.BlockSpec((chips // 2, 2, 6, 8, 128), lambda p: (0, 0, 0, 0, 0)),
        out_shape=jax.ShapeDtypeStruct((chips // 2, 2, 6, 8, 128), BF16),
        scratch_shapes=[pltpu.VMEM((chips, 64, 128), F32)],
        compiler_params=params(TRACK),
        name="track",
    )(core.reshape(1), tracks, mine, mine_other)
    attended = attended.reshape(chips, 6, 8, 128)
    returned = lax.all_to_all(attended, CHIP, 0, 0, tiled=True)

    pair = jnp.where(
        core == 0,
        jnp.concatenate([owners, owners_other]),
        jnp.concatenate([owners_other, owners]),
    )
    packed = pl.pallas_call(
        pack_kernel,
        in_specs=[
            pl.BlockSpec(memory_space=pltpu.SMEM),
            pl.BlockSpec(memory_space=pltpu.VMEM),
        ],
        out_specs=pl.BlockSpec(memory_space=pltpu.VMEM),
        out_shape=jax.ShapeDtypeStruct((sources, 3 * chips // 4, 8, 128), BF16),
        compiler_params=params(PACK),
        name="pack",
    )(pair, returned.reshape(chips // 2, 2, 6, 8, 128))
    gathered = lax.all_to_all(packed, ("c", "pool"), 0, 0, tiled=True)

    match = (owners == position) & (slots == 0)
    chosen = jnp.sum(jnp.where(match, jnp.arange(fr_count, dtype=jnp.int32), 0))
    pick = jnp.stack([chosen, jnp.any(match).astype(jnp.int32)])
    groups = width // GROUP
    return pl.pallas_call(
        deliver_kernel,
        grid_spec=pltpu.PrefetchScalarGridSpec(
            num_scalar_prefetch=1,
            grid=(1,),
            in_specs=[
                pl.BlockSpec((1, patch_count, width), lambda g, pick: (pick[0], 0, 0)),
                pl.BlockSpec(gathered.shape, lambda g, pick: (0, 0, 0, 0)),
                pl.BlockSpec(out_rows.shape, lambda g, pick: (0, 0, 0)),
            ],
            out_specs=[
                pl.BlockSpec((1, patch_count, width), lambda g, pick: (0, 0, 0)),
                pl.BlockSpec((1, groups, patch_count), lambda g, pick: (0, 0, 0)),
            ],
        ),
        out_shape=[
            jax.ShapeDtypeStruct((1, patch_count, width), BF16),
            jax.ShapeDtypeStruct((1, groups, patch_count), BF16),
        ],
        compiler_params=params(DELIVER),
        name="deliver",
    )(pick, frames_in, gathered, out_rows)


def solution(mesh):
    fine = Mesh(mesh.devices.reshape(4, 2, 4, 2, 8), ("zh", "zl", "x", "c", "pool"))
    run = jax.shard_map(
        local,
        mesh=fine,
        in_specs=(
            P(FRAME, None, None),
            P(FRAME, None, "pool"),
            P("pool", FRAME),
            P(FRAME),
            P(FRAME),
        ),
        out_specs=(P(FRAME + ("pool",), None, None), P(FRAME + ("pool",), None, None)),
        check_vma=False,
    )

    def whole(*args):
        shipped, scales = run(*args)
        return shipped, scales

    return whole
```

```python
import jax
import jax.numpy as jnp
from jax import lax
from jax.experimental import pallas as pl
from jax.experimental.pallas import tpu as pltpu
from jax.sharding import Mesh, PartitionSpec as P

HEAD_DIM = 88
GROUP = 128
MAIN = 64
SLOT = 32
STEP = 4
SHARE, ORDER, TRACK, PACK, DELIVER = 58, 30, 40, 40, 52
FACTOR = 1.4426950408889634 / HEAD_DIM**0.5
CHIP = ("zh", "zl", "x")
FRAME = CHIP + ("c",)
F32 = jnp.float32
BF16 = jnp.bfloat16


def lanes_of(shape):
    return lax.broadcasted_iota(jnp.int32, shape, len(shape) - 1)


def turn(value, shift):
    shift = shift % 128
    if shift == 0:
        return value
    return pltpu.roll(value, shift, len(value.shape) - 1)


def spread(value, axis):
    count = lax.axis_size(axis)
    copies = jnp.broadcast_to(value[None], (count,) + value.shape)
    return lax.all_to_all(copies, axis, 0, 0, tiled=True)


def share_kernel(at_ref, frames_ref, out_ref):
    count, patches, width = frames_ref.shape
    rows = out_ref.shape[0] * out_ref.shape[1]
    row = lax.broadcasted_iota(jnp.int32, (rows, count * patches), 0)
    column = lax.broadcasted_iota(jnp.int32, (rows, count * patches), 1)
    wanted = (row & 1) * patches + (row >> 2) * 8 + ((row >> 1) & 1) * 4 + (at_ref[0] >> 1)
    pick = jnp.where(column == wanted, 1.0, 0.0).astype(BF16)
    tokens = frames_ref[...].reshape(count * patches, width)
    xf = jnp.dot(pick, tokens, preferred_element_type=F32)
    mean = jnp.mean(xf, axis=-1, keepdims=True)
    centred = xf - mean
    var = jnp.mean(centred * centred, axis=-1, keepdims=True)
    normed = centred * lax.rsqrt(var + 1e-06)
    out_ref[...] = normed.reshape(out_ref.shape).astype(BF16)


def order_kernel(source_ref, right_ref, back_ref, order_ref):
    inner, height = source_ref.shape[:2]
    outer = 4
    rows = height // outer
    for low in range(inner):
        block = source_ref[low].astype(F32)
        for high in range(outer):
            start = (high * inner + low) * rows
            order_ref[start : start + rows, :] = block[high * rows : (high + 1) * rows]
    right_ref[...] = order_ref[...].astype(BF16)
    turned = [order_ref[:, at : at + 128].T[HEAD_DIM:] for at in (0, 128, 256)]
    back_ref[...] = jnp.concatenate(turned, axis=0)[:96].astype(BF16)


def track_kernel(core_ref, tokens_ref, own_ref, other_ref, out_ref, o_ref):
    step = pl.program_id(0)
    core = core_ref[0]
    here = tokens_ref.shape[0] // 2
    frames = 2 * tokens_ref.shape[1]
    lane = lanes_of((frames, 128))
    right = jnp.concatenate([own_ref[...], other_ref[...]], axis=1)
    ones = jnp.where(lane == 127, 1.0, 0.0)
    for track in range(here):
        tokens = tokens_ref[2 * track : 2 * track + 2].reshape(frames, tokens_ref.shape[2])
        both = jnp.dot(tokens, right, preferred_element_type=F32)
        for which in range(2):
            head = core if which == 0 else 1 - core
            out = both[:, which * 384 : which * 384 + 384]
            query = jnp.where(lane < HEAD_DIM, out[:, :128] * FACTOR, 0.0).astype(BF16)
            key = out[:, 128:256].astype(BF16)
            value = jnp.where(lane < HEAD_DIM, out[:, 256:], ones).astype(BF16)
            scores = lax.dot_general(
                query, key, (((1,), (1,)), ((), ())), preferred_element_type=F32
            )
            top = jnp.max(scores, axis=-1, keepdims=True)
            expo = jnp.exp2(scores - top).astype(BF16)
            mixed = jnp.dot(expo, value, preferred_element_type=F32)
            mixed = jnp.where(lane < HEAD_DIM, mixed * (1.0 / mixed[:, 127:]), 0.0)
            mixed = mixed.reshape(frames // 8, 8, 128)
            o_ref[:, pl.ds(head * 4 + step * here + track, 8, stride=8), :] = mixed

    @pl.when(step == pl.num_programs(0) - 1)
    def _():
        pairs = frames // 16
        lane_o = lanes_of((pairs, 8, 128))

        def piece_of(side, owner, late, odd):
            start = (side * 4 + owner * 2 + odd) * 8
            return o_ref[late * pairs : (late + 1) * pairs, start : start + 8, :]

        for side in range(2):
            for owner in range(2):
                rest = None
                for late in range(2):
                    even, odd = (piece_of(side, owner, late, at) for at in range(2))
                    main = jnp.where(lane_o < MAIN, even, turn(odd, MAIN))
                    out_ref[:, side, owner * 2 + late] = main.astype(BF16)
                    for at, piece in enumerate((even, odd)):
                        part = late * 2 + at
                        piece = turn(piece, SLOT * part - MAIN)
                        rest = piece if part == 0 else jnp.where(lane_o >= SLOT * part, piece, rest)
                out_ref[:, side, 4 + owner] = rest.astype(BF16)


def half_turn(value):
    return pltpu.roll(value, 4, 1)


def pack_kernel(owner_ref, x_ref, out_ref):
    pairs = x_ref.shape[0]
    out_ref[...] = jnp.zeros_like(out_ref)

    def join(even, odd, lane, edges):
        shape = even[0].shape
        upper = lax.broadcasted_iota(jnp.int32, shape, 1) < 4
        first = jnp.where(upper, even[0], half_turn(odd[0]))
        second = jnp.where(upper, half_turn(even[1]), odd[1])
        return jnp.where(lane < edges, first, second)

    lane = lanes_of((pairs, 8, 128))
    lane_h = lanes_of((pairs // 2, 8, 128))
    for fr in range(8):
        place = (fr // 4) * 8 + owner_ref[fr]
        tiles = [x_ref[:, side, fr // 2].astype(F32) for side in range(2)]
        even, odd = (
            [turn(tile, MAIN * head - MAIN * (fr % 2)) for head in range(2)] for tile in tiles
        )
        out_ref[place, :pairs] = join(even, odd, lane, MAIN).astype(BF16)
        tiles = [x_ref[:, side, 4 + fr // 4].astype(F32) for side in range(2)]
        rests = []
        for half in range(2):
            rows = slice(half * (pairs // 2), (half + 1) * (pairs // 2))
            even, odd = (
                [
                    turn(tile[rows], 2 * SLOT * half + SLOT * head - SLOT * (fr % 4))
                    for head in range(2)
                ]
                for tile in tiles
            )
            rests.append(join(even, odd, lane_h, 2 * SLOT * half + SLOT))
        rest = jnp.where(lane_h < 2 * SLOT, rests[0], rests[1])
        out_ref[place, pairs:] = rest.astype(BF16)


def deliver_kernel(pick_ref, frame_ref, y_ref, weight_ref, out_ref, scale_ref):
    sources = y_ref.shape[0]
    heads = sources // 2
    patches, width = frame_ref.shape[1:]
    half = patches // 2
    tiles = half // 8
    valid = pick_ref[1] > 0
    lane = lanes_of((half, 128))

    def weave(first, second):
        upper = lax.broadcasted_iota(jnp.int32, first.shape, 1) < 4
        even = jnp.where(upper, first, half_turn(second))
        odd = jnp.where(upper, half_turn(first), second)
        return jnp.stack([even, odd], axis=1).reshape(first.shape[0] * 16, 128)

    mains, rests = [], []
    for at in range(heads):
        pair = [y_ref[core * heads + at, :tiles].astype(F32) for core in range(2)]
        mains.append(weave(*pair).astype(BF16))
    for at in range(0, heads, 2):
        first, second = (
            weave(*(y_ref[core * heads + one, tiles:].astype(F32) for core in range(2)))
            for one in (at, at + 1)
        )
        low = jnp.where(lane < MAIN, first, turn(second, MAIN))
        high = jnp.where(lane < MAIN, turn(first, MAIN), second)
        rests.append(jnp.concatenate([low, high], axis=0).astype(BF16))
    left = jnp.concatenate(mains, axis=1)
    left_rest = jnp.concatenate(rests, axis=1)
    lane_p = lanes_of((patches, 128))
    scales = jnp.zeros((patches, 128), F32)
    for start in range(0, width, 256):
        stop = min(start + 256, width)
        right, right_rest = (
            jnp.concatenate(
                [weight_ref[at : at + heads, rows, start:stop] for at in (0, heads)], axis=1
            )
            for rows in (slice(0, MAIN), slice(MAIN, MAIN + SLOT))
        )
        right = right.reshape(heads * 2 * MAIN, stop - start)
        right_rest = right_rest.reshape(heads * 2 * SLOT, stop - start)
        total = jnp.dot(left, right, preferred_element_type=F32)
        total += jnp.dot(left_rest, right_rest, preferred_element_type=F32)
        total += frame_ref[0, :, start:stop].astype(F32)
        for at in range(0, stop - start, GROUP):
            part = total[:, at : at + GROUP]
            top = jnp.max(jnp.abs(part), axis=-1, keepdims=True)
            scale = (top + 1e-06).astype(BF16).astype(F32)
            coded = jnp.where(valid, part * (1.0 / scale), 0.0).astype(BF16)
            out_ref[0, :, start + at : start + at + GROUP] = coded
            scales = jnp.where(lane_p == (start + at) // GROUP, scale, scales)
    scales = jnp.where(valid, scales, 0.0).T
    scale_ref[0] = scales[: width // GROUP].astype(BF16)


def params(mebibytes):
    return pltpu.CompilerParams(vmem_limit_bytes=mebibytes * 1024 * 1024)


def local(frames_in, qkv_weight, out_weight, owners, slots):
    fr_count, patch_count, width = frames_in.shape
    rows_here = qkv_weight.shape[0]
    core = lax.axis_index("c")
    position = lax.axis_index("pool")
    chips = lax.axis_size("zh") * lax.axis_size("zl") * lax.axis_size("x")
    sources = 2 * lax.axis_size("pool")
    swap = [(0, 1), (1, 0)]

    share = pl.pallas_call(
        share_kernel,
        grid_spec=pltpu.PrefetchScalarGridSpec(
            num_scalar_prefetch=1,
            grid=(1,),
            in_specs=[pl.BlockSpec((2, patch_count, width), lambda g, at: (at[0] & 1, 0, 0))],
            out_specs=pl.BlockSpec((2 * chips, 2, width), lambda g, at: (0, 0, 0)),
        ),
        out_shape=jax.ShapeDtypeStruct((2 * chips, 2, width), BF16),
        compiler_params=params(SHARE),
        name="share",
    )(position.reshape(1), frames_in)
    share = lax.all_to_all(share, FRAME, 0, 0, tiled=True).reshape(4 * chips, width)
    tracks = lax.all_gather(share, "pool", axis=0, tiled=False)
    owners_other = lax.ppermute(owners, "c", swap)

    parts = qkv_weight.reshape(rows_here, 3, 2, HEAD_DIM)
    query, key, value = parts[:, 0], parts[:, 1], parts[:, 2]
    back = out_weight.T.reshape(rows_here, 2, HEAD_DIM)
    payload = jnp.concatenate(
        [
            query,
            back[..., :40],
            key,
            back[..., 40:80],
            value,
            back[..., 80:],
            jnp.zeros((rows_here, 2, 32), BF16),
        ],
        axis=-1,
    )
    both = lax.all_gather(payload, "c", axis=0, tiled=True)
    mine = lax.dynamic_index_in_dim(both, core, 1, keepdims=False)
    mine = spread(mine, "zh").reshape(-1, mine.shape[-1])
    mine = spread(mine, ("zl", "x"))
    mine, back_rows = pl.pallas_call(
        order_kernel,
        out_shape=[
            jax.ShapeDtypeStruct((width, 384), BF16),
            jax.ShapeDtypeStruct((96, width), BF16),
        ],
        scratch_shapes=[pltpu.VMEM((width, 384), F32)],
        compiler_params=params(ORDER),
        name="order",
    )(mine)
    mine_other = lax.ppermute(mine, "c", swap)
    out_rows = lax.all_gather(back_rows, ("c", "pool"), axis=0, tiled=False)

    attended = pl.pallas_call(
        track_kernel,
        grid=(4 // STEP,),
        in_specs=[
            pl.BlockSpec(memory_space=pltpu.SMEM),
            pl.BlockSpec((2 * STEP, 4 * chips, width), lambda p: (p, 0, 0)),
            pl.BlockSpec(mine.shape, lambda p: (0, 0)),
            pl.BlockSpec(mine.shape, lambda p: (0, 0)),
        ],
        out_specs=pl.BlockSpec((chips // 2, 2, 6, 8, 128), lambda p: (0, 0, 0, 0, 0)),
        out_shape=jax.ShapeDtypeStruct((chips // 2, 2, 6, 8, 128), BF16),
        scratch_shapes=[pltpu.VMEM((chips, 64, 128), F32)],
        compiler_params=params(TRACK),
        name="track",
    )(core.reshape(1), tracks, mine, mine_other)
    attended = attended.reshape(chips, 6, 8, 128)
    returned = lax.all_to_all(attended, CHIP, 0, 0, tiled=True)

    pair = jnp.where(
        core == 0,
        jnp.concatenate([owners, owners_other]),
        jnp.concatenate([owners_other, owners]),
    )
    packed = pl.pallas_call(
        pack_kernel,
        in_specs=[
            pl.BlockSpec(memory_space=pltpu.SMEM),
            pl.BlockSpec(memory_space=pltpu.VMEM),
        ],
        out_specs=pl.BlockSpec(memory_space=pltpu.VMEM),
        out_shape=jax.ShapeDtypeStruct((sources, 3 * chips // 4, 8, 128), BF16),
        compiler_params=params(PACK),
        name="pack",
    )(pair, returned.reshape(chips // 2, 2, 6, 8, 128))
    gathered = lax.all_to_all(packed, ("c", "pool"), 0, 0, tiled=True)

    match = (owners == position) & (slots == 0)
    chosen = jnp.sum(jnp.where(match, jnp.arange(fr_count, dtype=jnp.int32), 0))
    pick = jnp.stack([chosen, jnp.any(match).astype(jnp.int32)])
    groups = width // GROUP
    return pl.pallas_call(
        deliver_kernel,
        grid_spec=pltpu.PrefetchScalarGridSpec(
            num_scalar_prefetch=1,
            grid=(1,),
            in_specs=[
                pl.BlockSpec((1, patch_count, width), lambda g, pick: (pick[0], 0, 0)),
                pl.BlockSpec(gathered.shape, lambda g, pick: (0, 0, 0, 0)),
                pl.BlockSpec(out_rows.shape, lambda g, pick: (0, 0, 0)),
            ],
            out_specs=[
                pl.BlockSpec((1, patch_count, width), lambda g, pick: (0, 0, 0)),
                pl.BlockSpec((1, groups, patch_count), lambda g, pick: (0, 0, 0)),
            ],
        ),
        out_shape=[
            jax.ShapeDtypeStruct((1, patch_count, width), BF16),
            jax.ShapeDtypeStruct((1, groups, patch_count), BF16),
        ],
        compiler_params=params(DELIVER),
        name="deliver",
    )(pick, frames_in, gathered, out_rows)


def solution(mesh):
    fine = Mesh(mesh.devices.reshape(4, 2, 4, 2, 8), ("zh", "zl", "x", "c", "pool"))
    run = jax.shard_map(
        local,
        mesh=fine,
        in_specs=(
            P(FRAME, None, None),
            P(FRAME, None, "pool"),
            P("pool", FRAME),
            P(FRAME),
            P(FRAME),
        ),
        out_specs=(P(FRAME + ("pool",), None, None), P(FRAME + ("pool",), None, None)),
        check_vma=False,
    )

    def whole(*args):
        shipped, scales = run(*args)
        return shipped, scales

    return whole
```

```python
import jax
import jax.numpy as jnp
from jax import lax
from jax.experimental import pallas as pl
from jax.experimental.pallas import tpu as pltpu
from jax.sharding import Mesh, PartitionSpec as P

HEAD_DIM = 88
GROUP = 128
MAIN = 64
SLOT = 32
STEP = 1
SHARE, ORDER, TRACK, PACK, DELIVER = 58, 30, 50, 40, 52
FACTOR = 1.4426950408889634 / HEAD_DIM**0.5
CHIP = ("zh", "zl", "x")
FRAME = CHIP + ("c",)
F32 = jnp.float32
BF16 = jnp.bfloat16


def lanes_of(shape):
    return lax.broadcasted_iota(jnp.int32, shape, len(shape) - 1)


def turn(value, shift):
    shift = shift % 128
    if shift == 0:
        return value
    return pltpu.roll(value, shift, len(value.shape) - 1)


def spread(value, axis):
    count = lax.axis_size(axis)
    copies = jnp.broadcast_to(value[None], (count,) + value.shape)
    return lax.all_to_all(copies, axis, 0, 0, tiled=True)


def share_kernel(at_ref, frames_ref, out_ref):
    count, patches, width = frames_ref.shape
    rows = out_ref.shape[0] * out_ref.shape[1]
    row = lax.broadcasted_iota(jnp.int32, (rows, count * patches), 0)
    column = lax.broadcasted_iota(jnp.int32, (rows, count * patches), 1)
    wanted = (row & 1) * patches + (row >> 2) * 8 + ((row >> 1) & 1) * 4 + (at_ref[0] >> 1)
    pick = jnp.where(column == wanted, 1.0, 0.0).astype(BF16)
    tokens = frames_ref[...].reshape(count * patches, width)
    xf = jnp.dot(pick, tokens, preferred_element_type=F32)
    mean = jnp.mean(xf, axis=-1, keepdims=True)
    centred = xf - mean
    var = jnp.mean(centred * centred, axis=-1, keepdims=True)
    normed = centred * lax.rsqrt(var + 1e-06)
    out_ref[...] = normed.reshape(out_ref.shape).astype(BF16)


def order_kernel(source_ref, right_ref, back_ref, order_ref):
    inner, height = source_ref.shape[:2]
    outer = 4
    rows = height // outer
    for low in range(inner):
        block = source_ref[low].astype(F32)
        for high in range(outer):
            start = (high * inner + low) * rows
            order_ref[start : start + rows, :] = block[high * rows : (high + 1) * rows]
    right_ref[...] = order_ref[...].astype(BF16)
    turned = [order_ref[:, at : at + 128].T[HEAD_DIM:] for at in (0, 128, 256)]
    back_ref[...] = jnp.concatenate(turned, axis=0)[:96].astype(BF16)


def track_kernel(core_ref, tokens_ref, own_ref, other_ref, out_ref, o_ref):
    step = pl.program_id(0)
    core = core_ref[0]
    here = tokens_ref.shape[0] // 2
    frames = 2 * tokens_ref.shape[1]
    lane = lanes_of((frames, 128))
    right = jnp.concatenate([own_ref[...], other_ref[...]], axis=1)
    ones = jnp.where(lane == 127, 1.0, 0.0)
    for track in range(here):
        tokens = tokens_ref[2 * track : 2 * track + 2].reshape(frames, tokens_ref.shape[2])
        both = jnp.dot(tokens, right, preferred_element_type=F32)
        for which in range(2):
            head = core if which == 0 else 1 - core
            out = both[:, which * 384 : which * 384 + 384]
            query = jnp.where(lane < HEAD_DIM, out[:, :128] * FACTOR, 0.0).astype(BF16)
            key = out[:, 128:256].astype(BF16)
            value = jnp.where(lane < HEAD_DIM, out[:, 256:], ones).astype(BF16)
            scores = lax.dot_general(
                query, key, (((1,), (1,)), ((), ())), preferred_element_type=F32
            )
            top = jnp.max(scores, axis=-1, keepdims=True)
            expo = jnp.exp2(scores - top).astype(BF16)
            mixed = jnp.dot(expo, value, preferred_element_type=F32)
            mixed = jnp.where(lane < HEAD_DIM, mixed * (1.0 / mixed[:, 127:]), 0.0)
            mixed = mixed.reshape(frames // 8, 8, 128)
            o_ref[:, pl.ds(head * 4 + step * here + track, 8, stride=8), :] = mixed

    @pl.when(step == pl.num_programs(0) - 1)
    def _():
        pairs = frames // 16
        lane_o = lanes_of((pairs, 8, 128))

        def piece_of(side, owner, late, odd):
            start = (side * 4 + owner * 2 + odd) * 8
            return o_ref[late * pairs : (late + 1) * pairs, start : start + 8, :]

        for side in range(2):
            for owner in range(2):
                rest = None
                for late in range(2):
                    even, odd = (piece_of(side, owner, late, at) for at in range(2))
                    main = jnp.where(lane_o < MAIN, even, turn(odd, MAIN))
                    out_ref[:, side, owner * 2 + late] = main.astype(BF16)
                    for at, piece in enumerate((even, odd)):
                        part = late * 2 + at
                        piece = turn(piece, SLOT * part - MAIN)
                        rest = piece if part == 0 else jnp.where(lane_o >= SLOT * part, piece, rest)
                out_ref[:, side, 4 + owner] = rest.astype(BF16)


def half_turn(value):
    return pltpu.roll(value, 4, 1)


def pack_kernel(owner_ref, x_ref, out_ref):
    pairs = x_ref.shape[0]
    out_ref[...] = jnp.zeros_like(out_ref)

    def join(even, odd, lane, edges):
        shape = even[0].shape
        upper = lax.broadcasted_iota(jnp.int32, shape, 1) < 4
        first = jnp.where(upper, even[0], half_turn(odd[0]))
        second = jnp.where(upper, half_turn(even[1]), odd[1])
        return jnp.where(lane < edges, first, second)

    lane = lanes_of((pairs, 8, 128))
    lane_h = lanes_of((pairs // 2, 8, 128))
    for fr in range(8):
        place = (fr // 4) * 8 + owner_ref[fr]
        tiles = [x_ref[:, side, fr // 2].astype(F32) for side in range(2)]
        even, odd = (
            [turn(tile, MAIN * head - MAIN * (fr % 2)) for head in range(2)] for tile in tiles
        )
        out_ref[place, :pairs] = join(even, odd, lane, MAIN).astype(BF16)
        tiles = [x_ref[:, side, 4 + fr // 4].astype(F32) for side in range(2)]
        rests = []
        for half in range(2):
            rows = slice(half * (pairs // 2), (half + 1) * (pairs // 2))
            even, odd = (
                [
                    turn(tile[rows], 2 * SLOT * half + SLOT * head - SLOT * (fr % 4))
                    for head in range(2)
                ]
                for tile in tiles
            )
            rests.append(join(even, odd, lane_h, 2 * SLOT * half + SLOT))
        rest = jnp.where(lane_h < 2 * SLOT, rests[0], rests[1])
        out_ref[place, pairs:] = rest.astype(BF16)


def deliver_kernel(pick_ref, frame_ref, y_ref, weight_ref, out_ref, scale_ref):
    sources = y_ref.shape[0]
    heads = sources // 2
    patches, width = frame_ref.shape[1:]
    half = patches // 2
    tiles = half // 8
    valid = pick_ref[1] > 0
    lane = lanes_of((half, 128))

    def weave(first, second):
        upper = lax.broadcasted_iota(jnp.int32, first.shape, 1) < 4
        even = jnp.where(upper, first, half_turn(second))
        odd = jnp.where(upper, half_turn(first), second)
        return jnp.stack([even, odd], axis=1).reshape(first.shape[0] * 16, 128)

    mains, rests = [], []
    for at in range(heads):
        pair = [y_ref[core * heads + at, :tiles].astype(F32) for core in range(2)]
        mains.append(weave(*pair).astype(BF16))
    for at in range(0, heads, 2):
        first, second = (
            weave(*(y_ref[core * heads + one, tiles:].astype(F32) for core in range(2)))
            for one in (at, at + 1)
        )
        low = jnp.where(lane < MAIN, first, turn(second, MAIN))
        high = jnp.where(lane < MAIN, turn(first, MAIN), second)
        rests.append(jnp.concatenate([low, high], axis=0).astype(BF16))
    left = jnp.concatenate(mains, axis=1)
    left_rest = jnp.concatenate(rests, axis=1)
    lane_p = lanes_of((patches, 128))
    scales = jnp.zeros((patches, 128), F32)
    for start in range(0, width, 256):
        stop = min(start + 256, width)
        right, right_rest = (
            jnp.concatenate(
                [weight_ref[at : at + heads, rows, start:stop] for at in (0, heads)], axis=1
            )
            for rows in (slice(0, MAIN), slice(MAIN, MAIN + SLOT))
        )
        right = right.reshape(heads * 2 * MAIN, stop - start)
        right_rest = right_rest.reshape(heads * 2 * SLOT, stop - start)
        total = jnp.dot(left, right, preferred_element_type=F32)
        total += jnp.dot(left_rest, right_rest, preferred_element_type=F32)
        total += frame_ref[0, :, start:stop].astype(F32)
        for at in range(0, stop - start, GROUP):
            part = total[:, at : at + GROUP]
            top = jnp.max(jnp.abs(part), axis=-1, keepdims=True)
            scale = (top + 1e-06).astype(BF16).astype(F32)
            coded = jnp.where(valid, part * (1.0 / scale), 0.0).astype(BF16)
            out_ref[0, :, start + at : start + at + GROUP] = coded
            scales = jnp.where(lane_p == (start + at) // GROUP, scale, scales)
    scales = jnp.where(valid, scales, 0.0).T
    scale_ref[0] = scales[: width // GROUP].astype(BF16)


def params(mebibytes):
    return pltpu.CompilerParams(vmem_limit_bytes=mebibytes * 1024 * 1024)


def local(frames_in, qkv_weight, out_weight, owners, slots):
    fr_count, patch_count, width = frames_in.shape
    rows_here = qkv_weight.shape[0]
    core = lax.axis_index("c")
    position = lax.axis_index("pool")
    chips = lax.axis_size("zh") * lax.axis_size("zl") * lax.axis_size("x")
    sources = 2 * lax.axis_size("pool")
    swap = [(0, 1), (1, 0)]

    share = pl.pallas_call(
        share_kernel,
        grid_spec=pltpu.PrefetchScalarGridSpec(
            num_scalar_prefetch=1,
            grid=(1,),
            in_specs=[pl.BlockSpec((2, patch_count, width), lambda g, at: (at[0] & 1, 0, 0))],
            out_specs=pl.BlockSpec((2 * chips, 2, width), lambda g, at: (0, 0, 0)),
        ),
        out_shape=jax.ShapeDtypeStruct((2 * chips, 2, width), BF16),
        compiler_params=params(SHARE),
        name="share",
    )(position.reshape(1), frames_in)
    share = lax.all_to_all(share, FRAME, 0, 0, tiled=True).reshape(4 * chips, width)
    tracks = lax.all_gather(share, "pool", axis=0, tiled=False)
    owners_other = lax.ppermute(owners, "c", swap)

    parts = qkv_weight.reshape(rows_here, 3, 2, HEAD_DIM)
    query, key, value = parts[:, 0], parts[:, 1], parts[:, 2]
    back = out_weight.T.reshape(rows_here, 2, HEAD_DIM)
    payload = jnp.concatenate(
        [
            query,
            back[..., :40],
            key,
            back[..., 40:80],
            value,
            back[..., 80:],
            jnp.zeros((rows_here, 2, 32), BF16),
        ],
        axis=-1,
    )
    both = lax.all_gather(payload, "c", axis=0, tiled=True)
    mine = lax.dynamic_index_in_dim(both, core, 1, keepdims=False)
    mine = spread(mine, "zh").reshape(-1, mine.shape[-1])
    mine = spread(mine, ("zl", "x"))
    mine, back_rows = pl.pallas_call(
        order_kernel,
        out_shape=[
            jax.ShapeDtypeStruct((width, 384), BF16),
            jax.ShapeDtypeStruct((96, width), BF16),
        ],
        scratch_shapes=[pltpu.VMEM((width, 384), F32)],
        compiler_params=params(ORDER),
        name="order",
    )(mine)
    mine_other = lax.ppermute(mine, "c", swap)
    out_rows = lax.all_gather(back_rows, ("c", "pool"), axis=0, tiled=False)

    attended = pl.pallas_call(
        track_kernel,
        grid=(4 // STEP,),
        in_specs=[
            pl.BlockSpec(memory_space=pltpu.SMEM),
            pl.BlockSpec((2 * STEP, 4 * chips, width), lambda p: (p, 0, 0)),
            pl.BlockSpec(mine.shape, lambda p: (0, 0)),
            pl.BlockSpec(mine.shape, lambda p: (0, 0)),
        ],
        out_specs=pl.BlockSpec((chips // 2, 2, 6, 8, 128), lambda p: (0, 0, 0, 0, 0)),
        out_shape=jax.ShapeDtypeStruct((chips // 2, 2, 6, 8, 128), BF16),
        scratch_shapes=[pltpu.VMEM((chips, 64, 128), F32)],
        compiler_params=params(TRACK),
        name="track",
    )(core.reshape(1), tracks, mine, mine_other)
    attended = attended.reshape(chips, 6, 8, 128)
    returned = lax.all_to_all(attended, CHIP, 0, 0, tiled=True)

    pair = jnp.where(
        core == 0,
        jnp.concatenate([owners, owners_other]),
        jnp.concatenate([owners_other, owners]),
    )
    packed = pl.pallas_call(
        pack_kernel,
        in_specs=[
            pl.BlockSpec(memory_space=pltpu.SMEM),
            pl.BlockSpec(memory_space=pltpu.VMEM),
        ],
        out_specs=pl.BlockSpec(memory_space=pltpu.VMEM),
        out_shape=jax.ShapeDtypeStruct((sources, 3 * chips // 4, 8, 128), BF16),
        compiler_params=params(PACK),
        name="pack",
    )(pair, returned.reshape(chips // 2, 2, 6, 8, 128))
    gathered = lax.all_to_all(packed, ("c", "pool"), 0, 0, tiled=True)

    match = (owners == position) & (slots == 0)
    chosen = jnp.sum(jnp.where(match, jnp.arange(fr_count, dtype=jnp.int32), 0))
    pick = jnp.stack([chosen, jnp.any(match).astype(jnp.int32)])
    groups = width // GROUP
    return pl.pallas_call(
        deliver_kernel,
        grid_spec=pltpu.PrefetchScalarGridSpec(
            num_scalar_prefetch=1,
            grid=(1,),
            in_specs=[
                pl.BlockSpec((1, patch_count, width), lambda g, pick: (pick[0], 0, 0)),
                pl.BlockSpec(gathered.shape, lambda g, pick: (0, 0, 0, 0)),
                pl.BlockSpec(out_rows.shape, lambda g, pick: (0, 0, 0)),
            ],
            out_specs=[
                pl.BlockSpec((1, patch_count, width), lambda g, pick: (0, 0, 0)),
                pl.BlockSpec((1, groups, patch_count), lambda g, pick: (0, 0, 0)),
            ],
        ),
        out_shape=[
            jax.ShapeDtypeStruct((1, patch_count, width), BF16),
            jax.ShapeDtypeStruct((1, groups, patch_count), BF16),
        ],
        compiler_params=params(DELIVER),
        name="deliver",
    )(pick, frames_in, gathered, out_rows)


def solution(mesh):
    fine = Mesh(mesh.devices.reshape(4, 2, 4, 2, 8), ("zh", "zl", "x", "c", "pool"))
    run = jax.shard_map(
        local,
        mesh=fine,
        in_specs=(
            P(FRAME, None, None),
            P(FRAME, None, "pool"),
            P("pool", FRAME),
            P(FRAME),
            P(FRAME),
        ),
        out_specs=(P(FRAME + ("pool",), None, None), P(FRAME + ("pool",), None, None)),
        check_vma=False,
    )

    def whole(*args):
        shipped, scales = run(*args)
        return shipped, scales

    return whole
```

```python
import jax
import jax.numpy as jnp
from jax import lax
from jax.experimental import pallas as pl
from jax.experimental.pallas import tpu as pltpu
from jax.sharding import Mesh, PartitionSpec as P

HEAD_DIM = 88
GROUP = 128
MAIN = 64
SLOT = 32
STEP = 1
SHARE, ORDER, TRACK, PACK, DELIVER = 58, 30, 50, 40, 52
FACTOR = 1.4426950408889634 / HEAD_DIM**0.5
CHIP = ("zh", "zl", "x")
FRAME = CHIP + ("c",)
F32 = jnp.float32
BF16 = jnp.bfloat16


def lanes_of(shape):
    return lax.broadcasted_iota(jnp.int32, shape, len(shape) - 1)


def turn(value, shift):
    shift = shift % 128
    if shift == 0:
        return value
    return pltpu.roll(value, shift, len(value.shape) - 1)


def spread(value, axis):
    count = lax.axis_size(axis)
    copies = jnp.broadcast_to(value[None], (count,) + value.shape)
    return lax.all_to_all(copies, axis, 0, 0, tiled=True)


def share_kernel(at_ref, frames_ref, out_ref):
    count, patches, width = frames_ref.shape
    rows = out_ref.shape[0] * out_ref.shape[1]
    row = lax.broadcasted_iota(jnp.int32, (rows, count * patches), 0)
    column = lax.broadcasted_iota(jnp.int32, (rows, count * patches), 1)
    wanted = (row & 1) * patches + (row >> 2) * 8 + ((row >> 1) & 1) * 4 + (at_ref[0] >> 1)
    pick = jnp.where(column == wanted, 1.0, 0.0).astype(BF16)
    tokens = frames_ref[...].reshape(count * patches, width)
    xf = jnp.dot(pick, tokens, preferred_element_type=F32)
    mean = jnp.mean(xf, axis=-1, keepdims=True)
    centred = xf - mean
    var = jnp.mean(centred * centred, axis=-1, keepdims=True)
    normed = centred * lax.rsqrt(var + 1e-06)
    out_ref[...] = normed.reshape(out_ref.shape).astype(BF16)


def order_kernel(source_ref, right_ref, back_ref, order_ref):
    inner, height = source_ref.shape[:2]
    outer = 4
    rows = height // outer
    for low in range(inner):
        block = source_ref[low].astype(F32)
        for high in range(outer):
            start = (high * inner + low) * rows
            order_ref[start : start + rows, :] = block[high * rows : (high + 1) * rows]
    right_ref[...] = order_ref[...].astype(BF16)
    turned = [order_ref[:, at : at + 128].T[HEAD_DIM:] for at in (0, 128, 256)]
    back_ref[...] = jnp.concatenate(turned, axis=0)[:96].astype(BF16)


def track_kernel(core_ref, tokens_ref, own_ref, other_ref, out_ref, o_ref):
    step = pl.program_id(0)
    core = core_ref[0]
    here = tokens_ref.shape[0] // 2
    frames = 2 * tokens_ref.shape[1]
    lane = lanes_of((frames, 128))
    right = jnp.concatenate([own_ref[...], other_ref[...]], axis=1)
    ones = jnp.where(lane == 127, 1.0, 0.0)
    for track in range(here):
        tokens = tokens_ref[2 * track : 2 * track + 2].reshape(frames, tokens_ref.shape[2])
        both = jnp.dot(tokens, right, preferred_element_type=F32)
        for which in range(2):
            head = core if which == 0 else 1 - core
            out = both[:, which * 384 : which * 384 + 384]
            query = jnp.where(lane < HEAD_DIM, out[:, :128] * FACTOR, 0.0).astype(BF16)
            key = out[:, 128:256].astype(BF16)
            value = jnp.where(lane < HEAD_DIM, out[:, 256:], ones).astype(BF16)
            scores = lax.dot_general(
                query, key, (((1,), (1,)), ((), ())), preferred_element_type=F32
            )
            top = jnp.max(scores, axis=-1, keepdims=True)
            expo = jnp.exp2(scores - top).astype(BF16)
            mixed = jnp.dot(expo, value, preferred_element_type=F32)
            mixed = jnp.where(lane < HEAD_DIM, mixed * (1.0 / mixed[:, 127:]), 0.0)
            mixed = mixed.reshape(frames // 8, 8, 128)
            o_ref[:, pl.ds(head * 4 + step * here + track, 8, stride=8), :] = mixed

    @pl.when(step == pl.num_programs(0) - 1)
    def _():
        pairs = frames // 16
        lane_o = lanes_of((pairs, 8, 128))

        def piece_of(side, owner, late, odd):
            start = (side * 4 + owner * 2 + odd) * 8
            return o_ref[late * pairs : (late + 1) * pairs, start : start + 8, :]

        for side in range(2):
            for owner in range(2):
                rest = None
                for late in range(2):
                    even, odd = (piece_of(side, owner, late, at) for at in range(2))
                    main = jnp.where(lane_o < MAIN, even, turn(odd, MAIN))
                    out_ref[:, side, owner * 2 + late] = main.astype(BF16)
                    for at, piece in enumerate((even, odd)):
                        part = late * 2 + at
                        piece = turn(piece, SLOT * part - MAIN)
                        rest = piece if part == 0 else jnp.where(lane_o >= SLOT * part, piece, rest)
                out_ref[:, side, 4 + owner] = rest.astype(BF16)


def half_turn(value):
    return pltpu.roll(value, 4, 1)


def pack_kernel(owner_ref, x_ref, out_ref):
    pairs = x_ref.shape[0]
    out_ref[...] = jnp.zeros_like(out_ref)

    def join(even, odd, lane, edges):
        shape = even[0].shape
        upper = lax.broadcasted_iota(jnp.int32, shape, 1) < 4
        first = jnp.where(upper, even[0], half_turn(odd[0]))
        second = jnp.where(upper, half_turn(even[1]), odd[1])
        return jnp.where(lane < edges, first, second)

    lane = lanes_of((pairs, 8, 128))
    lane_h = lanes_of((pairs // 2, 8, 128))
    core = pl.program_id(0)
    for fr in range(4):
        place = owner_ref[core * 4 + fr]
        tiles = [x_ref[:, side, 2 * core + fr // 2].astype(F32) for side in range(2)]
        even, odd = (
            [turn(tile, MAIN * head - MAIN * (fr % 2)) for head in range(2)] for tile in tiles
        )
        out_ref[place, :pairs] = join(even, odd, lane, MAIN).astype(BF16)
        tiles = [x_ref[:, side, 4 + core].astype(F32) for side in range(2)]
        rests = []
        for half in range(2):
            rows = slice(half * (pairs // 2), (half + 1) * (pairs // 2))
            even, odd = (
                [
                    turn(tile[rows], 2 * SLOT * half + SLOT * head - SLOT * fr)
                    for head in range(2)
                ]
                for tile in tiles
            )
            rests.append(join(even, odd, lane_h, 2 * SLOT * half + SLOT))
        rest = jnp.where(lane_h < 2 * SLOT, rests[0], rests[1])
        out_ref[place, pairs:] = rest.astype(BF16)


def deliver_kernel(pick_ref, frame_ref, y_ref, weight_ref, out_ref, scale_ref):
    sources = y_ref.shape[0]
    heads = sources // 2
    patches, width = frame_ref.shape[1:]
    half = patches // 2
    tiles = half // 8
    valid = pick_ref[1] > 0
    lane = lanes_of((half, 128))

    def weave(first, second):
        upper = lax.broadcasted_iota(jnp.int32, first.shape, 1) < 4
        even = jnp.where(upper, first, half_turn(second))
        odd = jnp.where(upper, half_turn(first), second)
        return jnp.stack([even, odd], axis=1).reshape(first.shape[0] * 16, 128)

    mains, rests = [], []
    for at in range(heads):
        pair = [y_ref[core * heads + at, :tiles].astype(F32) for core in range(2)]
        mains.append(weave(*pair).astype(BF16))
    for at in range(0, heads, 2):
        first, second = (
            weave(*(y_ref[core * heads + one, tiles:].astype(F32) for core in range(2)))
            for one in (at, at + 1)
        )
        low = jnp.where(lane < MAIN, first, turn(second, MAIN))
        high = jnp.where(lane < MAIN, turn(first, MAIN), second)
        rests.append(jnp.concatenate([low, high], axis=0).astype(BF16))
    left = jnp.concatenate(mains, axis=1)
    left_rest = jnp.concatenate(rests, axis=1)
    lane_p = lanes_of((patches, 128))
    scales = jnp.zeros((patches, 128), F32)
    for start in range(0, width, 256):
        stop = min(start + 256, width)
        right, right_rest = (
            jnp.concatenate(
                [weight_ref[at : at + heads, rows, start:stop] for at in (0, heads)], axis=1
            )
            for rows in (slice(0, MAIN), slice(MAIN, MAIN + SLOT))
        )
        right = right.reshape(heads * 2 * MAIN, stop - start)
        right_rest = right_rest.reshape(heads * 2 * SLOT, stop - start)
        total = jnp.dot(left, right, preferred_element_type=F32)
        total += jnp.dot(left_rest, right_rest, preferred_element_type=F32)
        total += frame_ref[0, :, start:stop].astype(F32)
        for at in range(0, stop - start, GROUP):
            part = total[:, at : at + GROUP]
            top = jnp.max(jnp.abs(part), axis=-1, keepdims=True)
            scale = (top + 1e-06).astype(BF16).astype(F32)
            coded = jnp.where(valid, part * (1.0 / scale), 0.0).astype(BF16)
            out_ref[0, :, start + at : start + at + GROUP] = coded
            scales = jnp.where(lane_p == (start + at) // GROUP, scale, scales)
    scales = jnp.where(valid, scales, 0.0).T
    scale_ref[0] = scales[: width // GROUP].astype(BF16)


def params(mebibytes):
    return pltpu.CompilerParams(vmem_limit_bytes=mebibytes * 1024 * 1024)


def local(frames_in, qkv_weight, out_weight, owners, slots):
    fr_count, patch_count, width = frames_in.shape
    rows_here = qkv_weight.shape[0]
    core = lax.axis_index("c")
    position = lax.axis_index("pool")
    chips = lax.axis_size("zh") * lax.axis_size("zl") * lax.axis_size("x")
    sources = 2 * lax.axis_size("pool")
    swap = [(0, 1), (1, 0)]

    share = pl.pallas_call(
        share_kernel,
        grid_spec=pltpu.PrefetchScalarGridSpec(
            num_scalar_prefetch=1,
            grid=(1,),
            in_specs=[pl.BlockSpec((2, patch_count, width), lambda g, at: (at[0] & 1, 0, 0))],
            out_specs=pl.BlockSpec((2 * chips, 2, width), lambda g, at: (0, 0, 0)),
        ),
        out_shape=jax.ShapeDtypeStruct((2 * chips, 2, width), BF16),
        compiler_params=params(SHARE),
        name="share",
    )(position.reshape(1), frames_in)
    share = lax.all_to_all(share, FRAME, 0, 0, tiled=True).reshape(4 * chips, width)
    tracks = lax.all_gather(share, "pool", axis=0, tiled=False)
    owners_other = lax.ppermute(owners, "c", swap)

    parts = qkv_weight.reshape(rows_here, 3, 2, HEAD_DIM)
    query, key, value = parts[:, 0], parts[:, 1], parts[:, 2]
    back = out_weight.T.reshape(rows_here, 2, HEAD_DIM)
    payload = jnp.concatenate(
        [
            query,
            back[..., :40],
            key,
            back[..., 40:80],
            value,
            back[..., 80:],
            jnp.zeros((rows_here, 2, 32), BF16),
        ],
        axis=-1,
    )
    both = lax.all_gather(payload, "c", axis=0, tiled=True)
    mine = lax.dynamic_index_in_dim(both, core, 1, keepdims=False)
    mine = spread(mine, "zh").reshape(-1, mine.shape[-1])
    mine = spread(mine, ("zl", "x"))
    mine, back_rows = pl.pallas_call(
        order_kernel,
        out_shape=[
            jax.ShapeDtypeStruct((width, 384), BF16),
            jax.ShapeDtypeStruct((96, width), BF16),
        ],
        scratch_shapes=[pltpu.VMEM((width, 384), F32)],
        compiler_params=params(ORDER),
        name="order",
    )(mine)
    mine_other = lax.ppermute(mine, "c", swap)
    out_rows = lax.all_gather(back_rows, ("c", "pool"), axis=0, tiled=False)

    attended = pl.pallas_call(
        track_kernel,
        grid=(4 // STEP,),
        in_specs=[
            pl.BlockSpec(memory_space=pltpu.SMEM),
            pl.BlockSpec((2 * STEP, 4 * chips, width), lambda p: (p, 0, 0)),
            pl.BlockSpec(mine.shape, lambda p: (0, 0)),
            pl.BlockSpec(mine.shape, lambda p: (0, 0)),
        ],
        out_specs=pl.BlockSpec((chips // 2, 2, 6, 8, 128), lambda p: (0, 0, 0, 0, 0)),
        out_shape=jax.ShapeDtypeStruct((chips // 2, 2, 6, 8, 128), BF16),
        scratch_shapes=[pltpu.VMEM((chips, 64, 128), F32)],
        compiler_params=params(TRACK),
        name="track",
    )(core.reshape(1), tracks, mine, mine_other)
    attended = attended.reshape(chips, 6, 8, 128)
    returned = lax.all_to_all(attended, CHIP, 0, 0, tiled=True)

    pair = jnp.where(
        core == 0,
        jnp.concatenate([owners, owners_other]),
        jnp.concatenate([owners_other, owners]),
    )
    packed = pl.pallas_call(
        pack_kernel,
        grid=(2,),
        in_specs=[
            pl.BlockSpec(memory_space=pltpu.SMEM),
            pl.BlockSpec((chips // 2, 2, 6, 8, 128), lambda c: (0, 0, 0, 0, 0)),
        ],
        out_specs=pl.BlockSpec((sources // 2, 3 * chips // 4, 8, 128), lambda c: (c, 0, 0, 0)),
        out_shape=jax.ShapeDtypeStruct((sources, 3 * chips // 4, 8, 128), BF16),
        compiler_params=params(PACK),
        name="pack",
    )(pair, returned.reshape(chips // 2, 2, 6, 8, 128))
    gathered = lax.all_to_all(packed, ("c", "pool"), 0, 0, tiled=True)

    match = (owners == position) & (slots == 0)
    chosen = jnp.sum(jnp.where(match, jnp.arange(fr_count, dtype=jnp.int32), 0))
    pick = jnp.stack([chosen, jnp.any(match).astype(jnp.int32)])
    groups = width // GROUP
    return pl.pallas_call(
        deliver_kernel,
        grid_spec=pltpu.PrefetchScalarGridSpec(
            num_scalar_prefetch=1,
            grid=(1,),
            in_specs=[
                pl.BlockSpec((1, patch_count, width), lambda g, pick: (pick[0], 0, 0)),
                pl.BlockSpec(gathered.shape, lambda g, pick: (0, 0, 0, 0)),
                pl.BlockSpec(out_rows.shape, lambda g, pick: (0, 0, 0)),
            ],
            out_specs=[
                pl.BlockSpec((1, patch_count, width), lambda g, pick: (0, 0, 0)),
                pl.BlockSpec((1, groups, patch_count), lambda g, pick: (0, 0, 0)),
            ],
        ),
        out_shape=[
            jax.ShapeDtypeStruct((1, patch_count, width), BF16),
            jax.ShapeDtypeStruct((1, groups, patch_count), BF16),
        ],
        compiler_params=params(DELIVER),
        name="deliver",
    )(pick, frames_in, gathered, out_rows)


def solution(mesh):
    fine = Mesh(mesh.devices.reshape(4, 2, 4, 2, 8), ("zh", "zl", "x", "c", "pool"))
    run = jax.shard_map(
        local,
        mesh=fine,
        in_specs=(
            P(FRAME, None, None),
            P(FRAME, None, "pool"),
            P("pool", FRAME),
            P(FRAME),
            P(FRAME),
        ),
        out_specs=(P(FRAME + ("pool",), None, None), P(FRAME + ("pool",), None, None)),
        check_vma=False,
    )

    def whole(*args):
        shipped, scales = run(*args)
        return shipped, scales

    return whole
```

```python
import jax
import jax.numpy as jnp
from jax import lax
from jax.experimental import pallas as pl
from jax.experimental.pallas import tpu as pltpu
from jax.sharding import Mesh, PartitionSpec as P

HEAD_DIM = 88
GROUP = 128
MAIN = 64
SLOT = 32
STEP = 1
SHARE, ORDER, TRACK, PACK, DELIVER = 58, 30, 50, 40, 52
FACTOR = 1.4426950408889634 / HEAD_DIM**0.5
CHIP = ("zh", "zl", "x")
FRAME = CHIP + ("c",)
F32 = jnp.float32
BF16 = jnp.bfloat16


def lanes_of(shape):
    return lax.broadcasted_iota(jnp.int32, shape, len(shape) - 1)


def turn(value, shift):
    shift = shift % 128
    if shift == 0:
        return value
    return pltpu.roll(value, shift, len(value.shape) - 1)


def spread(value, axis):
    count = lax.axis_size(axis)
    copies = jnp.broadcast_to(value[None], (count,) + value.shape)
    return lax.all_to_all(copies, axis, 0, 0, tiled=True)


def share_kernel(at_ref, frame_ref, out_ref, rows_ref):
    step = pl.program_id(0)
    patches, width = frame_ref.shape[1:]
    shape = (rows_ref.shape[0], patches)
    row = lax.broadcasted_iota(jnp.int32, shape, 0)
    column = lax.broadcasted_iota(jnp.int32, shape, 1)
    wanted = (row >> 2) * 8 + ((row >> 1) & 1) * 4 + (at_ref[0] >> 1)
    pick = jnp.where((column == wanted) & ((row & 1) == step), 1.0, 0.0).astype(BF16)
    part = jnp.dot(pick, frame_ref[0], preferred_element_type=F32)

    @pl.when(step == 0)
    def _():
        rows_ref[...] = part

    @pl.when(step == 1)
    def _():
        xf = rows_ref[...] + part
        mean = jnp.mean(xf, axis=-1, keepdims=True)
        centred = xf - mean
        var = jnp.mean(centred * centred, axis=-1, keepdims=True)
        normed = centred * lax.rsqrt(var + 1e-06)
        out_ref[...] = normed.reshape(out_ref.shape).astype(BF16)


def order_kernel(source_ref, right_ref, back_ref, order_ref):
    inner, height = source_ref.shape[:2]
    outer = 4
    rows = height // outer
    for low in range(inner):
        block = source_ref[low].astype(F32)
        for high in range(outer):
            start = (high * inner + low) * rows
            order_ref[start : start + rows, :] = block[high * rows : (high + 1) * rows]
    right_ref[...] = order_ref[...].astype(BF16)
    turned = [order_ref[:, at : at + 128].T[HEAD_DIM:] for at in (0, 128, 256)]
    back_ref[...] = jnp.concatenate(turned, axis=0)[:96].astype(BF16)


def track_kernel(core_ref, tokens_ref, own_ref, other_ref, out_ref, o_ref):
    step = pl.program_id(0)
    core = core_ref[0]
    here = tokens_ref.shape[0] // 2
    frames = 2 * tokens_ref.shape[1]
    lane = lanes_of((frames, 128))
    right = jnp.concatenate([own_ref[...], other_ref[...]], axis=1)
    ones = jnp.where(lane == 127, 1.0, 0.0)
    for track in range(here):
        tokens = tokens_ref[2 * track : 2 * track + 2].reshape(frames, tokens_ref.shape[2])
        both = jnp.dot(tokens, right, preferred_element_type=F32)
        for which in range(2):
            head = core if which == 0 else 1 - core
            out = both[:, which * 384 : which * 384 + 384]
            query = jnp.where(lane < HEAD_DIM, out[:, :128] * FACTOR, 0.0).astype(BF16)
            key = out[:, 128:256].astype(BF16)
            value = jnp.where(lane < HEAD_DIM, out[:, 256:], ones).astype(BF16)
            scores = lax.dot_general(
                query, key, (((1,), (1,)), ((), ())), preferred_element_type=F32
            )
            top = jnp.max(scores, axis=-1, keepdims=True)
            expo = jnp.exp2(scores - top).astype(BF16)
            mixed = jnp.dot(expo, value, preferred_element_type=F32)
            mixed = jnp.where(lane < HEAD_DIM, mixed * (1.0 / mixed[:, 127:]), 0.0)
            mixed = mixed.reshape(frames // 8, 8, 128)
            o_ref[:, pl.ds(head * 4 + step * here + track, 8, stride=8), :] = mixed

    @pl.when(step == pl.num_programs(0) - 1)
    def _():
        pairs = frames // 16
        lane_o = lanes_of((pairs, 8, 128))

        def piece_of(side, owner, late, odd):
            start = (side * 4 + owner * 2 + odd) * 8
            return o_ref[late * pairs : (late + 1) * pairs, start : start + 8, :]

        for side in range(2):
            for owner in range(2):
                rest = None
                for late in range(2):
                    even, odd = (piece_of(side, owner, late, at) for at in range(2))
                    main = jnp.where(lane_o < MAIN, even, turn(odd, MAIN))
                    out_ref[:, side, owner * 2 + late] = main.astype(BF16)
                    for at, piece in enumerate((even, odd)):
                        part = late * 2 + at
                        piece = turn(piece, SLOT * part - MAIN)
                        rest = piece if part == 0 else jnp.where(lane_o >= SLOT * part, piece, rest)
                out_ref[:, side, 4 + owner] = rest.astype(BF16)


def half_turn(value):
    return pltpu.roll(value, 4, 1)


def pack_kernel(owner_ref, x_ref, out_ref):
    pairs = x_ref.shape[0]
    out_ref[...] = jnp.zeros_like(out_ref)

    def join(even, odd, lane, edges):
        shape = even[0].shape
        upper = lax.broadcasted_iota(jnp.int32, shape, 1) < 4
        first = jnp.where(upper, even[0], half_turn(odd[0]))
        second = jnp.where(upper, half_turn(even[1]), odd[1])
        return jnp.where(lane < edges, first, second)

    lane = lanes_of((pairs, 8, 128))
    lane_h = lanes_of((pairs // 2, 8, 128))
    core = pl.program_id(0)
    for fr in range(4):
        place = owner_ref[core * 4 + fr]
        tiles = [x_ref[:, side, 2 * core + fr // 2].astype(F32) for side in range(2)]
        even, odd = (
            [turn(tile, MAIN * head - MAIN * (fr % 2)) for head in range(2)] for tile in tiles
        )
        out_ref[place, :pairs] = join(even, odd, lane, MAIN).astype(BF16)
        tiles = [x_ref[:, side, 4 + core].astype(F32) for side in range(2)]
        rests = []
        for half in range(2):
            rows = slice(half * (pairs // 2), (half + 1) * (pairs // 2))
            even, odd = (
                [
                    turn(tile[rows], 2 * SLOT * half + SLOT * head - SLOT * fr)
                    for head in range(2)
                ]
                for tile in tiles
            )
            rests.append(join(even, odd, lane_h, 2 * SLOT * half + SLOT))
        rest = jnp.where(lane_h < 2 * SLOT, rests[0], rests[1])
        out_ref[place, pairs:] = rest.astype(BF16)


def deliver_kernel(pick_ref, frame_ref, y_ref, weight_ref, out_ref, scale_ref):
    sources = y_ref.shape[0]
    heads = sources // 2
    patches, width = frame_ref.shape[1:]
    half = patches // 2
    tiles = half // 8
    valid = pick_ref[1] > 0
    lane = lanes_of((half, 128))

    def weave(first, second):
        upper = lax.broadcasted_iota(jnp.int32, first.shape, 1) < 4
        even = jnp.where(upper, first, half_turn(second))
        odd = jnp.where(upper, half_turn(first), second)
        return jnp.stack([even, odd], axis=1).reshape(first.shape[0] * 16, 128)

    mains, rests = [], []
    for at in range(heads):
        pair = [y_ref[core * heads + at, :tiles].astype(F32) for core in range(2)]
        mains.append(weave(*pair).astype(BF16))
    for at in range(0, heads, 2):
        first, second = (
            weave(*(y_ref[core * heads + one, tiles:].astype(F32) for core in range(2)))
            for one in (at, at + 1)
        )
        low = jnp.where(lane < MAIN, first, turn(second, MAIN))
        high = jnp.where(lane < MAIN, turn(first, MAIN), second)
        rests.append(jnp.concatenate([low, high], axis=0).astype(BF16))
    left = jnp.concatenate(mains, axis=1)
    left_rest = jnp.concatenate(rests, axis=1)
    lane_p = lanes_of((patches, 128))
    scales = jnp.zeros((patches, 128), F32)
    for start in range(0, width, 256):
        stop = min(start + 256, width)
        right, right_rest = (
            jnp.concatenate(
                [weight_ref[at : at + heads, rows, start:stop] for at in (0, heads)], axis=1
            )
            for rows in (slice(0, MAIN), slice(MAIN, MAIN + SLOT))
        )
        right = right.reshape(heads * 2 * MAIN, stop - start)
        right_rest = right_rest.reshape(heads * 2 * SLOT, stop - start)
        total = jnp.dot(left, right, preferred_element_type=F32)
        total += jnp.dot(left_rest, right_rest, preferred_element_type=F32)
        total += frame_ref[0, :, start:stop].astype(F32)
        for at in range(0, stop - start, GROUP):
            part = total[:, at : at + GROUP]
            top = jnp.max(jnp.abs(part), axis=-1, keepdims=True)
            scale = (top + 1e-06).astype(BF16).astype(F32)
            coded = jnp.where(valid, part * (1.0 / scale), 0.0).astype(BF16)
            out_ref[0, :, start + at : start + at + GROUP] = coded
            scales = jnp.where(lane_p == (start + at) // GROUP, scale, scales)
    scales = jnp.where(valid, scales, 0.0).T
    scale_ref[0] = scales[: width // GROUP].astype(BF16)


def params(mebibytes):
    return pltpu.CompilerParams(vmem_limit_bytes=mebibytes * 1024 * 1024)


def local(frames_in, qkv_weight, out_weight, owners, slots):
    fr_count, patch_count, width = frames_in.shape
    rows_here = qkv_weight.shape[0]
    core = lax.axis_index("c")
    position = lax.axis_index("pool")
    chips = lax.axis_size("zh") * lax.axis_size("zl") * lax.axis_size("x")
    sources = 2 * lax.axis_size("pool")
    swap = [(0, 1), (1, 0)]

    share = pl.pallas_call(
        share_kernel,
        grid_spec=pltpu.PrefetchScalarGridSpec(
            num_scalar_prefetch=1,
            grid=(2,),
            in_specs=[
                pl.BlockSpec((1, patch_count, width), lambda g, at: (2 * (at[0] & 1) + g, 0, 0))
            ],
            out_specs=pl.BlockSpec((2 * chips, 2, width), lambda g, at: (0, 0, 0)),
            scratch_shapes=[pltpu.VMEM((4 * chips, width), F32)],
        ),
        out_shape=jax.ShapeDtypeStruct((2 * chips, 2, width), BF16),
        compiler_params=params(SHARE),
        name="share",
    )(position.reshape(1), frames_in)
    share = lax.all_to_all(share, FRAME, 0, 0, tiled=True).reshape(4 * chips, width)
    tracks = lax.all_gather(share, "pool", axis=0, tiled=False)
    owners_other = lax.ppermute(owners, "c", swap)

    parts = qkv_weight.reshape(rows_here, 3, 2, HEAD_DIM)
    query, key, value = parts[:, 0], parts[:, 1], parts[:, 2]
    back = out_weight.T.reshape(rows_here, 2, HEAD_DIM)
    payload = jnp.concatenate(
        [
            query,
            back[..., :40],
            key,
            back[..., 40:80],
            value,
            back[..., 80:],
            jnp.zeros((rows_here, 2, 32), BF16),
        ],
        axis=-1,
    )
    both = lax.all_gather(payload, "c", axis=0, tiled=True)
    mine = lax.dynamic_index_in_dim(both, core, 1, keepdims=False)
    mine = spread(mine, "zh").reshape(-1, mine.shape[-1])
    mine = spread(mine, ("zl", "x"))
    mine, back_rows = pl.pallas_call(
        order_kernel,
        out_shape=[
            jax.ShapeDtypeStruct((width, 384), BF16),
            jax.ShapeDtypeStruct((96, width), BF16),
        ],
        scratch_shapes=[pltpu.VMEM((width, 384), F32)],
        compiler_params=params(ORDER),
        name="order",
    )(mine)
    mine_other = lax.ppermute(mine, "c", swap)
    out_rows = lax.all_gather(back_rows, ("c", "pool"), axis=0, tiled=False)

    attended = pl.pallas_call(
        track_kernel,
        grid=(4 // STEP,),
        in_specs=[
            pl.BlockSpec(memory_space=pltpu.SMEM),
            pl.BlockSpec((2 * STEP, 4 * chips, width), lambda p: (p, 0, 0)),
            pl.BlockSpec(mine.shape, lambda p: (0, 0)),
            pl.BlockSpec(mine.shape, lambda p: (0, 0)),
        ],
        out_specs=pl.BlockSpec((chips // 2, 2, 6, 8, 128), lambda p: (0, 0, 0, 0, 0)),
        out_shape=jax.ShapeDtypeStruct((chips // 2, 2, 6, 8, 128), BF16),
        scratch_shapes=[pltpu.VMEM((chips, 64, 128), F32)],
        compiler_params=params(TRACK),
        name="track",
    )(core.reshape(1), tracks, mine, mine_other)
    attended = attended.reshape(chips, 6, 8, 128)
    returned = lax.all_to_all(attended, CHIP, 0, 0, tiled=True)

    pair = jnp.where(
        core == 0,
        jnp.concatenate([owners, owners_other]),
        jnp.concatenate([owners_other, owners]),
    )
    packed = pl.pallas_call(
        pack_kernel,
        grid=(2,),
        in_specs=[
            pl.BlockSpec(memory_space=pltpu.SMEM),
            pl.BlockSpec((chips // 2, 2, 6, 8, 128), lambda c: (0, 0, 0, 0, 0)),
        ],
        out_specs=pl.BlockSpec((sources // 2, 3 * chips // 4, 8, 128), lambda c: (c, 0, 0, 0)),
        out_shape=jax.ShapeDtypeStruct((sources, 3 * chips // 4, 8, 128), BF16),
        compiler_params=params(PACK),
        name="pack",
    )(pair, returned.reshape(chips // 2, 2, 6, 8, 128))
    gathered = lax.all_to_all(packed, ("c", "pool"), 0, 0, tiled=True)

    match = (owners == position) & (slots == 0)
    chosen = jnp.sum(jnp.where(match, jnp.arange(fr_count, dtype=jnp.int32), 0))
    pick = jnp.stack([chosen, jnp.any(match).astype(jnp.int32)])
    groups = width // GROUP
    return pl.pallas_call(
        deliver_kernel,
        grid_spec=pltpu.PrefetchScalarGridSpec(
            num_scalar_prefetch=1,
            grid=(1,),
            in_specs=[
                pl.BlockSpec((1, patch_count, width), lambda g, pick: (pick[0], 0, 0)),
                pl.BlockSpec(gathered.shape, lambda g, pick: (0, 0, 0, 0)),
                pl.BlockSpec(out_rows.shape, lambda g, pick: (0, 0, 0)),
            ],
            out_specs=[
                pl.BlockSpec((1, patch_count, width), lambda g, pick: (0, 0, 0)),
                pl.BlockSpec((1, groups, patch_count), lambda g, pick: (0, 0, 0)),
            ],
        ),
        out_shape=[
            jax.ShapeDtypeStruct((1, patch_count, width), BF16),
            jax.ShapeDtypeStruct((1, groups, patch_count), BF16),
        ],
        compiler_params=params(DELIVER),
        name="deliver",
    )(pick, frames_in, gathered, out_rows)


def solution(mesh):
    fine = Mesh(mesh.devices.reshape(4, 2, 4, 2, 8), ("zh", "zl", "x", "c", "pool"))
    run = jax.shard_map(
        local,
        mesh=fine,
        in_specs=(
            P(FRAME, None, None),
            P(FRAME, None, "pool"),
            P("pool", FRAME),
            P(FRAME),
            P(FRAME),
        ),
        out_specs=(P(FRAME + ("pool",), None, None), P(FRAME + ("pool",), None, None)),
        check_vma=False,
    )

    def whole(*args):
        shipped, scales = run(*args)
        return shipped, scales

    return whole
```
